32 devices in a mesh: lon: 4 (over y, x), lat: 4 (over z), rad: 2 (over core).
Axes of the slice: x: 2, y: 2, z: 4, core: 2. Of those that a mesh axis runs over, the one named last changes fastest.
Arguments:
- adj_now: float32 [16, 128, 512], P('rad', 'lat', 'lon'), may hold values from -6 to 6
- adj_next: float32 [16, 128, 512], P('rad', 'lat', 'lon'), may hold values from -6 to 6
- fwd_now: float32 [16, 128, 512], P('rad', 'lat', 'lon'), may hold values from -6 to 6
- fwd_next: float32 [16, 128, 512], P('rad', 'lat', 'lon'), may hold values from -6 to 6
- stiffness: float32 [16, 128, 512], P('rad', 'lat', 'lon'), may hold values from 0.04 to 0.15
- buoyancy: float32 [16, 128, 512], P('rad', 'lat', 'lon'), may hold values from 0.6 to 1.5
- kernel_bulk_in: float32 [16, 128, 512], P('rad', 'lat', 'lon'), may hold values from -6 to 6
- kernel_density_in: float32 [16, 128, 512], P('rad', 'lat', 'lon'), may hold values from -6 to 6
Outputs:
- adj_out_now: float32 [16, 128, 512], P('rad', 'lat', 'lon')
- adj_out_next: float32 [16, 128, 512], P('rad', 'lat', 'lon')
- fwd_out_now: float32 [16, 128, 512], P('rad', 'lat', 'lon')
- fwd_out_next: float32 [16, 128, 512], P('rad', 'lat', 'lon')
- kernel_bulk: float32 [16, 128, 512], P('rad', 'lat', 'lon')
- kernel_density: float32 [16, 128, 512], P('rad', 'lat', 'lon')
The draws below stay inside these ranges and needn't reach their ends.
All inputs are finite; a program needn't handle non-finite values.
Results may differ from the reference program's by a relative error of at most 0.00002.
Values sent between devices are 32-bit elements; how exact they have to be, the bound alone decides.
No kernel may reach another device: no remote copies, remote signals or barrier semaphores. Data moves between devices by JAX's collectives and lax.ppermute only.
A program may use at most 64 MiB of HBM per device.

```python
import math
import jax
import jax.numpy as jnp
from jax import lax

STEPS = 2
NRAD = 16
NLAT = 128
NLON = 512


def block_scale(stream_key, extent, cuts, smallest, high):
    loudness = 1.0
    for axis_at, shards_of in cuts:
        steps = jax.random.uniform(jax.random.fold_in(jax.random.fold_in(stream_key, 6), axis_at), (shards_of,), jnp.float32, smallest / len(cuts), high / len(cuts))
        loudness = loudness * jnp.repeat(jnp.exp(steps), extent[axis_at] // shards_of).reshape((-1,) + (1,) * (len(extent) - 1 - axis_at))
    return loudness


def normal_values(rng, extent, spread, bound, shards=(), kind=jnp.bfloat16):
    loudness = block_scale(rng, extent, shards, -0.22, 0.18) if shards else 1.0
    drawn = jax.random.normal(rng, extent, jnp.float32) * spread * loudness
    return jnp.minimum(jnp.maximum(drawn, -bound), bound).astype(kind)


def setup_inputs(seed: int = 0) -> dict:
    key_of = jax.random.split(jax.random.key(seed), 9)
    return {
        "adj_now": normal_values(key_of[0], (NRAD, NLAT, NLON), 1.0, 6.0, ((0, 2), (1, 4), (2, 4)), jnp.float32),
        "adj_next": normal_values(key_of[1], (NRAD, NLAT, NLON), 1.0, 6.0, ((0, 2), (1, 4), (2, 4)), jnp.float32),
        "fwd_now": normal_values(key_of[2], (NRAD, NLAT, NLON), 1.0, 6.0, ((0, 2), (1, 4), (2, 4)), jnp.float32),
        "fwd_next": normal_values(key_of[3], (NRAD, NLAT, NLON), 1.0, 6.0, ((0, 2), (1, 4), (2, 4)), jnp.float32),
        "stiffness": jnp.clip(0.04 + 0.11000001 * jax.random.uniform(key_of[4], (NRAD, NLAT, NLON), jnp.float32) ** block_scale(key_of[4], (NRAD, NLAT, NLON), ((0, 2), (1, 4), (2, 4)), -0.2, 0.2), 0.04, 0.15),
        "buoyancy": jnp.clip(jnp.exp(math.log(1.5) - 0.9162907 * jax.random.uniform(key_of[5], (NRAD, NLAT, NLON), jnp.float32) ** block_scale(key_of[5], (NRAD, NLAT, NLON), ((0, 2), (1, 4), (2, 4)), -0.2, 0.2)), 0.6, 1.5),
        "kernel_bulk_in": normal_values(key_of[6], (NRAD, NLAT, NLON), 1.0, 6.0, ((0, 2), (1, 4), (2, 4)), jnp.float32),
        "kernel_density_in": normal_values(key_of[7], (NRAD, NLAT, NLON), 1.0, 6.0, ((0, 2), (1, 4), (2, 4)), jnp.float32),
    }


coef_near = 9.0 / 8.0
coef_far = -1.0 / 24.0


def pad_all(field, width):
    field = jnp.pad(field, ((0, 0), (0, 0), (width, width)), mode="wrap")
    return jnp.pad(field, ((width, width), (width, width), (0, 0)))


def piece(field, first, last, axis_num):
    return lax.slice_in_dim(field, first, last, axis=axis_num)


def operate(adj_pad, fwd_pad, buoy_pad):
    lap_adj = None
    lap_fwd = None
    rho_term = None
    for dim_index in range(3):
        arrays = []
        for source in (adj_pad, fwd_pad, buoy_pad):
            for other in range(3):
                if other != dim_index:
                    source = piece(source, 3, source.shape[other] - 3, other)
            arrays.append(source)
        adj_part, fwd_part, buoy_part = arrays
        length = adj_part.shape[dim_index]

        def faces(field):
            near = piece(field, 2, length - 1, dim_index) - piece(field, 1, length - 2, dim_index)
            far = piece(field, 3, length, dim_index) - piece(field, 0, length - 3, dim_index)
            return coef_near * near + coef_far * far

        face_buoy = 0.5 * (piece(buoy_part, 1, length - 2, dim_index) + piece(buoy_part, 2, length - 1, dim_index))
        grad_adj = faces(adj_part)
        grad_fwd = faces(fwd_part)
        count = length - 3

        def diverge(flux):
            near = piece(flux, 2, count - 1, dim_index) - piece(flux, 1, count - 2, dim_index)
            far = piece(flux, 3, count, dim_index) - piece(flux, 0, count - 3, dim_index)
            return coef_near * near + coef_far * far

        term_adj = diverge(face_buoy * grad_adj)
        term_fwd = diverge(face_buoy * grad_fwd)
        product = face_buoy * grad_adj * grad_fwd
        term_rho = 0.5 * (piece(product, 2, count - 1, dim_index) + piece(product, 1, count - 2, dim_index))
        if lap_adj is None:
            lap_adj, lap_fwd, rho_term = term_adj, term_fwd, term_rho
        else:
            lap_adj = lap_adj + term_adj
            lap_fwd = lap_fwd + term_fwd
            rho_term = rho_term + term_rho
    return lap_adj, lap_fwd, rho_term


def reference(adj_now, adj_next, fwd_now, fwd_next, stiffness, buoyancy, kernel_bulk_in, kernel_density_in):
    buoy_pad = pad_all(buoyancy, 3)
    kernel_bulk = kernel_bulk_in
    kernel_density = kernel_density_in
    for turn_index in range(STEPS):
        lap_adj, lap_fwd, rho_term = operate(pad_all(adj_now, 3), pad_all(fwd_now, 3), buoy_pad)
        kernel_bulk = kernel_bulk + adj_now * (stiffness * lap_fwd)
        kernel_density = kernel_density + rho_term
        new_adj = 2.0 * adj_now - adj_next + stiffness * lap_adj
        new_fwd = 2.0 * fwd_now - fwd_next + stiffness * lap_fwd
        adj_next, adj_now = adj_now, new_adj
        fwd_next, fwd_now = fwd_now, new_fwd
    return adj_now, adj_next, fwd_now, fwd_next, kernel_bulk, kernel_density
```

```python
import jax
import jax.numpy as jnp
from jax import lax
from jax.experimental import pallas as pl
from jax.experimental.pallas import tpu as pltpu
from jax.sharding import PartitionSpec as P

F32 = jnp.float32
SUB = 8
LAP_SCALE = 1.0 / 1152.0
RHO_SCALE = 1.0 / 2304.0
WIDTHS = (6, 6, 6, 3, 3, 3)
OFFSETS = (0, 6, 12, 21, 24, 27)
SEGMENT = 32
VMEM = pl.BlockSpec(memory_space=pltpu.VMEM)
PARAMS = pltpu.CompilerParams(vmem_limit_bytes=24 * 1024 * 1024)


def iotas(lanes):
    return (
        lax.broadcasted_iota(jnp.int32, (SUB, lanes), 0),
        lax.broadcasted_iota(jnp.int32, (SUB, lanes), 1),
    )


def rolled(x, shift, axis):
    size = x.shape[axis]
    shift = shift % size
    return x if shift == 0 else pltpu.roll(x, shift, axis)


def lane_shift(here, there, by, lane):
    size = here.shape[1]
    if by > 0:
        return rolled(jnp.where(lane < by, there, here), size - by, 1)
    return rolled(jnp.where(lane >= size + by, there, here), -by, 1)


def row_shift(tiles, t, by, sub):
    if by > 0:
        return rolled(jnp.where(sub < by, tiles[(t + 1) % len(tiles)], tiles[t]), SUB - by, 0)
    return rolled(jnp.where(sub >= SUB + by, tiles[t - 1], tiles[t]), -by, 0)


def slope(ahead, here, ahead2, behind):
    return 27.0 * (ahead - here) - (ahead2 - behind)


def pack_three(a, b, c, low, sub):
    if low:
        return jnp.where(sub < 3, a, jnp.where(sub < 6, rolled(b, 3, 0), rolled(c, 6, 0)))
    return jnp.where(sub >= 5, a, jnp.where(sub >= 2, rolled(b, -3, 0), rolled(c, -6, 0)))


def unpack_three(x, low):
    sign = -1 if low else 1
    return x, rolled(x, 3 * sign, 0), rolled(x, 6 * sign, 0)


def edges_kernel(*refs):
    sources, fields, (to_right, to_left, to_core), sems = refs[:6], refs[6:12], refs[12:15], refs[15]
    copies = [pltpu.make_async_copy(x, y, sems.at[k]) for k, (x, y) in enumerate(zip(sources, fields))]
    for copy in copies:
        copy.start()
    for copy in copies:
        copy.wait()
    layers, rows, lanes = fields[0].shape
    _, lane = iotas(lanes)
    core = lax.axis_index("rad")
    per = lanes // SEGMENT
    for group in range(to_right.shape[0]):
        for t in range(rows // SUB):
            at = pl.ds(t * SUB, SUB)
            right = left = None
            for s in range(per):
                layer = group * per + s
                if layer >= layers:
                    break
                for f, (width, offset) in enumerate(zip(WIDTHS, OFFSETS)):
                    first = s * SEGMENT + offset
                    x = rolled(fields[f][layer, at, :], first + width, 1)
                    second = first + width
                    wrap = second + width - lanes
                    mask = lane >= second
                    if wrap > 0:
                        mask = mask | (lane < wrap)
                    right = x if right is None else jnp.where(lane >= first, x, right)
                    left = x if left is None else jnp.where(mask, x, left)
            to_right[group, at, :] = right
            to_left[group, at, :] = left
    at = 0
    for f, width in enumerate(WIDTHS):
        to_core[at : at + width] = fields[f][pl.ds((layers - width) * (1 - core), width)]
        at += width


def halo_kernel(*refs):
    fields = refs[:6]
    from_left, from_right, from_core = refs[6:9]
    halo, to_first, to_second, to_core = refs[9:]
    layers, rows, lanes = fields[0].shape
    tiles = rows // SUB
    sub, lane = iotas(lanes)
    core = lax.axis_index("rad")
    even = lax.axis_index("lat") % 2 == 0
    per = lanes // SEGMENT
    for layer in range(layers):
        group, s = divmod(layer, per)
        for t in range(tiles):
            at = pl.ds(t * SUB, SUB)
            left, right = from_left[group, at, :], from_right[group, at, :]
            for f, (width, offset) in enumerate(zip(WIDTHS, OFFSETS)):
                first = s * SEGMENT + offset
                mask = (lane >= first) & (lane < first + width)
                halo[f, layer, at, :] = rolled(jnp.where(mask, left, right), -first - width, 1)

    def send(k, low, high):
        to_first[k] = jnp.where(even, high, low)
        to_second[k] = jnp.where(even, low, high)

    bottom, top = pl.ds(0, SUB), pl.ds(rows - SUB, SUB)
    for layer in range(layers):
        adj, fwd, buoy, adj2, fwd2, stiff = (x[layer, bottom, :] for x in fields)
        low = (
            adj,
            fwd,
            jnp.where(sub < 5, buoy, rolled(adj2, 5, 0)),
            jnp.where(sub < 3, fwd2, rolled(stiff, 3, 0)),
        )
        adj, fwd, buoy, adj2, fwd2, stiff = (x[layer, top, :] for x in fields)
        high = (
            adj,
            fwd,
            jnp.where(sub >= 3, buoy, rolled(adj2, 3, 0)),
            jnp.where(sub >= 5, fwd2, rolled(stiff, -3, 0)),
        )
        for k in range(4):
            send(4 * layer + k, low[k], high[k])
    for e in range(3):
        low, high = (
            pack_three(*(from_core[6 * f + 3 * core + e, at, :] for f in range(3)), is_low, sub)
            for at, is_low in ((bottom, True), (top, False))
        )
        send(4 * layers + e, low, high)
    both = []
    for at, is_low in ((bottom, True), (top, False)):
        packed = None
        for layer in range(layers):
            x = pack_three(*(halo[f, layer, at, :] for f in range(3)), is_low, sub)
            x = rolled(x, 16 * layer + 6, 1)
            packed = x if packed is None else jnp.where(lane >= 16 * layer, x, packed)
        both.append(packed)
    send(4 * layers + 3, *both)
    for f in range(3):
        to_core[3 * f : 3 * f + 3] = halo[f, pl.ds((layers - 3) * (1 - core), 3)]


def radial(p_at, b_at, layers):
    flux, rho = [], []
    p = [[p_at(f, k) for k in range(-3, layers + 3)] for f in range(2)]
    b = [b_at(k) for k in range(-2, layers + 2)]
    for k in range(layers + 3):
        buoy = b[k] + b[k + 1]
        grads = [slope(x[k + 2], x[k + 1], x[k + 3], x[k]) for x in p]
        flux.append([buoy * g for g in grads])
        rho.append(flux[k][0] * grads[1])
    out = []
    for k in range(layers):
        laps = [slope(flux[k + 2][f], flux[k + 1][f], flux[k + 3][f], flux[k][f]) for f in range(2)]
        out.append((laps[0], laps[1], rho[k + 1] + rho[k + 2]))
    return out


def longitudinal(here, there, lane, want_there, want_rho):
    flux, rho = [], []
    for x, y in ((here, there), (there, here)):
        buoy = x[2] + lane_shift(x[2], y[2], 1, lane)
        grads = [
            slope(
                lane_shift(x[f], y[f], 1, lane),
                x[f],
                lane_shift(x[f], y[f], 2, lane),
                lane_shift(x[f], y[f], -1, lane),
            )
            for f in range(2)
        ]
        flux.append([buoy * g for g in grads])
        rho.append(flux[-1][0] * grads[1])
    laps = []
    for x, y in ((0, 1), (1, 0))[: 2 if want_there else 1]:
        laps.append(
            [
                slope(
                    flux[x][f],
                    lane_shift(flux[x][f], flux[y][f], -1, lane),
                    lane_shift(flux[x][f], flux[y][f], 1, lane),
                    lane_shift(flux[x][f], flux[y][f], -2, lane),
                )
                for f in range(2)
            ]
        )
    density = rho[0] + lane_shift(rho[0], rho[1], -1, lane) if want_rho else None
    return laps, density


def latitudinal(adj, fwd, buoy, sub, wanted, want_rho):
    count = len(adj)
    flux, rho = ([], []), []
    for t in range(count):
        face = buoy[t] + row_shift(buoy, t, 1, sub)
        grads = [
            slope(row_shift(x, t, 1, sub), x[t], row_shift(x, t, 2, sub), row_shift(x, t, -1, sub))
            for x in (adj, fwd)
        ]
        for f in range(2):
            flux[f].append(face * grads[f])
        rho.append(flux[0][t] * grads[1])
    out = []
    for t in range(wanted):
        laps = [
            slope(x[t], row_shift(x, t, -1, sub), row_shift(x, t, 1, sub), row_shift(x, t, -2, sub))
            for x in flux
        ]
        out.append((laps[0], laps[1], rho[t] + row_shift(rho, t, -1, sub) if want_rho else None))
    return out


def steps_kernel(*refs):
    fields, (bulk_in, density_in) = refs[:6], refs[6:8]
    halo, from_core, from_core2, from_first, from_second = refs[8:13]
    adj_out, adj_out2, fwd_out, fwd_out2, bulk, density = refs[13:19]
    wide, wide_halo, first, first_halo, part, part_halo = refs[19:]
    layers, rows, lanes = fields[0].shape
    tiles = rows // SUB
    sub, lane = iotas(lanes)
    core = lax.axis_index("rad")
    even = lax.axis_index("lat") % 2 == 0
    ahead, behind = tiles, tiles + 1
    zero = jnp.zeros((SUB, lanes), F32)

    def at(t):
        return pl.ds(t * SUB, SUB)

    near = (layers + 6) * (1 - core) + 3 * core
    for f in range(3):
        for layer in range(layers):
            for t in range(tiles):
                wide[f, layer + 6, t] = fields[f][layer, at(t), :]
                wide_halo[f, layer + 3, t] = halo[f, layer, at(t), :]
        for k in range(6):
            for t in range(tiles):
                wide[f, (layers + 6) * (1 - core) + k, t] = from_core[6 * f + k, at(t), :]
        for k in range(3):
            for t in range(tiles):
                wide_halo[f, (layers + 3) * (1 - core) + k, t] = from_core2[3 * f + k, at(t), :]
                wide_halo[f, (layers + 3) * core + k, t] = zero
            for t in range(tiles + 2):
                wide[f, 3 + (layers + 3) * core + k, t] = zero
            for t in range(tiles):
                for g in range(2):
                    first[g, (layers + 3) * core + k, t] = zero

    def received(k):
        one, two = from_first[k], from_second[k]
        return jnp.where(even, one, two), jnp.where(even, two, one)

    for e in range(3):
        low, high = received(4 * layers + e)
        for f, (x, y) in enumerate(zip(unpack_three(low, True), unpack_three(high, False))):
            wide[f, near + e, ahead] = x
            wide[f, near + e, behind] = y
    low, high = received(4 * layers + 3)
    for layer in range(layers):
        x, y = (rolled(z, -6 - 16 * layer, 1) for z in (low, high))
        for f, (u, v) in enumerate(zip(unpack_three(x, True), unpack_three(y, False))):
            wide_halo[f, layer + 3, ahead] = u
            wide_halo[f, layer + 3, behind] = v
        for f in range(3):
            low2, high2 = received(4 * layer + f)
            wide[f, layer + 6, ahead] = low2
            wide[f, layer + 6, behind] = high2

    start = 6 - 3 * core
    for t in range(tiles):
        terms = radial(
            lambda f, k: wide[f, start + k, t], lambda k: wide[2, start + k, t], layers + 3
        )
        for k, term in enumerate(terms):
            for g in range(3):
                part[g, start - 3 + k, t] = term[g]
        terms = radial(
            lambda f, k: wide_halo[f, 3 + k, t], lambda k: wide_halo[2, 3 + k, t], layers
        )
        for k, term in enumerate(terms):
            for g in range(2):
                part_halo[g, k, t] = term[g]
    for t in (ahead, behind):
        terms = radial(lambda f, k: wide[f, 6 + k, t], lambda k: wide[2, 6 + k, t], layers)
        for k, term in enumerate(terms):
            for g in range(2):
                part[g, 3 + k, t] = term[g]

    def own(layer, carry):
        here = [[wide[f, layer + 6, t] for t in range(tiles + 2)] for f in range(3)]
        there = [[wide_halo[f, layer + 3, t] for t in range(tiles + 2)] for f in range(3)]
        lat = latitudinal(*here, sub, tiles + 2, True)
        lat_halo = latitudinal(*there, sub, tiles, False)
        low, high = received(4 * layer + 2)
        low3, high3 = received(4 * layer + 3)
        before = (
            (rolled(low, -5, 0), low3, rolled(low3, -3, 0)),
            (rolled(high, 5, 0), high3, rolled(high3, 3, 0)),
        )
        for t in range(tiles + 2):
            inside = t < tiles
            laps, rho = longitudinal(
                [x[t] for x in here], [x[t] for x in there], lane, inside, inside
            )
            if inside:
                adj2, fwd2, stiff = (fields[f][layer, at(t), :] for f in range(3, 6))
            else:
                adj2, fwd2, stiff = before[t - tiles]
            stiff = stiff * LAP_SCALE
            update = []
            for g, past in enumerate((adj2, fwd2)):
                update.append(stiff * (part[g, layer + 3, t] + lat[t][g] + laps[0][g]))
                first[g, layer + 3, t] = 2.0 * here[g][t] - past + update[g]
            if inside:
                bulk[layer, at(t), :] = bulk_in[layer, at(t), :] + here[0][t] * update[1]
                density[layer, at(t), :] = density_in[layer, at(t), :] + RHO_SCALE * (
                    part[2, layer + 3, t] + lat[t][2] + rho
                )
                stiff = halo[5, layer, at(t), :] * LAP_SCALE
                for g in range(2):
                    first_halo[g, layer, t] = (
                        2.0 * there[g][t]
                        - halo[3 + g, layer, at(t), :]
                        + stiff * (part_halo[g, layer, t] + lat_halo[t][g] + laps[1][g])
                    )
        return carry

    lax.fori_loop(0, layers, own, 0)

    def other(e, carry):
        here = [[wide[f, near + e, t] for t in range(tiles + 2)] for f in range(3)]
        lat = latitudinal(*here, sub, tiles, False)
        for t in range(tiles):
            there = [wide_halo[f, (layers + 3) * (1 - core) + e, t] for f in range(3)]
            laps, _ = longitudinal([x[t] for x in here], there, lane, False, False)
            stiff = from_core[24 + e, at(t), :] * LAP_SCALE
            for g in range(2):
                first[g, near - 3 + e, t] = (
                    2.0 * here[g][t]
                    - from_core[18 + 3 * g + e, at(t), :]
                    + stiff * (part[g, near - 3 + e, t] + lat[t][g] + laps[0][g])
                )
        return carry

    lax.fori_loop(0, 3, other, 0)

    for t in range(tiles):
        terms = radial(lambda f, k: first[f, 3 + k, t], lambda k: wide[2, 6 + k, t], layers)
        for k, term in enumerate(terms):
            for g in range(3):
                part[g, 3 + k, t] = term[g]

    def last(layer, carry):
        here = [[first[f, layer + 3, t] for t in range(tiles + 2)] for f in range(2)]
        here.append([wide[2, layer + 6, t] for t in range(tiles + 2)])
        lat = latitudinal(*here, sub, tiles, True)
        for t in range(tiles):
            there = [first_halo[0, layer, t], first_halo[1, layer, t], wide_halo[2, layer + 3, t]]
            laps, rho = longitudinal([x[t] for x in here], there, lane, False, True)
            stiff = fields[5][layer, at(t), :] * LAP_SCALE
            update = [stiff * (part[g, layer + 3, t] + lat[t][g] + laps[0][g]) for g in range(2)]
            for g, (now, before) in enumerate(((adj_out, adj_out2), (fwd_out, fwd_out2))):
                before[layer, at(t), :] = here[g][t]
                now[layer, at(t), :] = 2.0 * here[g][t] - fields[g][layer, at(t), :] + update[g]
            bulk[layer, at(t), :] += here[0][t] * update[1]
            density[layer, at(t), :] += RHO_SCALE * (part[2, layer + 3, t] + lat[t][2] + rho)
        return carry

    lax.fori_loop(0, layers, last, 0)


def pairs(count, start):
    firsts = range(start, count - 1, 2)
    return [p for i in firsts for p in ((i, i + 1), (i + 1, i))]


def shards(
    adj_now, adj_next, fwd_now, fwd_next, stiffness, buoyancy, kernel_bulk_in, kernel_density_in
):
    layers, rows, lanes = adj_now.shape
    tiles = rows // SUB
    fields = (adj_now, fwd_now, buoyancy, adj_next, fwd_next, stiffness)
    groups = -(-layers // (lanes // SEGMENT))
    edge = pltpu.VMEM((groups, rows, lanes), F32)
    *fields, to_right, to_left, to_core = pl.pallas_call(
        edges_kernel,
        out_shape=(pltpu.VMEM((layers, rows, lanes), F32),) * 6
        + (edge, edge, pltpu.VMEM((sum(WIDTHS), rows, lanes), F32)),
        in_specs=[pl.BlockSpec(memory_space=pltpu.HBM)] * 6,
        out_specs=(VMEM,) * 9,
        scratch_shapes=[pltpu.SemaphoreType.DMA((6,))],
        compiler_params=PARAMS,
    )(*(pltpu.with_memory_space_constraint(x, pltpu.HBM) for x in fields))
    around = lax.axis_size("lon")
    ring = [(i, (i + 1) % around) for i in range(around)]
    swap = [(0, 1), (1, 0)]
    from_left = lax.ppermute(to_right, "lon", ring)
    from_right = lax.ppermute(to_left, "lon", [(b, a) for a, b in ring])
    from_core = lax.ppermute(to_core, "rad", swap)
    lat_edge = pltpu.VMEM((4 * layers + 4, SUB, lanes), F32)
    halo, to_first, to_second, to_core = pl.pallas_call(
        halo_kernel,
        out_shape=(
            pltpu.VMEM((6, layers, rows, lanes), F32),
            lat_edge,
            lat_edge,
            pltpu.VMEM((9, rows, lanes), F32),
        ),
        in_specs=[VMEM] * 9,
        out_specs=(VMEM,) * 4,
        compiler_params=PARAMS,
    )(*fields, from_left, from_right, from_core)
    count = lax.axis_size("lat")
    from_first = lax.ppermute(to_first, "lat", pairs(count, 0))
    from_second = lax.ppermute(to_second, "lat", pairs(count, 1))
    from_core2 = lax.ppermute(to_core, "rad", swap)
    block = jax.ShapeDtypeStruct((layers, rows, lanes), F32)
    return pl.pallas_call(
        steps_kernel,
        out_shape=(block,) * 6,
        in_specs=[VMEM] * 13,
        out_specs=(VMEM,) * 6,
        scratch_shapes=[
            pltpu.VMEM((3, layers + 12, tiles + 2, SUB, lanes), F32),
            pltpu.VMEM((3, layers + 6, tiles + 2, SUB, lanes), F32),
            pltpu.VMEM((2, layers + 6, tiles + 2, SUB, lanes), F32),
            pltpu.VMEM((2, layers, tiles, SUB, lanes), F32),
            pltpu.VMEM((3, layers + 6, tiles + 2, SUB, lanes), F32),
            pltpu.VMEM((2, layers, tiles, SUB, lanes), F32),
        ],
        compiler_params=PARAMS,
    )(
        *fields,
        kernel_bulk_in,
        kernel_density_in,
        halo,
        from_core,
        from_core2,
        from_first,
        from_second,
    )


def solution(mesh):
    spec = P("rad", "lat", "lon")
    return jax.shard_map(
        shards, mesh=mesh, in_specs=(spec,) * 8, out_specs=(spec,) * 6, check_vma=False
    )
```

```python
import jax
import jax.numpy as jnp
from jax import lax
from jax.experimental import pallas as pl
from jax.experimental.pallas import tpu as pltpu
from jax.sharding import PartitionSpec as P

F32 = jnp.float32
SUB = 8
LAP_SCALE = 1.0 / 1152.0
RHO_SCALE = 1.0 / 2304.0
WIDTHS = (6, 6, 6, 3, 3, 3)
OFFSETS = (0, 6, 12, 21, 24, 27)
SEGMENT = 32
VMEM = pl.BlockSpec(memory_space=pltpu.VMEM)
PARAMS = pltpu.CompilerParams(vmem_limit_bytes=24 * 1024 * 1024)
HEAVY = pl.CostEstimate(flops=4000000000, bytes_accessed=1000000, transcendentals=0)


def iotas(lanes):
    return (
        lax.broadcasted_iota(jnp.int32, (SUB, lanes), 0),
        lax.broadcasted_iota(jnp.int32, (SUB, lanes), 1),
    )


def rolled(x, shift, axis):
    size = x.shape[axis]
    shift = shift % size
    return x if shift == 0 else pltpu.roll(x, shift, axis)


def lane_shift(here, there, by, lane):
    size = here.shape[1]
    if by > 0:
        return rolled(jnp.where(lane < by, there, here), size - by, 1)
    return rolled(jnp.where(lane >= size + by, there, here), -by, 1)


def row_shift(tiles, t, by, sub):
    if by > 0:
        return rolled(jnp.where(sub < by, tiles[(t + 1) % len(tiles)], tiles[t]), SUB - by, 0)
    return rolled(jnp.where(sub >= SUB + by, tiles[t - 1], tiles[t]), -by, 0)


def slope(ahead, here, ahead2, behind):
    return 27.0 * (ahead - here) - (ahead2 - behind)


def pack_three(a, b, c, low, sub):
    if low:
        return jnp.where(sub < 3, a, jnp.where(sub < 6, rolled(b, 3, 0), rolled(c, 6, 0)))
    return jnp.where(sub >= 5, a, jnp.where(sub >= 2, rolled(b, -3, 0), rolled(c, -6, 0)))


def unpack_three(x, low):
    sign = -1 if low else 1
    return x, rolled(x, 3 * sign, 0), rolled(x, 6 * sign, 0)


def edges_kernel(*refs):
    sources, fields, (to_right, to_left, to_core), sems = refs[:6], refs[6:12], refs[12:15], refs[15]
    copies = [pltpu.make_async_copy(x, y, sems.at[k]) for k, (x, y) in enumerate(zip(sources, fields))]
    for copy in copies:
        copy.start()
    for copy in copies:
        copy.wait()
    layers, rows, lanes = fields[0].shape
    _, lane = iotas(lanes)
    core = lax.axis_index("rad")
    per = lanes // SEGMENT
    for group in range(to_right.shape[0]):
        for t in range(rows // SUB):
            at = pl.ds(t * SUB, SUB)
            right = left = None
            for s in range(per):
                layer = group * per + s
                if layer >= layers:
                    break
                for f, (width, offset) in enumerate(zip(WIDTHS, OFFSETS)):
                    first = s * SEGMENT + offset
                    x = rolled(fields[f][layer, at, :], first + width, 1)
                    second = first + width
                    wrap = second + width - lanes
                    mask = lane >= second
                    if wrap > 0:
                        mask = mask | (lane < wrap)
                    right = x if right is None else jnp.where(lane >= first, x, right)
                    left = x if left is None else jnp.where(mask, x, left)
            to_right[group, at, :] = right
            to_left[group, at, :] = left
    at = 0
    for f, width in enumerate(WIDTHS):
        to_core[at : at + width] = fields[f][pl.ds((layers - width) * (1 - core), width)]
        at += width


def radial(p_at, b_at, layers):
    flux, rho = [], []
    p = [[p_at(f, k) for k in range(-3, layers + 3)] for f in range(2)]
    b = [b_at(k) for k in range(-2, layers + 2)]
    for k in range(layers + 3):
        buoy = b[k] + b[k + 1]
        grads = [slope(x[k + 2], x[k + 1], x[k + 3], x[k]) for x in p]
        flux.append([buoy * g for g in grads])
        rho.append(flux[k][0] * grads[1])
    out = []
    for k in range(layers):
        laps = [slope(flux[k + 2][f], flux[k + 1][f], flux[k + 3][f], flux[k][f]) for f in range(2)]
        out.append((laps[0], laps[1], rho[k + 1] + rho[k + 2]))
    return out


def longitudinal(here, there, lane, want_there, want_rho):
    flux, rho = [], []
    for x, y in ((here, there), (there, here)):
        buoy = x[2] + lane_shift(x[2], y[2], 1, lane)
        grads = [
            slope(
                lane_shift(x[f], y[f], 1, lane),
                x[f],
                lane_shift(x[f], y[f], 2, lane),
                lane_shift(x[f], y[f], -1, lane),
            )
            for f in range(2)
        ]
        flux.append([buoy * g for g in grads])
        rho.append(flux[-1][0] * grads[1])
    laps = []
    for x, y in ((0, 1), (1, 0))[: 2 if want_there else 1]:
        laps.append(
            [
                slope(
                    flux[x][f],
                    lane_shift(flux[x][f], flux[y][f], -1, lane),
                    lane_shift(flux[x][f], flux[y][f], 1, lane),
                    lane_shift(flux[x][f], flux[y][f], -2, lane),
                )
                for f in range(2)
            ]
        )
    density = rho[0] + lane_shift(rho[0], rho[1], -1, lane) if want_rho else None
    return laps, density


def unpacked(left, right, f, s, lane):
    width, offset = WIDTHS[f], OFFSETS[f]
    first = s * SEGMENT + offset
    mask = (lane >= first) & (lane < first + width)
    return rolled(jnp.where(mask, left, right), -first - width, 1)


def lat_flux(ring, t, sub):
    adj, fwd, buoy = ring
    face = buoy[t] + row_shift(buoy, t, 1, sub)
    grads = [
        slope(row_shift(x, t, 1, sub), x[t], row_shift(x, t, 2, sub), row_shift(x, t, -1, sub))
        for x in (adj, fwd)
    ]
    flux = [face * g for g in grads]
    return flux[0], flux[1], flux[0] * grads[1]


def lat_terms(flux, t, sub, want_rho):
    adj, fwd, rho = ([x[k] for x in flux] for k in range(3))
    laps = [
        slope(x[t], row_shift(x, t, -1, sub), row_shift(x, t, 1, sub), row_shift(x, t, -2, sub))
        for x in (adj, fwd)
    ]
    return laps[0], laps[1], rho[t] + row_shift(rho, t, -1, sub) if want_rho else None


def lat_inner(ring, sub, want_rho):
    count = len(ring[0])
    flux = [list(lat_flux(ring, t, sub)) for t in range(count)]
    zero = jnp.zeros_like(ring[0][0])
    for k in range(3):
        flux[0][k] = jnp.where(sub >= 1, flux[0][k], zero)
        flux[-1][k] = jnp.where(sub < SUB - 2, flux[-1][k], zero)
    flux.append([zero] * 3)
    return [lat_terms(flux, t, sub, want_rho) for t in range(count)]


def lat_outer(adj, fwd, buoy, sub):
    ring = ([adj], [fwd], [buoy])
    mask = (sub >= SUB - 2) | (sub < 1)
    flux = [[jnp.where(mask, x, 0.0) for x in lat_flux(ring, 0, sub)]]
    return lat_terms(flux, 0, sub, True)


def places(core, layers):
    return (layers + 3) * (1 - core), (layers + 3) * core


def inner_kernel(*refs):
    fields, from_core = refs[:6], refs[6]
    wide, part, to_first, to_second = refs[7:]
    layers, rows, lanes = fields[0].shape
    tiles = rows // SUB
    sub, lane = iotas(lanes)
    core = lax.axis_index("rad")
    even = lax.axis_index("lat") % 2 == 0
    near, border = places(core, layers)
    zero = jnp.zeros((SUB, lanes), F32)

    def at(t):
        return pl.ds(t * SUB, SUB)

    for f in range(3):
        for t in range(tiles):
            for layer in range(layers):
                wide[f, layer + 6, t] = fields[f][layer, at(t), :]
            for k in range(6):
                wide[f, (layers + 6) * (1 - core) + k, t] = from_core[6 * f + k, at(t), :]
            for k in range(3):
                wide[f, border + 3 + k, t] = zero

    def send(k, low, high):
        to_first[k] = jnp.where(even, high, low)
        to_second[k] = jnp.where(even, low, high)

    ends = ((0, True), (tiles - 1, False))
    third = [None, None]
    for layer in range(layers):
        send(
            layers + layer,
            *(pack_three(*(x[layer, at(t), :] for x in fields[:3]), low, sub) for t, low in ends),
        )
        for k, row in enumerate((2, SUB - 3)):
            x = rolled(fields[5][layer, at(ends[k][0]), :], layer - row, 0)
            third[k] = x if layer == 0 else jnp.where(sub == layer, x, third[k])
    send(2 * layers, *third)
    for e in range(3):
        send(
            2 * layers + 1 + e,
            *(pack_three(*(wide[f, near + 3 + e, t] for f in range(3)), low, sub) for t, low in ends),
        )

    start = 6 - 3 * core
    for t in range(tiles):
        terms = radial(
            lambda f, k: wide[f, start + k, t], lambda k: wide[2, start + k, t], layers + 3
        )
        for k, term in enumerate(terms):
            for g in range(3):
                part[g, start - 3 + k, t] = term[g]

    def own(layer, carry):
        terms = lat_inner([[wide[f, layer + 6, t] for t in range(tiles)] for f in range(3)], sub, True)
        for t in range(tiles):
            for g in range(3):
                part[g, layer + 3, t] += terms[t][g]
        return carry

    lax.fori_loop(0, layers, own, 0, unroll=True)

    def other(e, carry):
        terms = lat_inner(
            [[wide[f, near + 3 + e, t] for t in range(tiles)] for f in range(3)], sub, False
        )
        for t in range(tiles):
            for g in range(2):
                part[g, near + e, t] += terms[t][g]
        return carry

    lax.fori_loop(0, 3, other, 0, unroll=True)


def turn_kernel(*refs):
    fields, from_left, from_right, part = refs[:6], refs[6], refs[7], refs[8]
    to_first, to_second, to_core, edges = refs[11:]
    layers, rows, lanes = fields[0].shape
    tiles = rows // SUB
    sub, lane = iotas(lanes)
    core = lax.axis_index("rad")
    even = lax.axis_index("lat") % 2 == 0
    per = lanes // SEGMENT

    def send(k, low, high):
        to_first[k] = jnp.where(even, high, low)
        to_second[k] = jnp.where(even, low, high)

    def ends(ref, *index):
        low, high = (ref[(*index, pl.ds(t * SUB, SUB), slice(None))] for t in (0, tiles - 1))
        return jnp.where(sub < 4, low, high)

    group = (from_left.shape[0] - 1) * (1 - core)
    for k, ref in enumerate((from_left, from_right)):
        to_core[k] = ref[group]
    packed = [None, None]
    for g in range(from_left.shape[0]):
        left, right = ends(from_left, g), ends(from_right, g)
        for s in range(min(per, layers - g * per)):
            layer = g * per + s
            here = [ends(x, layer) for x in fields]
            there = [unpacked(left, right, f, s, lane) for f in range(3)]
            laps, _ = longitudinal(here[:3], there, lane, False, False)
            stiff = here[5] * LAP_SCALE
            made = []
            for f in range(2):
                before = jnp.where(sub < 4, part[f, layer + 3, 0], part[f, layer + 3, tiles - 1])
                made.append(2.0 * here[f] - here[3 + f] + stiff * (before + laps[0][f]))
            send(layer, *(pack_three(*made, here[5], low, sub) for low in (True, False)))
            for k, low in enumerate((True, False)):
                x = rolled(pack_three(*there, low, sub), 16 * layer + 6, 1)
                packed[k] = x if layer == 0 else jnp.where(lane >= 16 * layer, x, packed[k])
    send(2 * layers + 4, *packed)
    for k in range(2):
        edges[k] = packed[k]


def middle_kernel(*refs):
    fields, (bulk_in, density_in) = refs[:6], refs[6:8]
    from_left, from_right, from_core, from_core2, wide, part = refs[8:14]
    first, first_halo, rest_halo, flux_out, sums, done = refs[14:20]
    halo, wide_halo, part_halo = refs[20:]
    layers, rows, lanes = fields[0].shape
    tiles = rows // SUB
    sub, lane = iotas(lanes)
    core = lax.axis_index("rad")
    near, border = places(core, layers)
    per = lanes // SEGMENT
    zero = jnp.zeros((SUB, lanes), F32)
    inside = range(1, tiles - 1)

    def at(t):
        return pl.ds(t * SUB, SUB)

    for t in range(tiles):
        for layer in range(layers):
            group, s = divmod(layer, per)
            left, right = from_left[group, at(t), :], from_right[group, at(t), :]
            for f in range(6):
                x = unpacked(left, right, f, s, lane)
                if f < 3:
                    wide_halo[f, layer + 3, t] = x
                else:
                    halo[f - 3, layer, t] = x
                if f in (2, 5):
                    rest_halo[f // 3, layer, t] = x
        left, right = from_core2[0, at(t), :], from_core2[1, at(t), :]
        for f in range(3):
            for e in range(3):
                x, y = (unpacked(left, right, f, e + skip, lane) for skip in (0, per - 3))
                wide_halo[f, near + e, t] = jnp.where(core == 0, x, y)
                wide_halo[f, border + e, t] = zero
        for g in range(2):
            for k in range(3):
                first[g, border + k, t] = zero
        terms = radial(
            lambda f, k: wide_halo[f, 3 + k, t], lambda k: wide_halo[2, 3 + k, t], layers
        )
        for k, term in enumerate(terms):
            for g in range(2):
                part_halo[g, k, t] = term[g]

    def own(layer, carry):
        here = [[wide[f, layer + 6, t] for t in range(tiles)] for f in range(3)]
        there = [[wide_halo[f, layer + 3, t] for t in range(tiles)] for f in range(3)]
        lat_halo = lat_inner(there, sub, False)
        for t in range(tiles):
            laps, rho = longitudinal([x[t] for x in here], [x[t] for x in there], lane, True, True)
            stiff = fields[5][layer, at(t), :] * LAP_SCALE
            stiff_halo = halo[2, layer, t] * LAP_SCALE
            for g in range(2):
                update = stiff * (part[g, layer + 3, t] + laps[0][g])
                first[g, layer + 3, t] = 2.0 * here[g][t] - fields[3 + g][layer, at(t), :] + update
                first_halo[g, layer, t] = (
                    2.0 * there[g][t]
                    - halo[g, layer, t]
                    + stiff_halo * (part_halo[g, layer, t] + lat_halo[t][g] + laps[1][g])
                )
            sums[0, layer, t] = bulk_in[layer, at(t), :] + here[0][t] * update
            sums[1, layer, t] = density_in[layer, at(t), :] + RHO_SCALE * (
                part[2, layer + 3, t] + rho
            )
        return carry

    lax.fori_loop(0, layers, own, 0)

    def other(e, carry):
        for t in range(tiles):
            here = [wide[f, near + 3 + e, t] for f in range(3)]
            there = [wide_halo[f, near + e, t] for f in range(3)]
            laps, _ = longitudinal(here, there, lane, False, False)
            stiff = from_core[24 + e, at(t), :] * LAP_SCALE
            for g in range(2):
                first[g, near + e, t] = (
                    2.0 * here[g]
                    - from_core[18 + 3 * g + e, at(t), :]
                    + stiff * (part[g, near + e, t] + laps[0][g])
                )
        return carry

    lax.fori_loop(0, 3, other, 0, unroll=True)

    for t in inside:
        terms = radial(lambda f, k: first[f, 3 + k, t], lambda k: wide[2, 6 + k, t], layers)
        for k, term in enumerate(terms):
            for g in range(3):
                part_halo[g, k, t] = term[g]

    def last(layer, carry):
        here = [[first[f, layer + 3, t] for t in range(tiles)] for f in range(2)]
        here.append([wide[2, layer + 6, t] for t in range(tiles)])
        flux = [lat_flux(here, t, sub) for t in range(tiles)]
        for k in range(3):
            for n, t in enumerate((1, tiles - 2)):
                flux_out[k, n, layer] = flux[t][k]
        for t in inside:
            lat = lat_terms(flux, t, sub, True)
            there = [first_halo[0, layer, t], first_halo[1, layer, t], wide_halo[2, layer + 3, t]]
            laps, rho = longitudinal([x[t] for x in here], there, lane, False, True)
            stiff = fields[5][layer, at(t), :] * LAP_SCALE
            for g in range(2):
                update = stiff * (part_halo[g, layer, t] + lat[g] + laps[0][g])
                done[2 * g, layer, at(t - 1), :] = (
                    2.0 * here[g][t] - fields[g][layer, at(t), :] + update
                )
                done[2 * g + 1, layer, at(t - 1), :] = here[g][t]
            done[4, layer, at(t - 1), :] = sums[0, layer, t] + here[0][t] * update
            done[5, layer, at(t - 1), :] = sums[1, layer, t] + RHO_SCALE * (
                part_halo[2, layer, t] + lat[2] + rho
            )
        return carry

    lax.fori_loop(0, layers, last, 0, unroll=4)


def last_kernel(*refs):
    fields, from_core = refs[:6], refs[6]
    wide, first, first_halo, rest_halo, flux_in, sums, done = refs[7:14]
    edges, from_first, from_second = refs[14:17]
    outs = refs[17:23]
    fixed, fixed_halo, ring_buoy, part, made, sems = refs[23:]
    layers, rows, lanes = fields[0].shape
    tiles = rows // SUB
    sub, lane = iotas(lanes)
    core = lax.axis_index("rad")
    even = lax.axis_index("lat") % 2 == 0
    near, border = places(core, layers)
    zero = jnp.zeros((SUB, lanes), F32)
    ends = ((0, sub < 3), (tiles - 1, sub >= SUB - 3))
    copies = [
        pltpu.make_async_copy(done.at[k], out.at[:, pl.ds(SUB, rows - 2 * SUB), :], sems.at[k, 0])
        for k, out in enumerate(outs)
    ]
    for copy in copies:
        copy.start()

    def at(t):
        return pl.ds(t * SUB, SUB)

    def received(k):
        one, two = from_first[k], from_second[k]
        return jnp.where(even, two, one), jnp.where(even, one, two)

    def join(behind, ahead):
        return jnp.where(sub < 4, ahead, behind)

    def three(k):
        behind, ahead = received(k)
        return list(zip(unpack_three(behind, False), unpack_three(ahead, True)))

    def outer(own, halos):
        low = [jnp.where(sub < 4, x[0], h[0]) for x, h in zip(own, halos)]
        high = [jnp.where(sub < 4, h[1], x[1]) for x, h in zip(own, halos)]
        return lat_outer(*low, sub), lat_outer(*high, sub)

    for g in range(2):
        for k in range(3):
            for n in range(2):
                fixed[g, border + k, n] = zero

    halos = three(2 * layers + 4)
    mine = list(zip(unpack_three(edges[0], True), unpack_three(edges[1], False)))
    side = outer(mine, halos)
    for layer in range(layers):
        for n, (t, mask) in enumerate(ends):
            stiff = rest_halo[1, layer, t] * LAP_SCALE
            for g in range(2):
                lap = jnp.where(mask, rolled(side[n][g], -16 * layer - 6, 1), 0.0)
                fixed_halo[g, layer, n] = first_halo[g, layer, t] + stiff * lap

    for e in range(3):
        halos = three(2 * layers + 1 + e)
        mine = [(wide[f, near + 3 + e, 0], wide[f, near + 3 + e, tiles - 1]) for f in range(3)]
        side = outer(mine, halos)
        for n, (t, mask) in enumerate(ends):
            stiff = from_core[24 + e, at(t), :] * LAP_SCALE
            for g in range(2):
                lap = jnp.where(mask, side[n][g], 0.0)
                fixed[g, near + e, n] = first[g, near + e, t] + stiff * lap

    third = received(2 * layers)
    for layer in range(layers):
        halos = three(layers + layer)
        mine = [(x[layer, at(0), :], x[layer, at(tiles - 1), :]) for x in fields[:3]]
        side = outer(mine, halos)
        for n, (t, mask) in enumerate(ends):
            stiff = fields[5][layer, at(t), :] * LAP_SCALE
            for g in range(2):
                update = stiff * jnp.where(mask, side[n][g], 0.0)
                fixed[g, layer + 3, n] = first[g, layer + 3, t] + update
            made[4, layer, n] = sums[0, layer, t] + mine[0][n] * update
            made[5, layer, n] = sums[1, layer, t] + RHO_SCALE * jnp.where(mask, side[n][2], 0.0)
        adj, fwd, stiff = three(layer)
        low, high = (rolled(third[k], row - layer, 0) for k, row in enumerate((SUB - 3, 2)))
        stiff = jnp.where(
            sub < 4,
            jnp.where(sub == 2, high, stiff[1]),
            jnp.where(sub == SUB - 3, low, stiff[0]),
        )
        for g, x in enumerate((adj, fwd)):
            lap = join(side[0][g], side[1][g])
            fixed[g, layer + 3, 2] = join(*x) + stiff * LAP_SCALE * lap
        ring_buoy[layer] = join(*halos[2])

    for n, (t, _) in enumerate(ends):
        terms = radial(lambda f, k: fixed[f, 3 + k, n], lambda k: wide[2, 6 + k, t], layers)
        for k, term in enumerate(terms):
            for g in range(3):
                part[g, k, n] = term[g]

    def last(layer, carry):
        buoys = [wide[2, layer + 6, t] for t in (0, 1, tiles - 2, tiles - 1)]
        rings = [
            [fixed[f, layer + 3, 2], fixed[f, layer + 3, 0], first[f, layer + 3, 1]]
            + [first[f, layer + 3, tiles - 2], fixed[f, layer + 3, 1]]
            for f in range(2)
        ] + [[ring_buoy[layer], *buoys]]
        flux = [None] * 5
        for t in (0, 1, 4):
            flux[t] = lat_flux(rings, t, sub)
        for n in range(2):
            flux[2 + n] = [flux_in[k, n, layer] for k in range(3)]
        for n, (t, _) in enumerate(ends):
            k = (1, 4)[n]
            here = [x[k] for x in rings]
            lat = lat_terms(flux, k, sub, True)
            there = [fixed_halo[0, layer, n], fixed_halo[1, layer, n], rest_halo[0, layer, t]]
            laps, rho = longitudinal(here, there, lane, False, True)
            stiff = fields[5][layer, at(t), :] * LAP_SCALE
            for g in range(2):
                update = stiff * (part[g, layer, n] + lat[g] + laps[0][g])
                made[2 * g, layer, n] = 2.0 * here[g] - fields[g][layer, at(t), :] + update
                made[2 * g + 1, layer, n] = here[g]
            made[4, layer, n] += here[0] * update
            made[5, layer, n] += RHO_SCALE * (part[2, layer, n] + lat[2] + rho)
        return carry

    lax.fori_loop(0, layers, last, 0, unroll=True)
    for k, out in enumerate(outs):
        for n, (t, _) in enumerate(ends):
            copy = pltpu.make_async_copy(made.at[k, :, n], out.at[:, at(t), :], sems.at[k, 1 + n])
            copy.start()
            copies.append(copy)
    for copy in copies:
        copy.wait()


def pairs(count, start):
    firsts = range(start, count - 1, 2)
    return [p for i in firsts for p in ((i, i + 1), (i + 1, i))]


def call(kernel, out_shape, args, in_specs=None, out_specs=None, **more):
    return pl.pallas_call(
        kernel,
        out_shape=out_shape,
        in_specs=in_specs or [VMEM] * len(args),
        out_specs=out_specs or (VMEM,) * len(out_shape),
        compiler_params=PARAMS,
        **more,
    )(*args)


def shards(
    adj_now, adj_next, fwd_now, fwd_next, stiffness, buoyancy, kernel_bulk_in, kernel_density_in
):
    layers, rows, lanes = adj_now.shape
    tiles = rows // SUB
    fields = (adj_now, fwd_now, buoyancy, adj_next, fwd_next, stiffness)
    groups = -(-layers // (lanes // SEGMENT))
    around, count = lax.axis_size("lon"), lax.axis_size("lat")
    ring = [(i, (i + 1) % around) for i in range(around)]
    swap = [(0, 1), (1, 0)]

    def made(*shape):
        return pltpu.VMEM(shape, F32)

    block = (layers, rows, lanes)
    edge = made(groups, rows, lanes)
    hbm = pl.BlockSpec(memory_space=pltpu.HBM)
    *fields, to_right, to_left, to_core = call(
        edges_kernel,
        (made(*block),) * 6 + (edge, edge, made(sum(WIDTHS), rows, lanes)),
        [pltpu.with_memory_space_constraint(x, pltpu.HBM) for x in fields],
        in_specs=[hbm] * 6,
        scratch_shapes=[pltpu.SemaphoreType.DMA((6,))],
    )
    from_left = lax.ppermute(to_right, "lon", ring)
    from_right = lax.ppermute(to_left, "lon", [(b, a) for a, b in ring])
    from_core = lax.ppermute(to_core, "rad", swap)
    lat_edge = made(2 * layers + 5, SUB, lanes)
    wide, part, to_first, to_second = call(
        inner_kernel,
        (
            made(3, layers + 12, tiles, SUB, lanes),
            made(3, layers + 6, tiles, SUB, lanes),
            lat_edge,
            lat_edge,
        ),
        [*fields, from_core],
    )
    to_first, to_second, to_core, edges = call(
        turn_kernel,
        (lat_edge, lat_edge, made(2, rows, lanes), made(2, SUB, lanes)),
        [*fields, from_left, from_right, part, to_first, to_second],
        input_output_aliases={9: 0, 10: 1},
    )
    from_first = lax.ppermute(to_first, "lat", pairs(count, 0))
    from_second = lax.ppermute(to_second, "lat", pairs(count, 1))
    from_core2 = lax.ppermute(to_core, "rad", swap)
    first, first_halo, rest_halo, flux, sums, done = call(
        middle_kernel,
        (
            made(2, layers + 6, tiles, SUB, lanes),
            made(2, layers, tiles, SUB, lanes),
            made(2, layers, tiles, SUB, lanes),
            made(3, 2, layers, SUB, lanes),
            made(2, layers, tiles, SUB, lanes),
            made(6, layers, rows - 2 * SUB, lanes),
        ),
        [
            *fields,
            kernel_bulk_in,
            kernel_density_in,
            from_left,
            from_right,
            from_core,
            from_core2,
            wide,
            part,
        ],
        cost_estimate=HEAVY,
        scratch_shapes=[
            made(3, layers, tiles, SUB, lanes),
            made(3, layers + 6, tiles, SUB, lanes),
            made(3, layers, tiles, SUB, lanes),
        ],
    )
    return call(
        last_kernel,
        (jax.ShapeDtypeStruct(block, F32),) * 6,
        [
            *fields,
            from_core,
            wide,
            first,
            first_halo,
            rest_halo,
            flux,
            sums,
            done,
            edges,
            from_first,
            from_second,
        ],
        out_specs=(hbm,) * 6,
        scratch_shapes=[
            made(2, layers + 6, 3, SUB, lanes),
            made(2, layers, 2, SUB, lanes),
            made(layers, SUB, lanes),
            made(3, layers, 2, SUB, lanes),
            made(6, layers, 2, SUB, lanes),
            pltpu.SemaphoreType.DMA((6, 3)),
        ],
    )


def solution(mesh):
    spec = P("rad", "lat", "lon")
    return jax.shard_map(
        shards, mesh=mesh, in_specs=(spec,) * 8, out_specs=(spec,) * 6, check_vma=False
    )
```

```python
import jax
import jax.numpy as jnp
from jax import lax
from jax.experimental import pallas as pl
from jax.experimental.pallas import tpu as pltpu
from jax.sharding import PartitionSpec as P

F32 = jnp.float32
SUB = 8
LAP_SCALE = 1.0 / 1152.0
RHO_SCALE = 1.0 / 2304.0
WIDTHS = (6, 6, 6, 3, 3, 3)
OFFSETS = (0, 6, 12, 21, 24, 27)
SEGMENT = 32
VMEM = pl.BlockSpec(memory_space=pltpu.VMEM)
PARAMS = pltpu.CompilerParams(vmem_limit_bytes=24 * 1024 * 1024)
HEAVY = pl.CostEstimate(flops=4000000000, bytes_accessed=1000000, transcendentals=0)


def iotas(lanes):
    return (
        lax.broadcasted_iota(jnp.int32, (SUB, lanes), 0),
        lax.broadcasted_iota(jnp.int32, (SUB, lanes), 1),
    )


def rolled(x, shift, axis):
    size = x.shape[axis]
    shift = shift % size
    return x if shift == 0 else pltpu.roll(x, shift, axis)


def lane_shift(here, there, by, lane):
    size = here.shape[1]
    if by > 0:
        return rolled(jnp.where(lane < by, there, here), size - by, 1)
    return rolled(jnp.where(lane >= size + by, there, here), -by, 1)


def row_shift(tiles, t, by, sub):
    if by > 0:
        return rolled(jnp.where(sub < by, tiles[(t + 1) % len(tiles)], tiles[t]), SUB - by, 0)
    return rolled(jnp.where(sub >= SUB + by, tiles[t - 1], tiles[t]), -by, 0)


def slope(ahead, here, ahead2, behind):
    return 27.0 * (ahead - here) - (ahead2 - behind)


def pack_three(a, b, c, low, sub):
    if low:
        return jnp.where(sub < 3, a, jnp.where(sub < 6, rolled(b, 3, 0), rolled(c, 6, 0)))
    return jnp.where(sub >= 5, a, jnp.where(sub >= 2, rolled(b, -3, 0), rolled(c, -6, 0)))


def unpack_three(x, low):
    sign = -1 if low else 1
    return x, rolled(x, 3 * sign, 0), rolled(x, 6 * sign, 0)


def edges_kernel(*refs):
    sources, fields, (to_right, to_left, to_core), sems = refs[:6], refs[6:12], refs[12:15], refs[15]
    copies = [pltpu.make_async_copy(x, y, sems.at[k]) for k, (x, y) in enumerate(zip(sources, fields))]
    for copy in copies:
        copy.start()
    for copy in copies:
        copy.wait()
    layers, rows, lanes = fields[0].shape
    _, lane = iotas(lanes)
    core = lax.axis_index("rad")
    per = lanes // SEGMENT
    for group in range(to_right.shape[0]):
        for t in range(rows // SUB):
            at = pl.ds(t * SUB, SUB)
            right = left = None
            for s in range(per):
                layer = group * per + s
                if layer >= layers:
                    break
                for f, (width, offset) in enumerate(zip(WIDTHS, OFFSETS)):
                    first = s * SEGMENT + offset
                    x = rolled(fields[f][layer, at, :], first + width, 1)
                    second = first + width
                    wrap = second + width - lanes
                    mask = lane >= second
                    if wrap > 0:
                        mask = mask | (lane < wrap)
                    right = x if right is None else jnp.where(lane >= first, x, right)
                    left = x if left is None else jnp.where(mask, x, left)
            to_right[group, at, :] = right
            to_left[group, at, :] = left
    at = 0
    for f, width in enumerate(WIDTHS):
        to_core[at : at + width] = fields[f][pl.ds((layers - width) * (1 - core), width)]
        at += width


def radial(p_at, b_at, layers):
    flux, rho = [], []
    p = [[p_at(f, k) for k in range(-3, layers + 3)] for f in range(2)]
    b = [b_at(k) for k in range(-2, layers + 2)]
    for k in range(layers + 3):
        buoy = b[k] + b[k + 1]
        grads = [slope(x[k + 2], x[k + 1], x[k + 3], x[k]) for x in p]
        flux.append([buoy * g for g in grads])
        rho.append(flux[k][0] * grads[1])
    out = []
    for k in range(layers):
        laps = [slope(flux[k + 2][f], flux[k + 1][f], flux[k + 3][f], flux[k][f]) for f in range(2)]
        out.append((laps[0], laps[1], rho[k + 1] + rho[k + 2]))
    return out


def longitudinal(here, there, lane, want_there, want_rho):
    flux, rho = [], []
    for x, y in ((here, there), (there, here)):
        buoy = x[2] + lane_shift(x[2], y[2], 1, lane)
        grads = [
            slope(
                lane_shift(x[f], y[f], 1, lane),
                x[f],
                lane_shift(x[f], y[f], 2, lane),
                lane_shift(x[f], y[f], -1, lane),
            )
            for f in range(2)
        ]
        flux.append([buoy * g for g in grads])
        rho.append(flux[-1][0] * grads[1])
    laps = []
    for x, y in ((0, 1), (1, 0))[: 2 if want_there else 1]:
        laps.append(
            [
                slope(
                    flux[x][f],
                    lane_shift(flux[x][f], flux[y][f], -1, lane),
                    lane_shift(flux[x][f], flux[y][f], 1, lane),
                    lane_shift(flux[x][f], flux[y][f], -2, lane),
                )
                for f in range(2)
            ]
        )
    density = rho[0] + lane_shift(rho[0], rho[1], -1, lane) if want_rho else None
    return laps, density


def unpacked(left, right, f, s, lane):
    width, offset = WIDTHS[f], OFFSETS[f]
    first = s * SEGMENT + offset
    mask = (lane >= first) & (lane < first + width)
    return rolled(jnp.where(mask, left, right), -first - width, 1)


def lat_flux(ring, t, sub):
    adj, fwd, buoy = ring
    face = buoy[t] + row_shift(buoy, t, 1, sub)
    grads = [
        slope(row_shift(x, t, 1, sub), x[t], row_shift(x, t, 2, sub), row_shift(x, t, -1, sub))
        for x in (adj, fwd)
    ]
    flux = [face * g for g in grads]
    return flux[0], flux[1], flux[0] * grads[1]


def lat_terms(flux, t, sub, want_rho):
    adj, fwd, rho = ([x[k] for x in flux] for k in range(3))
    laps = [
        slope(x[t], row_shift(x, t, -1, sub), row_shift(x, t, 1, sub), row_shift(x, t, -2, sub))
        for x in (adj, fwd)
    ]
    return laps[0], laps[1], rho[t] + row_shift(rho, t, -1, sub) if want_rho else None


def lat_inner(ring, sub, want_rho):
    count = len(ring[0])
    flux = [list(lat_flux(ring, t, sub)) for t in range(count)]
    zero = jnp.zeros_like(ring[0][0])
    for k in range(3):
        flux[0][k] = jnp.where(sub >= 1, flux[0][k], zero)
        flux[-1][k] = jnp.where(sub < SUB - 2, flux[-1][k], zero)
    flux.append([zero] * 3)
    return [lat_terms(flux, t, sub, want_rho) for t in range(count)]


def lat_outer(adj, fwd, buoy, sub):
    ring = ([adj], [fwd], [buoy])
    mask = (sub >= SUB - 2) | (sub < 1)
    flux = [[jnp.where(mask, x, 0.0) for x in lat_flux(ring, 0, sub)]]
    return lat_terms(flux, 0, sub, True)


def places(core, layers):
    return (layers + 3) * (1 - core), (layers + 3) * core


def inner_kernel(*refs):
    fields, from_core = refs[:6], refs[6]
    wide, part, to_first, to_second = refs[7:]
    layers, rows, lanes = fields[0].shape
    tiles = rows // SUB
    sub, lane = iotas(lanes)
    core = lax.axis_index("rad")
    even = lax.axis_index("lat") % 2 == 0
    near, border = places(core, layers)
    zero = jnp.zeros((SUB, lanes), F32)

    def at(t):
        return pl.ds(t * SUB, SUB)

    for f in range(3):
        for t in range(tiles):
            for layer in range(layers):
                wide[f, layer + 6, t] = fields[f][layer, at(t), :]
            for k in range(6):
                wide[f, (layers + 6) * (1 - core) + k, t] = from_core[6 * f + k, at(t), :]
            for k in range(3):
                wide[f, border + 3 + k, t] = zero

    def send(k, low, high):
        to_first[k] = jnp.where(even, high, low)
        to_second[k] = jnp.where(even, low, high)

    ends = ((0, True), (tiles - 1, False))
    third = [None, None]
    for layer in range(layers):
        send(
            layers + layer,
            *(pack_three(*(x[layer, at(t), :] for x in fields[:3]), low, sub) for t, low in ends),
        )
        for k, row in enumerate((2, SUB - 3)):
            x = rolled(fields[5][layer, at(ends[k][0]), :], layer - row, 0)
            third[k] = x if layer == 0 else jnp.where(sub == layer, x, third[k])
    send(2 * layers, *third)
    for e in range(3):
        send(
            2 * layers + 1 + e,
            *(pack_three(*(wide[f, near + 3 + e, t] for f in range(3)), low, sub) for t, low in ends),
        )

    start = 6 - 3 * core
    for t in range(tiles):
        terms = radial(
            lambda f, k: wide[f, start + k, t], lambda k: wide[2, start + k, t], layers + 3
        )
        for k, term in enumerate(terms):
            for g in range(3):
                part[g, start - 3 + k, t] = term[g]

    def own(layer, carry):
        terms = lat_inner([[wide[f, layer + 6, t] for t in range(tiles)] for f in range(3)], sub, True)
        for t in range(tiles):
            for g in range(3):
                part[g, layer + 3, t] += terms[t][g]
        return carry

    lax.fori_loop(0, layers, own, 0, unroll=True)

    def other(e, carry):
        terms = lat_inner(
            [[wide[f, near + 3 + e, t] for t in range(tiles)] for f in range(3)], sub, False
        )
        for t in range(tiles):
            for g in range(2):
                part[g, near + e, t] += terms[t][g]
        return carry

    lax.fori_loop(0, 3, other, 0, unroll=True)


def turn_kernel(*refs):
    fields, from_left, from_right, part = refs[:6], refs[6], refs[7], refs[8]
    to_first, to_second, to_core, edges = refs[11:]
    layers, rows, lanes = fields[0].shape
    tiles = rows // SUB
    sub, lane = iotas(lanes)
    core = lax.axis_index("rad")
    even = lax.axis_index("lat") % 2 == 0
    per = lanes // SEGMENT

    def send(k, low, high):
        to_first[k] = jnp.where(even, high, low)
        to_second[k] = jnp.where(even, low, high)

    def ends(ref, *index):
        low, high = (ref[(*index, pl.ds(t * SUB, SUB), slice(None))] for t in (0, tiles - 1))
        return jnp.where(sub < 4, low, high)

    group = (from_left.shape[0] - 1) * (1 - core)
    for k, ref in enumerate((from_left, from_right)):
        to_core[k] = ref[group]
    packed = [None, None]
    for g in range(from_left.shape[0]):
        left, right = ends(from_left, g), ends(from_right, g)
        for s in range(min(per, layers - g * per)):
            layer = g * per + s
            here = [ends(x, layer) for x in fields]
            there = [unpacked(left, right, f, s, lane) for f in range(3)]
            laps, _ = longitudinal(here[:3], there, lane, False, False)
            stiff = here[5] * LAP_SCALE
            made = []
            for f in range(2):
                before = jnp.where(sub < 4, part[f, layer + 3, 0], part[f, layer + 3, tiles - 1])
                made.append(2.0 * here[f] - here[3 + f] + stiff * (before + laps[0][f]))
            send(layer, *(pack_three(*made, here[5], low, sub) for low in (True, False)))
            for k, low in enumerate((True, False)):
                x = rolled(pack_three(*there, low, sub), 16 * layer + 6, 1)
                packed[k] = x if layer == 0 else jnp.where(lane >= 16 * layer, x, packed[k])
    send(2 * layers + 4, *packed)
    for k in range(2):
        edges[k] = packed[k]


def middle_kernel(*refs):
    fields, (bulk_in, density_in) = refs[:6], refs[6:8]
    from_left, from_right, from_core, from_core2, wide, part = refs[8:14]
    first, first_halo, rest_halo, flux_out, sums, done = refs[14:20]
    halo, wide_halo, part_halo = refs[20:]
    layers, rows, lanes = fields[0].shape
    tiles = rows // SUB
    sub, lane = iotas(lanes)
    core = lax.axis_index("rad")
    near, border = places(core, layers)
    per = lanes // SEGMENT
    zero = jnp.zeros((SUB, lanes), F32)
    inside = range(1, tiles - 1)

    def at(t):
        return pl.ds(t * SUB, SUB)

    for t in range(tiles):
        for layer in range(layers):
            group, s = divmod(layer, per)
            left, right = from_left[group, at(t), :], from_right[group, at(t), :]
            for f in range(6):
                x = unpacked(left, right, f, s, lane)
                if f < 3:
                    wide_halo[f, layer + 3, t] = x
                else:
                    halo[f - 3, layer, t] = x
                if f in (2, 5):
                    rest_halo[f // 3, layer, t] = x
        left, right = from_core2[0, at(t), :], from_core2[1, at(t), :]
        for f in range(3):
            for e in range(3):
                x, y = (unpacked(left, right, f, e + skip, lane) for skip in (0, per - 3))
                wide_halo[f, near + e, t] = jnp.where(core == 0, x, y)
                wide_halo[f, border + e, t] = zero
        for g in range(2):
            for k in range(3):
                first[g, border + k, t] = zero
        terms = radial(
            lambda f, k: wide_halo[f, 3 + k, t], lambda k: wide_halo[2, 3 + k, t], layers
        )
        for k, term in enumerate(terms):
            for g in range(2):
                part_halo[g, k, t] = term[g]

    def own(layer, carry):
        here = [[wide[f, layer + 6, t] for t in range(tiles)] for f in range(3)]
        there = [[wide_halo[f, layer + 3, t] for t in range(tiles)] for f in range(3)]
        lat_halo = lat_inner(there, sub, False)
        for t in range(tiles):
            laps, rho = longitudinal([x[t] for x in here], [x[t] for x in there], lane, True, True)
            stiff = fields[5][layer, at(t), :] * LAP_SCALE
            stiff_halo = halo[2, layer, t] * LAP_SCALE
            for g in range(2):
                update = stiff * (part[g, layer + 3, t] + laps[0][g])
                first[g, layer + 3, t] = 2.0 * here[g][t] - fields[3 + g][layer, at(t), :] + update
                first_halo[g, layer, t] = (
                    2.0 * there[g][t]
                    - halo[g, layer, t]
                    + stiff_halo * (part_halo[g, layer, t] + lat_halo[t][g] + laps[1][g])
                )
            sums[0, layer, t] = bulk_in[layer, at(t), :] + here[0][t] * update
            sums[1, layer, t] = density_in[layer, at(t), :] + RHO_SCALE * (
                part[2, layer + 3, t] + rho
            )
        return carry

    lax.fori_loop(0, layers, own, 0)

    def other(e, carry):
        for t in range(tiles):
            here = [wide[f, near + 3 + e, t] for f in range(3)]
            there = [wide_halo[f, near + e, t] for f in range(3)]
            laps, _ = longitudinal(here, there, lane, False, False)
            stiff = from_core[24 + e, at(t), :] * LAP_SCALE
            for g in range(2):
                first[g, near + e, t] = (
                    2.0 * here[g]
                    - from_core[18 + 3 * g + e, at(t), :]
                    + stiff * (part[g, near + e, t] + laps[0][g])
                )
        return carry

    lax.fori_loop(0, 3, other, 0, unroll=True)

    for t in inside:
        terms = radial(lambda f, k: first[f, 3 + k, t], lambda k: wide[2, 6 + k, t], layers)
        for k, term in enumerate(terms):
            for g in range(3):
                part_halo[g, k, t] = term[g]

    def last(layer, carry):
        here = [[first[f, layer + 3, t] for t in range(tiles)] for f in range(2)]
        here.append([wide[2, layer + 6, t] for t in range(tiles)])
        flux = [lat_flux(here, t, sub) for t in range(tiles)]
        for k in range(3):
            for n, t in enumerate((1, tiles - 2)):
                flux_out[k, n, layer] = flux[t][k]
        for t in inside:
            lat = lat_terms(flux, t, sub, True)
            there = [first_halo[0, layer, t], first_halo[1, layer, t], wide_halo[2, layer + 3, t]]
            laps, rho = longitudinal([x[t] for x in here], there, lane, False, True)
            stiff = fields[5][layer, at(t), :] * LAP_SCALE
            for g in range(2):
                update = stiff * (part_halo[g, layer, t] + lat[g] + laps[0][g])
                done[2 * g, layer, at(t - 1), :] = (
                    2.0 * here[g][t] - fields[g][layer, at(t), :] + update
                )
                done[2 * g + 1, layer, at(t - 1), :] = here[g][t]
            done[4, layer, at(t - 1), :] = sums[0, layer, t] + here[0][t] * update
            done[5, layer, at(t - 1), :] = sums[1, layer, t] + RHO_SCALE * (
                part_halo[2, layer, t] + lat[2] + rho
            )
        return carry

    lax.fori_loop(0, layers, last, 0, unroll=4)


def last_kernel(*refs):
    fields, from_core = refs[:6], refs[6]
    wide, first, first_halo, rest_halo, flux_in, sums, done = refs[7:14]
    edges, from_first, from_second = refs[14:17]
    outs = refs[17:23]
    fixed, fixed_halo, ring_buoy, part, made, sems = refs[23:]
    layers, rows, lanes = fields[0].shape
    tiles = rows // SUB
    sub, lane = iotas(lanes)
    core = lax.axis_index("rad")
    place, count = lax.axis_index("lat"), lax.axis_size("lat")
    even = place % 2 == 0
    near, border = places(core, layers)
    zero = jnp.zeros((SUB, lanes), F32)
    ends = ((0, sub < 3), (tiles - 1, sub >= SUB - 3))
    copies = [
        pltpu.make_async_copy(done.at[k], out.at[:, pl.ds(SUB, rows - 2 * SUB), :], sems.at[k, 0])
        for k, out in enumerate(outs)
    ]
    for copy in copies:
        copy.start()

    def at(t):
        return pl.ds(t * SUB, SUB)

    def received(k):
        one, two = from_first[k], from_second[k]
        behind, ahead = jnp.where(even, two, one), jnp.where(even, one, two)
        return jnp.where(place > 0, behind, 0.0), jnp.where(place < count - 1, ahead, 0.0)

    def join(behind, ahead):
        return jnp.where(sub < 4, ahead, behind)

    def three(k):
        behind, ahead = received(k)
        return list(zip(unpack_three(behind, False), unpack_three(ahead, True)))

    def outer(own, halos):
        low = [jnp.where(sub < 4, x[0], h[0]) for x, h in zip(own, halos)]
        high = [jnp.where(sub < 4, h[1], x[1]) for x, h in zip(own, halos)]
        return lat_outer(*low, sub), lat_outer(*high, sub)

    for g in range(2):
        for k in range(3):
            for n in range(2):
                fixed[g, border + k, n] = zero

    halos = three(2 * layers + 4)
    mine = list(zip(unpack_three(edges[0], True), unpack_three(edges[1], False)))
    side = outer(mine, halos)
    for layer in range(layers):
        for n, (t, mask) in enumerate(ends):
            stiff = rest_halo[1, layer, t] * LAP_SCALE
            for g in range(2):
                lap = jnp.where(mask, rolled(side[n][g], -16 * layer - 6, 1), 0.0)
                fixed_halo[g, layer, n] = first_halo[g, layer, t] + stiff * lap

    for e in range(3):
        halos = three(2 * layers + 1 + e)
        mine = [(wide[f, near + 3 + e, 0], wide[f, near + 3 + e, tiles - 1]) for f in range(3)]
        side = outer(mine, halos)
        for n, (t, mask) in enumerate(ends):
            stiff = from_core[24 + e, at(t), :] * LAP_SCALE
            for g in range(2):
                lap = jnp.where(mask, side[n][g], 0.0)
                fixed[g, near + e, n] = first[g, near + e, t] + stiff * lap

    third = received(2 * layers)
    for layer in range(layers):
        halos = three(layers + layer)
        mine = [(x[layer, at(0), :], x[layer, at(tiles - 1), :]) for x in fields[:3]]
        side = outer(mine, halos)
        for n, (t, mask) in enumerate(ends):
            stiff = fields[5][layer, at(t), :] * LAP_SCALE
            for g in range(2):
                update = stiff * jnp.where(mask, side[n][g], 0.0)
                fixed[g, layer + 3, n] = first[g, layer + 3, t] + update
            made[4, layer, n] = sums[0, layer, t] + mine[0][n] * update
            made[5, layer, n] = sums[1, layer, t] + RHO_SCALE * jnp.where(mask, side[n][2], 0.0)
        adj, fwd, stiff = three(layer)
        low, high = (rolled(third[k], row - layer, 0) for k, row in enumerate((SUB - 3, 2)))
        stiff = jnp.where(
            sub < 4,
            jnp.where(sub == 2, high, stiff[1]),
            jnp.where(sub == SUB - 3, low, stiff[0]),
        )
        for g, x in enumerate((adj, fwd)):
            lap = join(side[0][g], side[1][g])
            fixed[g, layer + 3, 2] = join(*x) + stiff * LAP_SCALE * lap
        ring_buoy[layer] = join(*halos[2])

    for n, (t, _) in enumerate(ends):
        terms = radial(lambda f, k: fixed[f, 3 + k, n], lambda k: wide[2, 6 + k, t], layers)
        for k, term in enumerate(terms):
            for g in range(3):
                part[g, k, n] = term[g]

    def last(layer, carry):
        buoys = [wide[2, layer + 6, t] for t in (0, 1, tiles - 2, tiles - 1)]
        rings = [
            [fixed[f, layer + 3, 2], fixed[f, layer + 3, 0], first[f, layer + 3, 1]]
            + [first[f, layer + 3, tiles - 2], fixed[f, layer + 3, 1]]
            for f in range(2)
        ] + [[ring_buoy[layer], *buoys]]
        flux = [None] * 5
        for t in (0, 1, 4):
            flux[t] = lat_flux(rings, t, sub)
        for n in range(2):
            flux[2 + n] = [flux_in[k, n, layer] for k in range(3)]
        for n, (t, _) in enumerate(ends):
            k = (1, 4)[n]
            here = [x[k] for x in rings]
            lat = lat_terms(flux, k, sub, True)
            there = [fixed_halo[0, layer, n], fixed_halo[1, layer, n], rest_halo[0, layer, t]]
            laps, rho = longitudinal(here, there, lane, False, True)
            stiff = fields[5][layer, at(t), :] * LAP_SCALE
            for g in range(2):
                update = stiff * (part[g, layer, n] + lat[g] + laps[0][g])
                made[2 * g, layer, n] = 2.0 * here[g] - fields[g][layer, at(t), :] + update
                made[2 * g + 1, layer, n] = here[g]
            made[4, layer, n] += here[0] * update
            made[5, layer, n] += RHO_SCALE * (part[2, layer, n] + lat[2] + rho)
        return carry

    lax.fori_loop(0, layers, last, 0, unroll=True)
    for k, out in enumerate(outs):
        for n, (t, _) in enumerate(ends):
            copy = pltpu.make_async_copy(made.at[k, :, n], out.at[:, at(t), :], sems.at[k, 1 + n])
            copy.start()
            copies.append(copy)
    for copy in copies:
        copy.wait()


def pairs(count, start):
    partner = {i: i for i in range(count)}
    for i in range(start, count - 1, 2):
        partner[i], partner[i + 1] = i + 1, i
    return [
        (2 * i + core, 2 * j + (core if i != j else 1 - core))
        for i, j in partner.items()
        for core in range(2)
    ]


def call(kernel, out_shape, args, in_specs=None, out_specs=None, **more):
    return pl.pallas_call(
        kernel,
        out_shape=out_shape,
        in_specs=in_specs or [VMEM] * len(args),
        out_specs=out_specs or (VMEM,) * len(out_shape),
        compiler_params=PARAMS,
        **more,
    )(*args)


def shards(
    adj_now, adj_next, fwd_now, fwd_next, stiffness, buoyancy, kernel_bulk_in, kernel_density_in
):
    layers, rows, lanes = adj_now.shape
    tiles = rows // SUB
    fields = (adj_now, fwd_now, buoyancy, adj_next, fwd_next, stiffness)
    groups = -(-layers // (lanes // SEGMENT))
    around, count = lax.axis_size("lon"), lax.axis_size("lat")
    ring = [(i, (i + 1) % around) for i in range(around)]
    swap = [(0, 1), (1, 0)]

    def made(*shape):
        return pltpu.VMEM(shape, F32)

    block = (layers, rows, lanes)
    edge = made(groups, rows, lanes)
    hbm = pl.BlockSpec(memory_space=pltpu.HBM)
    *fields, to_right, to_left, to_core = call(
        edges_kernel,
        (made(*block),) * 6 + (edge, edge, made(sum(WIDTHS), rows, lanes)),
        [pltpu.with_memory_space_constraint(x, pltpu.HBM) for x in fields],
        in_specs=[hbm] * 6,
        scratch_shapes=[pltpu.SemaphoreType.DMA((6,))],
    )
    from_left = lax.ppermute(to_right, "lon", ring)
    from_right = lax.ppermute(to_left, "lon", [(b, a) for a, b in ring])
    from_core = lax.ppermute(to_core, "rad", swap)
    lat_edge = made(2 * layers + 5, SUB, lanes)
    wide, part, to_first, to_second = call(
        inner_kernel,
        (
            made(3, layers + 12, tiles, SUB, lanes),
            made(3, layers + 6, tiles, SUB, lanes),
            lat_edge,
            lat_edge,
        ),
        [*fields, from_core],
    )
    to_first, to_second, to_core, edges = call(
        turn_kernel,
        (lat_edge, lat_edge, made(2, rows, lanes), made(2, SUB, lanes)),
        [*fields, from_left, from_right, part, to_first, to_second],
        input_output_aliases={9: 0, 10: 1},
    )
    from_first = lax.ppermute(to_first, ("lat", "rad"), pairs(count, 0))
    from_second = lax.ppermute(to_second, ("lat", "rad"), pairs(count, 1))
    from_core2 = lax.ppermute(to_core, "rad", swap)
    first, first_halo, rest_halo, flux, sums, done = call(
        middle_kernel,
        (
            made(2, layers + 6, tiles, SUB, lanes),
            made(2, layers, tiles, SUB, lanes),
            made(2, layers, tiles, SUB, lanes),
            made(3, 2, layers, SUB, lanes),
            made(2, layers, tiles, SUB, lanes),
            made(6, layers, rows - 2 * SUB, lanes),
        ),
        [
            *fields,
            kernel_bulk_in,
            kernel_density_in,
            from_left,
            from_right,
            from_core,
            from_core2,
            wide,
            part,
        ],
        cost_estimate=HEAVY,
        scratch_shapes=[
            made(3, layers, tiles, SUB, lanes),
            made(3, layers + 6, tiles, SUB, lanes),
            made(3, layers, tiles, SUB, lanes),
        ],
    )
    return call(
        last_kernel,
        (jax.ShapeDtypeStruct(block, F32),) * 6,
        [
            *fields,
            from_core,
            wide,
            first,
            first_halo,
            rest_halo,
            flux,
            sums,
            done,
            edges,
            from_first,
            from_second,
        ],
        out_specs=(hbm,) * 6,
        scratch_shapes=[
            made(2, layers + 6, 3, SUB, lanes),
            made(2, layers, 2, SUB, lanes),
            made(layers, SUB, lanes),
            made(3, layers, 2, SUB, lanes),
            made(6, layers, 2, SUB, lanes),
            pltpu.SemaphoreType.DMA((6, 3)),
        ],
    )


def solution(mesh):
    spec = P("rad", "lat", "lon")
    return jax.shard_map(
        shards, mesh=mesh, in_specs=(spec,) * 8, out_specs=(spec,) * 6, check_vma=False
    )
```

```python
import jax
import jax.numpy as jnp
from jax import lax
from jax.experimental import pallas as pl
from jax.experimental.pallas import tpu as pltpu
from jax.sharding import PartitionSpec as P

F32 = jnp.float32
SUB = 8
LAP_SCALE = 1.0 / 1152.0
RHO_SCALE = 1.0 / 2304.0
WIDTHS = (6, 6, 6, 3, 3, 3)
OFFSETS = (0, 6, 12, 21, 24, 27)
SEGMENT = 32
VMEM = pl.BlockSpec(memory_space=pltpu.VMEM)
PARAMS = pltpu.CompilerParams(vmem_limit_bytes=24 * 1024 * 1024)
HEAVY = pl.CostEstimate(flops=4000000000, bytes_accessed=1000000, transcendentals=0)


def iotas(lanes):
    return (
        lax.broadcasted_iota(jnp.int32, (SUB, lanes), 0),
        lax.broadcasted_iota(jnp.int32, (SUB, lanes), 1),
    )


def rolled(x, shift, axis):
    size = x.shape[axis]
    shift = shift % size
    return x if shift == 0 else pltpu.roll(x, shift, axis)


def lane_shift(here, there, by, lane):
    size = here.shape[1]
    if by > 0:
        return rolled(jnp.where(lane < by, there, here), size - by, 1)
    return rolled(jnp.where(lane >= size + by, there, here), -by, 1)


def row_shift(tiles, t, by, sub):
    if by > 0:
        return rolled(jnp.where(sub < by, tiles[(t + 1) % len(tiles)], tiles[t]), SUB - by, 0)
    return rolled(jnp.where(sub >= SUB + by, tiles[t - 1], tiles[t]), -by, 0)


def slope(ahead, here, ahead2, behind):
    return 27.0 * (ahead - here) - (ahead2 - behind)


def pack_three(a, b, c, low, sub):
    if low:
        return jnp.where(sub < 3, a, jnp.where(sub < 6, rolled(b, 3, 0), rolled(c, 6, 0)))
    return jnp.where(sub >= 5, a, jnp.where(sub >= 2, rolled(b, -3, 0), rolled(c, -6, 0)))


def unpack_three(x, low):
    sign = -1 if low else 1
    return x, rolled(x, 3 * sign, 0), rolled(x, 6 * sign, 0)


def edges_kernel(*refs):
    sources, fields, (to_right, to_left, to_core), sems = refs[:6], refs[6:12], refs[12:15], refs[15]
    copies = [pltpu.make_async_copy(x, y, sems.at[k]) for k, (x, y) in enumerate(zip(sources, fields))]
    for copy in copies:
        copy.start()
    layers, rows, lanes = fields[0].shape
    _, lane = iotas(lanes)
    core = lax.axis_index("rad")
    per = lanes // SEGMENT
    row = 0
    packed = {}
    for f, (width, offset) in enumerate(zip(WIDTHS, OFFSETS)):
        copies[f].wait()
        for layer in range(layers):
            group, s = divmod(layer, per)
            first = s * SEGMENT + offset
            second = first + width
            mask = lane >= second
            if second + width > lanes:
                mask = mask | (lane < second + width - lanes)
            mine = (lane >= first) & (lane < second)
            theirs = mask & (lane < second + width) if second + width <= lanes else mask
            for t in range(rows // SUB):
                x = rolled(fields[f][layer, pl.ds(t * SUB, SUB), :], second, 1)
                right, left = packed.get((group, t), (x, x))
                packed[group, t] = jnp.where(mine, x, right), jnp.where(theirs, x, left)
        to_core[row : row + width] = fields[f][pl.ds((layers - width) * (1 - core), width)]
        row += width
    for (group, t), (right, left) in packed.items():
        to_right[group, pl.ds(t * SUB, SUB), :] = right
        to_left[group, pl.ds(t * SUB, SUB), :] = left


def radial(p_at, b_at, layers):
    flux, rho = [], []
    p = [[p_at(f, k) for k in range(-3, layers + 3)] for f in range(2)]
    b = [b_at(k) for k in range(-2, layers + 2)]
    for k in range(layers + 3):
        buoy = b[k] + b[k + 1]
        grads = [slope(x[k + 2], x[k + 1], x[k + 3], x[k]) for x in p]
        flux.append([buoy * g for g in grads])
        rho.append(flux[k][0] * grads[1])
    out = []
    for k in range(layers):
        laps = [slope(flux[k + 2][f], flux[k + 1][f], flux[k + 3][f], flux[k][f]) for f in range(2)]
        out.append((laps[0], laps[1], rho[k + 1] + rho[k + 2]))
    return out


def longitudinal(here, there, lane, want_there, want_rho):
    flux, rho = [], []
    for x, y in ((here, there), (there, here)):
        buoy = x[2] + lane_shift(x[2], y[2], 1, lane)
        grads = [
            slope(
                lane_shift(x[f], y[f], 1, lane),
                x[f],
                lane_shift(x[f], y[f], 2, lane),
                lane_shift(x[f], y[f], -1, lane),
            )
            for f in range(2)
        ]
        flux.append([buoy * g for g in grads])
        rho.append(flux[-1][0] * grads[1])
    laps = []
    for x, y in ((0, 1), (1, 0))[: 2 if want_there else 1]:
        laps.append(
            [
                slope(
                    flux[x][f],
                    lane_shift(flux[x][f], flux[y][f], -1, lane),
                    lane_shift(flux[x][f], flux[y][f], 1, lane),
                    lane_shift(flux[x][f], flux[y][f], -2, lane),
                )
                for f in range(2)
            ]
        )
    density = rho[0] + lane_shift(rho[0], rho[1], -1, lane) if want_rho else None
    return laps, density


def windows(from_left, from_right, to_left, to_right, f, seg):
    offset = OFFSETS[f]
    mask = (seg >= offset) & (seg < offset + WIDTHS[f])
    return (
        rolled(jnp.where(mask, from_left, to_left), -offset, 1),
        rolled(jnp.where(mask, to_right, from_right), -offset, 1),
    )


def lon_flux(adj, fwd, buoy):
    face = buoy + rolled(buoy, -1, 1)
    grads = [slope(rolled(x, -1, 1), x, rolled(x, -2, 1), rolled(x, 1, 1)) for x in (adj, fwd)]
    flux = [face * g for g in grads]
    return flux[0], flux[1], flux[0] * grads[1]


def lon_terms(adj, fwd, buoy, want_rho):
    flux = lon_flux(adj, fwd, buoy)
    terms = [slope(x, rolled(x, 1, 1), rolled(x, -1, 1), rolled(x, 2, 1)) for x in flux[:2]]
    return terms + [flux[2] + rolled(flux[2], 1, 1)] if want_rho else terms


def edge_terms(wins, seg, want_rho):
    left = lon_terms(*(x[0] for x in wins), want_rho)
    right = lon_terms(*(x[1] for x in wins), want_rho)
    valid = (seg >= 3) & (seg < 9)
    own = [jnp.where(valid, jnp.where(seg < 6, y, x), 0.0) for x, y in zip(left, right)]
    return own, [jnp.where(seg < 6, x, y) for x, y in zip(left[:2], right[:2])]


def halos_of(wins, seg):
    return [jnp.where(seg < 6, x, y) for x, y in wins]


def spread(x, s):
    return rolled(x, -s * SEGMENT - 6, 1)


def at_ends(x, s, lane):
    return jnp.where((lane < 3) | (lane >= x.shape[1] - 3), spread(x, s), 0.0)


def merged(tiles, seg):
    half = SEGMENT // 2
    out = []
    for k in range(0, len(tiles), 2):
        x = tiles[k]
        if k + 1 < len(tiles):
            x = jnp.where(seg < half, x, rolled(tiles[k + 1], half, 1))
        out.append(x)
    return out


def unmerged(x, group):
    return rolled(x, -(SEGMENT // 2) * (group % 2), 1)


def packed_radial(groups, lane):
    size = lane.shape[1]

    def shift(x, i, by):
        step = by * SEGMENT
        if by > 0:
            return rolled(jnp.where(lane < step, x[min(i + 1, len(x) - 1)], x[i]), -step, 1)
        return rolled(jnp.where(lane >= size + step, x[max(i - 1, 0)], x[i]), -step, 1)

    adj, fwd, buoy = ([x[f] for x in groups] for f in range(3))
    flux = ([], [])
    for i in range(len(groups)):
        face = buoy[i] + shift(buoy, i, 1)
        for f, x in enumerate((adj, fwd)):
            flux[f].append(face * slope(shift(x, i, 1), x[i], shift(x, i, 2), shift(x, i, -1)))
    return [
        [slope(x[i], shift(x, i, -1), shift(x, i, 1), shift(x, i, -2)) for x in flux]
        for i in range(1, len(groups) - 1)
    ]


def lat_flux(ring, t, sub):
    adj, fwd, buoy = ring
    face = buoy[t] + row_shift(buoy, t, 1, sub)
    grads = [
        slope(row_shift(x, t, 1, sub), x[t], row_shift(x, t, 2, sub), row_shift(x, t, -1, sub))
        for x in (adj, fwd)
    ]
    flux = [face * g for g in grads]
    return flux[0], flux[1], flux[0] * grads[1]


def lat_terms(flux, t, sub, want_rho):
    adj, fwd, rho = ([x[k] for x in flux] for k in range(3))
    laps = [
        slope(x[t], row_shift(x, t, -1, sub), row_shift(x, t, 1, sub), row_shift(x, t, -2, sub))
        for x in (adj, fwd)
    ]
    return laps[0], laps[1], rho[t] + row_shift(rho, t, -1, sub) if want_rho else None


def lat_inner(ring, sub, want_rho):
    count = len(ring[0])
    flux = [list(lat_flux(ring, t, sub)) for t in range(count)]
    zero = jnp.zeros_like(ring[0][0])
    for k in range(3):
        flux[0][k] = jnp.where(sub >= 1, flux[0][k], zero)
        flux[-1][k] = jnp.where(sub < SUB - 2, flux[-1][k], zero)
    flux.append([zero] * 3)
    return [lat_terms(flux, t, sub, want_rho) for t in range(count)]


def lat_outer(adj, fwd, buoy, sub):
    ring = ([adj], [fwd], [buoy])
    mask = (sub >= SUB - 2) | (sub < 1)
    flux = [[jnp.where(mask, x, 0.0) for x in lat_flux(ring, 0, sub)]]
    return lat_terms(flux, 0, sub, True)


def places(core, layers):
    return (layers + 3) * (1 - core), (layers + 3) * core


def inner_kernel(*refs):
    fields, from_core = refs[:6], refs[6]
    wide, part, to_first, to_second = refs[7:]
    layers, rows, lanes = fields[0].shape
    tiles = rows // SUB
    sub, lane = iotas(lanes)
    core = lax.axis_index("rad")
    even = lax.axis_index("lat") % 2 == 0
    near, border = places(core, layers)
    zero = jnp.zeros((SUB, lanes), F32)
    away = (lane >= 3) & (lane < lanes - 3)

    def at(t):
        return pl.ds(t * SUB, SUB)

    for f in range(3):
        for t in range(tiles):
            for layer in range(layers):
                wide[f, layer + 6, t] = fields[f][layer, at(t), :]
            for k in range(6):
                wide[f, (layers + 6) * (1 - core) + k, t] = from_core[6 * f + k, at(t), :]
            for k in range(3):
                wide[f, border + 3 + k, t] = zero

    def send(k, low, high):
        to_first[k] = jnp.where(even, high, low)
        to_second[k] = jnp.where(even, low, high)

    ends = ((0, True), (tiles - 1, False))
    third = [None, None]
    for layer in range(layers):
        send(
            layers + layer,
            *(pack_three(*(x[layer, at(t), :] for x in fields[:3]), low, sub) for t, low in ends),
        )
        for k, row in enumerate((2, SUB - 3)):
            x = rolled(fields[5][layer, at(ends[k][0]), :], layer - row, 0)
            third[k] = x if layer == 0 else jnp.where(sub == layer, x, third[k])
    send(2 * layers, *third)
    for e in range(3):
        send(
            2 * layers + 1 + e,
            *(pack_three(*(wide[f, near + 3 + e, t] for f in range(3)), low, sub) for t, low in ends),
        )

    start = 6 - 3 * core
    for t in range(tiles):
        terms = radial(
            lambda f, k: wide[f, start + k, t], lambda k: wide[2, start + k, t], layers + 3
        )
        for k, term in enumerate(terms):
            for g in range(3):
                part[g, start - 3 + k, t] = term[g]

    def own(layer, carry):
        here = [[wide[f, layer + 6, t] for t in range(tiles)] for f in range(3)]
        terms = lat_inner(here, sub, True)
        for t in range(tiles):
            lon = lon_terms(*(x[t] for x in here), True)
            for g in range(3):
                part[g, layer + 3, t] += terms[t][g] + jnp.where(away, lon[g], 0.0)
        return carry

    lax.fori_loop(0, layers, own, 0, unroll=2)

    def other(e, carry):
        here = [[wide[f, near + 3 + e, t] for t in range(tiles)] for f in range(3)]
        terms = lat_inner(here, sub, False)
        for t in range(tiles):
            lon = lon_terms(*(x[t] for x in here), False)
            for g in range(2):
                part[g, near + e, t] += terms[t][g] + jnp.where(away, lon[g], 0.0)
        return carry

    lax.fori_loop(0, 3, other, 0, unroll=True)


def turn_kernel(*refs):
    fields, packs, part = refs[:6], refs[6:10], refs[10]
    to_first, to_second, to_core, edges = refs[13:]
    layers, rows, lanes = fields[0].shape
    tiles = rows // SUB
    sub, lane = iotas(lanes)
    seg = lane % SEGMENT
    core = lax.axis_index("rad")
    even = lax.axis_index("lat") % 2 == 0
    per = lanes // SEGMENT
    groups = packs[0].shape[0]

    def send(k, low, high):
        to_first[k] = jnp.where(even, high, low)
        to_second[k] = jnp.where(even, low, high)

    def ends(ref, *index):
        low, high = (ref[(*index, pl.ds(t * SUB, SUB), slice(None))] for t in (0, tiles - 1))
        return jnp.where(sub < 4, low, high)

    for k, ref in enumerate(packs):
        to_core[k] = ref[(groups - 1) * (1 - core)]
    halos = []
    for g in range(groups):
        pack = [ends(x, g) for x in packs]
        wins = [windows(*pack, f, seg) for f in range(3)]
        laps, _ = edge_terms(wins, seg, False)
        halos.append(halos_of(wins, seg))
        for s in range(min(per, layers - g * per)):
            layer = g * per + s
            here = [ends(x, layer) for x in fields]
            stiff = here[5] * LAP_SCALE
            made = []
            for f in range(2):
                before = jnp.where(sub < 4, part[f, layer + 3, 0], part[f, layer + 3, tiles - 1])
                lap = before + at_ends(laps[f], s, lane)
                made.append(2.0 * here[f] - here[3 + f] + stiff * lap)
            send(layer, *(pack_three(*made, here[5], low, sub) for low in (True, False)))
    both = [merged([pack_three(*x, low, sub) for x in halos], seg) for low in (True, False)]
    for k, (low, high) in enumerate(zip(*both)):
        send(2 * layers + 4 + k, low, high)
        edges[0, k] = low
        edges[1, k] = high


def middle_kernel(*refs):
    fields, (bulk_in, density_in) = refs[:6], refs[6:8]
    packs, from_core, from_core2, wide, part = refs[8:12], refs[12], refs[13], refs[14], refs[15]
    first, first_pack, stiff_pack, buoy_halo, flux_out, sums, done = refs[16:23]
    first_halo, own_pack, part_last, halo_pack, lap_pack = refs[23:]
    layers, rows, lanes = fields[0].shape
    tiles = rows // SUB
    sub, lane = iotas(lanes)
    seg = lane % SEGMENT
    core = lax.axis_index("rad")
    near, border = places(core, layers)
    per = lanes // SEGMENT
    groups = packs[0].shape[0]
    zero = jnp.zeros((SUB, lanes), F32)
    inside = range(1, tiles - 1)

    def at(t):
        return pl.ds(pl.multiple_of(t * SUB, SUB), SUB)

    def edges_at(t, carry):
        sources = [[x[group, at(t), :] for x in packs] for group in range(groups)]
        sources.append([from_core2[k, at(t), :] for k in range(4)])
        wins = [[windows(*x, f, seg) for f in range(3)] for x in sources]
        halos = [halos_of(x, seg) for x in wins]
        before = [jnp.where(core == 0, 0.0, x) for x in halos[-1]]
        after = [jnp.where(core == 0, x, 0.0) for x in halos[-1]]
        radials = packed_radial([before, *halos[:-1], after], lane)
        terms = [edge_terms(x, seg, k < groups) for k, x in enumerate(wins)]
        own = [x for x, _ in terms]
        own[groups] = [
            jnp.where(core == 0, x, rolled(x, -(per - 3) * SEGMENT, 1)) for x in own[groups]
        ]
        for group in range(groups):
            for f in range(3):
                halo_pack[f, group, t] = halos[group][f]
            for g in range(2):
                lap_pack[g, group, t] = terms[group][1][g] + radials[group][g]
        for group in range(groups + 1):
            for g, x in enumerate(own[group]):
                own_pack[g, group, t] = x
        return carry

    lax.fori_loop(0, tiles, edges_at, 0)
    for group in range(groups):
        halo = [[halo_pack[f, group, t] for t in range(tiles)] for f in range(3)]
        lat = lat_inner(halo, sub, False)
        for t in range(tiles):
            rest = []
            for f in range(3, 6):
                offset = OFFSETS[f]
                mask = (seg >= offset) & (seg < offset + WIDTHS[f])
                x = jnp.where(mask, packs[0][group, at(t), :], packs[1][group, at(t), :])
                rest.append(rolled(x, 3 - offset, 1))
            stiff = rest[2] * LAP_SCALE
            stiff_pack[group, t] = stiff
            for g in range(2):
                lap = lap_pack[g, group, t] + lat[t][g]
                first_pack[g, group, t] = 2.0 * halo[g][t] - rest[g] + stiff * lap
    for g in range(2):
        for k in range(3):
            for t in range(tiles):
                first[g, border + k, t] = zero

    def first_at(t, carry):
        for layer in range(layers):
            group, s = divmod(layer, per)
            buoy_halo[layer, t] = spread(halo_pack[2, group, t], s)
            stiff = fields[5][layer, at(t), :] * LAP_SCALE
            here = [wide[f, layer + 6, t] for f in range(2)]
            for g in range(2):
                first_halo[g, layer, t] = spread(first_pack[g, group, t], s)
                lap = part[g, layer + 3, t] + at_ends(own_pack[g, group, t], s, lane)
                update = stiff * lap
                first[g, layer + 3, t] = 2.0 * here[g] - fields[3 + g][layer, at(t), :] + update
            sums[0, layer, t] = bulk_in[layer, at(t), :] + here[0] * update
            rho = part[2, layer + 3, t] + at_ends(own_pack[2, group, t], s, lane)
            sums[1, layer, t] = density_in[layer, at(t), :] + RHO_SCALE * rho
        for e in range(3):
            stiff = from_core[24 + e, at(t), :] * LAP_SCALE
            for g in range(2):
                lap = part[g, near + e, t] + at_ends(own_pack[g, groups, t], e, lane)
                past = from_core[18 + 3 * g + e, at(t), :]
                first[g, near + e, t] = 2.0 * wide[g, near + 3 + e, t] - past + stiff * lap
        return carry

    lax.fori_loop(0, tiles, first_at, 0)

    for t in inside:
        terms = radial(lambda f, k: first[f, 3 + k, t], lambda k: wide[2, 6 + k, t], layers)
        for k, term in enumerate(terms):
            for g in range(3):
                part_last[g, k, t - 1] = term[g]

    def last(layer, carry):
        here = [[first[f, layer + 3, t] for t in range(tiles)] for f in range(2)]
        here.append([wide[2, layer + 6, t] for t in range(tiles)])
        flux = [lat_flux(here, t, sub) for t in range(tiles)]
        for k in range(3):
            for n, t in enumerate((1, tiles - 2)):
                flux_out[k, n, layer] = flux[t][k]
        for t in inside:
            lat = lat_terms(flux, t, sub, True)
            there = [first_halo[0, layer, t], first_halo[1, layer, t], buoy_halo[layer, t]]
            laps, rho = longitudinal([x[t] for x in here], there, lane, False, True)
            stiff = fields[5][layer, at(t), :] * LAP_SCALE
            for g in range(2):
                update = stiff * (part_last[g, layer, t - 1] + lat[g] + laps[0][g])
                done[2 * g, layer, at(t - 1), :] = (
                    2.0 * here[g][t] - fields[g][layer, at(t), :] + update
                )
                done[2 * g + 1, layer, at(t - 1), :] = here[g][t]
            done[4, layer, at(t - 1), :] = sums[0, layer, t] + here[0][t] * update
            done[5, layer, at(t - 1), :] = sums[1, layer, t] + RHO_SCALE * (
                part_last[2, layer, t - 1] + lat[2] + rho
            )
        return carry

    lax.fori_loop(0, layers, last, 0, unroll=4)


def last_kernel(*refs):
    fields, from_core = refs[:6], refs[6]
    wide, first, first_pack, stiff_pack, buoy_halo, flux_in, sums, done = refs[7:15]
    edges, from_first, from_second = refs[15:18]
    outs = refs[18:24]
    fixed, fixed_halo, ring_buoy, part, made, sems = refs[24:]
    layers, rows, lanes = fields[0].shape
    tiles = rows // SUB
    sub, lane = iotas(lanes)
    core = lax.axis_index("rad")
    place, count = lax.axis_index("lat"), lax.axis_size("lat")
    even = place % 2 == 0
    near, border = places(core, layers)
    zero = jnp.zeros((SUB, lanes), F32)
    ends = ((0, sub < 3), (tiles - 1, sub >= SUB - 3))
    copies = [
        pltpu.make_async_copy(done.at[k], out.at[:, pl.ds(SUB, rows - 2 * SUB), :], sems.at[k, 0])
        for k, out in enumerate(outs)
    ]
    for copy in copies:
        copy.start()

    def at(t):
        return pl.ds(t * SUB, SUB)

    def received(k):
        one, two = from_first[k], from_second[k]
        behind, ahead = jnp.where(even, two, one), jnp.where(even, one, two)
        return jnp.where(place > 0, behind, 0.0), jnp.where(place < count - 1, ahead, 0.0)

    def join(behind, ahead):
        return jnp.where(sub < 4, ahead, behind)

    def three(k):
        behind, ahead = received(k)
        return list(zip(unpack_three(behind, False), unpack_three(ahead, True)))

    def outer(own, halos):
        low = [jnp.where(sub < 4, x[0], h[0]) for x, h in zip(own, halos)]
        high = [jnp.where(sub < 4, h[1], x[1]) for x, h in zip(own, halos)]
        return lat_outer(*low, sub), lat_outer(*high, sub)

    for g in range(2):
        for k in range(3):
            for n in range(2):
                fixed[g, border + k, n] = zero

    per = lanes // SEGMENT
    for group in range(stiff_pack.shape[0]):
        if group % 2 == 0:
            k = group // 2
            mine = list(zip(unpack_three(edges[0, k], True), unpack_three(edges[1, k], False)))
            side = outer(mine, three(2 * layers + 4 + k))
        for n, (t, mask) in enumerate(ends):
            for g in range(2):
                lap = jnp.where(mask, unmerged(side[n][g], group), 0.0)
                x = first_pack[g, group, t] + stiff_pack[group, t] * lap
                for s in range(min(per, layers - group * per)):
                    fixed_halo[g, group * per + s, n] = spread(x, s)

    for e in range(3):
        halos = three(2 * layers + 1 + e)
        mine = [(wide[f, near + 3 + e, 0], wide[f, near + 3 + e, tiles - 1]) for f in range(3)]
        side = outer(mine, halos)
        for n, (t, mask) in enumerate(ends):
            stiff = from_core[24 + e, at(t), :] * LAP_SCALE
            for g in range(2):
                lap = jnp.where(mask, side[n][g], 0.0)
                fixed[g, near + e, n] = first[g, near + e, t] + stiff * lap

    third = received(2 * layers)
    for layer in range(layers):
        halos = three(layers + layer)
        mine = [(x[layer, at(0), :], x[layer, at(tiles - 1), :]) for x in fields[:3]]
        side = outer(mine, halos)
        for n, (t, mask) in enumerate(ends):
            stiff = fields[5][layer, at(t), :] * LAP_SCALE
            for g in range(2):
                update = stiff * jnp.where(mask, side[n][g], 0.0)
                fixed[g, layer + 3, n] = first[g, layer + 3, t] + update
            made[4, layer, n] = sums[0, layer, t] + mine[0][n] * update
            made[5, layer, n] = sums[1, layer, t] + RHO_SCALE * jnp.where(mask, side[n][2], 0.0)
        adj, fwd, stiff = three(layer)
        low, high = (rolled(third[k], row - layer, 0) for k, row in enumerate((SUB - 3, 2)))
        stiff = jnp.where(
            sub < 4,
            jnp.where(sub == 2, high, stiff[1]),
            jnp.where(sub == SUB - 3, low, stiff[0]),
        )
        for g, x in enumerate((adj, fwd)):
            lap = join(side[0][g], side[1][g])
            fixed[g, layer + 3, 2] = join(*x) + stiff * LAP_SCALE * lap
        ring_buoy[layer] = join(*halos[2])

    for n, (t, _) in enumerate(ends):
        terms = radial(lambda f, k: fixed[f, 3 + k, n], lambda k: wide[2, 6 + k, t], layers)
        for k, term in enumerate(terms):
            for g in range(3):
                part[g, k, n] = term[g]

    def last(layer, carry):
        buoys = [wide[2, layer + 6, t] for t in (0, 1, tiles - 2, tiles - 1)]
        rings = [
            [fixed[f, layer + 3, 2], fixed[f, layer + 3, 0], first[f, layer + 3, 1]]
            + [first[f, layer + 3, tiles - 2], fixed[f, layer + 3, 1]]
            for f in range(2)
        ] + [[ring_buoy[layer], *buoys]]
        flux = [None] * 5
        for t in (0, 1, 4):
            flux[t] = lat_flux(rings, t, sub)
        for n in range(2):
            flux[2 + n] = [flux_in[k, n, layer] for k in range(3)]
        for n, (t, _) in enumerate(ends):
            k = (1, 4)[n]
            here = [x[k] for x in rings]
            lat = lat_terms(flux, k, sub, True)
            there = [fixed_halo[0, layer, n], fixed_halo[1, layer, n], buoy_halo[layer, t]]
            laps, rho = longitudinal(here, there, lane, False, True)
            stiff = fields[5][layer, at(t), :] * LAP_SCALE
            for g in range(2):
                update = stiff * (part[g, layer, n] + lat[g] + laps[0][g])
                made[2 * g, layer, n] = 2.0 * here[g] - fields[g][layer, at(t), :] + update
                made[2 * g + 1, layer, n] = here[g]
            made[4, layer, n] += here[0] * update
            made[5, layer, n] += RHO_SCALE * (part[2, layer, n] + lat[2] + rho)
        return carry

    lax.fori_loop(0, layers, last, 0, unroll=True)
    for k, out in enumerate(outs):
        for n, (t, _) in enumerate(ends):
            copy = pltpu.make_async_copy(made.at[k, :, n], out.at[:, at(t), :], sems.at[k, 1 + n])
            copy.start()
            copies.append(copy)
    for copy in copies:
        copy.wait()


def pairs(count, start):
    partner = {i: i for i in range(count)}
    for i in range(start, count - 1, 2):
        partner[i], partner[i + 1] = i + 1, i
    return [
        (2 * i + core, 2 * j + (core if i != j else 1 - core))
        for i, j in partner.items()
        for core in range(2)
    ]


def call(kernel, out_shape, args, in_specs=None, out_specs=None, **more):
    return pl.pallas_call(
        kernel,
        out_shape=out_shape,
        in_specs=in_specs or [VMEM] * len(args),
        out_specs=out_specs or (VMEM,) * len(out_shape),
        compiler_params=PARAMS,
        **more,
    )(*args)


def shards(
    adj_now, adj_next, fwd_now, fwd_next, stiffness, buoyancy, kernel_bulk_in, kernel_density_in
):
    layers, rows, lanes = adj_now.shape
    tiles = rows // SUB
    fields = (adj_now, fwd_now, buoyancy, adj_next, fwd_next, stiffness)
    groups = -(-layers // (lanes // SEGMENT))
    around, count = lax.axis_size("lon"), lax.axis_size("lat")
    ring = [(i, (i + 1) % around) for i in range(around)]
    swap = [(0, 1), (1, 0)]

    def made(*shape):
        return pltpu.VMEM(shape, F32)

    block = (layers, rows, lanes)
    edge = made(groups, rows, lanes)
    hbm = pl.BlockSpec(memory_space=pltpu.HBM)
    *fields, to_right, to_left, to_core = call(
        edges_kernel,
        (made(*block),) * 6 + (edge, edge, made(sum(WIDTHS), rows, lanes)),
        [pltpu.with_memory_space_constraint(x, pltpu.HBM) for x in fields],
        in_specs=[hbm] * 6,
        scratch_shapes=[pltpu.SemaphoreType.DMA((6,))],
    )
    from_left = lax.ppermute(to_right, "lon", ring)
    from_right = lax.ppermute(to_left, "lon", [(b, a) for a, b in ring])
    from_core = lax.ppermute(to_core, "rad", swap)
    pairs_of_groups = -(-groups // 2)
    lat_edge = made(2 * layers + 4 + pairs_of_groups, SUB, lanes)
    packs = [from_left, from_right, to_left, to_right]
    wide, part, to_first, to_second = call(
        inner_kernel,
        (
            made(3, layers + 12, tiles, SUB, lanes),
            made(3, layers + 6, tiles, SUB, lanes),
            lat_edge,
            lat_edge,
        ),
        [*fields, from_core],
    )
    to_first, to_second, to_core, edges = call(
        turn_kernel,
        (lat_edge, lat_edge, made(4, rows, lanes), made(2, pairs_of_groups, SUB, lanes)),
        [*fields, *packs, part, to_first, to_second],
        input_output_aliases={11: 0, 12: 1},
    )
    from_first = lax.ppermute(to_first, ("lat", "rad"), pairs(count, 0))
    from_second = lax.ppermute(to_second, ("lat", "rad"), pairs(count, 1))
    from_core2 = lax.ppermute(to_core, "rad", swap)
    first, first_pack, stiff_pack, buoy_halo, flux, sums, done = call(
        middle_kernel,
        (
            made(2, layers + 6, tiles, SUB, lanes),
            made(2, groups, tiles, SUB, lanes),
            made(groups, tiles, SUB, lanes),
            made(layers, tiles, SUB, lanes),
            made(3, 2, layers, SUB, lanes),
            made(2, layers, tiles, SUB, lanes),
            made(6, layers, rows - 2 * SUB, lanes),
        ),
        [
            *fields,
            kernel_bulk_in,
            kernel_density_in,
            *packs,
            from_core,
            from_core2,
            wide,
            part,
        ],
        cost_estimate=HEAVY,
        scratch_shapes=[
            made(2, layers, tiles, SUB, lanes),
            made(3, groups + 1, tiles, SUB, lanes),
            made(3, layers, tiles - 2, SUB, lanes),
            made(3, groups, tiles, SUB, lanes),
            made(2, groups, tiles, SUB, lanes),
        ],
    )
    return call(
        last_kernel,
        (jax.ShapeDtypeStruct(block, F32),) * 6,
        [
            *fields,
            from_core,
            wide,
            first,
            first_pack,
            stiff_pack,
            buoy_halo,
            flux,
            sums,
            done,
            edges,
            from_first,
            from_second,
        ],
        out_specs=(hbm,) * 6,
        scratch_shapes=[
            made(2, layers + 6, 3, SUB, lanes),
            made(2, layers, 2, SUB, lanes),
            made(layers, SUB, lanes),
            made(3, layers, 2, SUB, lanes),
            made(6, layers, 2, SUB, lanes),
            pltpu.SemaphoreType.DMA((6, 3)),
        ],
    )


def solution(mesh):
    spec = P("rad", "lat", "lon")
    return jax.shard_map(
        shards, mesh=mesh, in_specs=(spec,) * 8, out_specs=(spec,) * 6, check_vma=False
    )
```

```python
import jax
import jax.numpy as jnp
from jax import lax
from jax.experimental import pallas as pl
from jax.experimental.pallas import tpu as pltpu
from jax.sharding import PartitionSpec as P

F32 = jnp.float32
SUB = 8
LAP_SCALE = 1.0 / 1152.0
RHO_SCALE = 1.0 / 2304.0
WIDTHS = (6, 6, 6, 3, 3, 3)
OFFSETS = (0, 6, 12, 21, 24, 27)
SEGMENT = 32
VMEM = pl.BlockSpec(memory_space=pltpu.VMEM)
PARAMS = pltpu.CompilerParams(vmem_limit_bytes=24 * 1024 * 1024)
HEAVY = pl.CostEstimate(flops=4000000000, bytes_accessed=1000000, transcendentals=0)


def iotas(lanes):
    return (
        lax.broadcasted_iota(jnp.int32, (SUB, lanes), 0),
        lax.broadcasted_iota(jnp.int32, (SUB, lanes), 1),
    )


def rolled(x, shift, axis):
    size = x.shape[axis]
    shift = shift % size
    return x if shift == 0 else pltpu.roll(x, shift, axis)


def lane_shift(here, there, by, lane):
    size = here.shape[1]
    if by > 0:
        return rolled(jnp.where(lane < by, there, here), size - by, 1)
    return rolled(jnp.where(lane >= size + by, there, here), -by, 1)


def row_shift(tiles, t, by, sub):
    if by > 0:
        return rolled(jnp.where(sub < by, tiles[(t + 1) % len(tiles)], tiles[t]), SUB - by, 0)
    return rolled(jnp.where(sub >= SUB + by, tiles[t - 1], tiles[t]), -by, 0)


def slope(ahead, here, ahead2, behind):
    return 27.0 * (ahead - here) - (ahead2 - behind)


def pack_three(a, b, c, low, sub):
    if low:
        return jnp.where(sub < 3, a, jnp.where(sub < 6, rolled(b, 3, 0), rolled(c, 6, 0)))
    return jnp.where(sub >= 5, a, jnp.where(sub >= 2, rolled(b, -3, 0), rolled(c, -6, 0)))


def unpack_three(x, low):
    sign = -1 if low else 1
    return x, rolled(x, 3 * sign, 0), rolled(x, 6 * sign, 0)


def edges_kernel(*refs):
    sources, fields, (to_right, to_left, to_core), sems = refs[:6], refs[6:12], refs[12:15], refs[15]
    copies = [pltpu.make_async_copy(x, y, sems.at[k]) for k, (x, y) in enumerate(zip(sources, fields))]
    for copy in copies:
        copy.start()
    layers, rows, lanes = fields[0].shape
    _, lane = iotas(lanes)
    core = lax.axis_index("rad")
    per = lanes // SEGMENT
    row = 0
    packed = {}
    for f, (width, offset) in enumerate(zip(WIDTHS, OFFSETS)):
        copies[f].wait()
        for layer in range(layers):
            group, s = divmod(layer, per)
            first = s * SEGMENT + offset
            second = first + width
            mask = lane >= second
            if second + width > lanes:
                mask = mask | (lane < second + width - lanes)
            mine = (lane >= first) & (lane < second)
            theirs = mask & (lane < second + width) if second + width <= lanes else mask
            for t in range(rows // SUB):
                x = rolled(fields[f][layer, pl.ds(t * SUB, SUB), :], second, 1)
                right, left = packed.get((group, t), (x, x))
                packed[group, t] = jnp.where(mine, x, right), jnp.where(theirs, x, left)
        to_core[row : row + width] = fields[f][pl.ds((layers - width) * (1 - core), width)]
        row += width
    for (group, t), (right, left) in packed.items():
        to_right[group, pl.ds(t * SUB, SUB), :] = right
        to_left[group, pl.ds(t * SUB, SUB), :] = left


def radial(p_at, b_at, layers):
    flux, rho = [], []
    p = [[p_at(f, k) for k in range(-3, layers + 3)] for f in range(2)]
    b = [b_at(k) for k in range(-2, layers + 2)]
    for k in range(layers + 3):
        buoy = b[k] + b[k + 1]
        grads = [slope(x[k + 2], x[k + 1], x[k + 3], x[k]) for x in p]
        flux.append([buoy * g for g in grads])
        rho.append(flux[k][0] * grads[1])
    out = []
    for k in range(layers):
        laps = [slope(flux[k + 2][f], flux[k + 1][f], flux[k + 3][f], flux[k][f]) for f in range(2)]
        out.append((laps[0], laps[1], rho[k + 1] + rho[k + 2]))
    return out


def longitudinal(here, there, lane, want_there, want_rho):
    flux, rho = [], []
    for x, y in ((here, there), (there, here)):
        buoy = x[2] + lane_shift(x[2], y[2], 1, lane)
        grads = [
            slope(
                lane_shift(x[f], y[f], 1, lane),
                x[f],
                lane_shift(x[f], y[f], 2, lane),
                lane_shift(x[f], y[f], -1, lane),
            )
            for f in range(2)
        ]
        flux.append([buoy * g for g in grads])
        rho.append(flux[-1][0] * grads[1])
    laps = []
    for x, y in ((0, 1), (1, 0))[: 2 if want_there else 1]:
        laps.append(
            [
                slope(
                    flux[x][f],
                    lane_shift(flux[x][f], flux[y][f], -1, lane),
                    lane_shift(flux[x][f], flux[y][f], 1, lane),
                    lane_shift(flux[x][f], flux[y][f], -2, lane),
                )
                for f in range(2)
            ]
        )
    density = rho[0] + lane_shift(rho[0], rho[1], -1, lane) if want_rho else None
    return laps, density


def windows(from_left, from_right, to_left, to_right, f, seg):
    offset = OFFSETS[f]
    mask = (seg >= offset) & (seg < offset + WIDTHS[f])
    return (
        rolled(jnp.where(mask, from_left, to_left), -offset, 1),
        rolled(jnp.where(mask, to_right, from_right), -offset, 1),
    )


def lon_flux(adj, fwd, buoy):
    face = buoy + rolled(buoy, -1, 1)
    grads = [slope(rolled(x, -1, 1), x, rolled(x, -2, 1), rolled(x, 1, 1)) for x in (adj, fwd)]
    flux = [face * g for g in grads]
    return flux[0], flux[1], flux[0] * grads[1]


def lon_terms(adj, fwd, buoy, want_rho):
    flux = lon_flux(adj, fwd, buoy)
    terms = [slope(x, rolled(x, 1, 1), rolled(x, -1, 1), rolled(x, 2, 1)) for x in flux[:2]]
    return terms + [flux[2] + rolled(flux[2], 1, 1)] if want_rho else terms


def edge_terms(wins, seg, want_rho):
    left = lon_terms(*(x[0] for x in wins), want_rho)
    right = lon_terms(*(x[1] for x in wins), want_rho)
    valid = (seg >= 3) & (seg < 9)
    own = [jnp.where(valid, jnp.where(seg < 6, y, x), 0.0) for x, y in zip(left, right)]
    return own, [jnp.where(seg < 6, x, y) for x, y in zip(left[:2], right[:2])]


def halos_of(wins, seg):
    return [jnp.where(seg < 6, x, y) for x, y in wins]


def spread(x, s):
    return rolled(x, -s * SEGMENT - 6, 1)


def at_ends(x, s, lane):
    return jnp.where((lane < 3) | (lane >= x.shape[1] - 3), spread(x, s), 0.0)


def merged(tiles, seg):
    half = SEGMENT // 2
    out = []
    for k in range(0, len(tiles), 2):
        x = tiles[k]
        if k + 1 < len(tiles):
            x = jnp.where(seg < half, x, rolled(tiles[k + 1], half, 1))
        out.append(x)
    return out


def unmerged(x, group):
    return rolled(x, -(SEGMENT // 2) * (group % 2), 1)


def packed_radial(groups, lane):
    size = lane.shape[1]

    def shift(x, i, by):
        step = by * SEGMENT
        if by > 0:
            return rolled(jnp.where(lane < step, x[min(i + 1, len(x) - 1)], x[i]), -step, 1)
        return rolled(jnp.where(lane >= size + step, x[max(i - 1, 0)], x[i]), -step, 1)

    adj, fwd, buoy = ([x[f] for x in groups] for f in range(3))
    flux = ([], [])
    for i in range(len(groups)):
        face = buoy[i] + shift(buoy, i, 1)
        for f, x in enumerate((adj, fwd)):
            flux[f].append(face * slope(shift(x, i, 1), x[i], shift(x, i, 2), shift(x, i, -1)))
    return [
        [slope(x[i], shift(x, i, -1), shift(x, i, 1), shift(x, i, -2)) for x in flux]
        for i in range(1, len(groups) - 1)
    ]


def lat_flux(ring, t, sub):
    adj, fwd, buoy = ring
    face = buoy[t] + row_shift(buoy, t, 1, sub)
    grads = [
        slope(row_shift(x, t, 1, sub), x[t], row_shift(x, t, 2, sub), row_shift(x, t, -1, sub))
        for x in (adj, fwd)
    ]
    flux = [face * g for g in grads]
    return flux[0], flux[1], flux[0] * grads[1]


def lat_terms(flux, t, sub, want_rho):
    adj, fwd, rho = ([x[k] for x in flux] for k in range(3))
    laps = [
        slope(x[t], row_shift(x, t, -1, sub), row_shift(x, t, 1, sub), row_shift(x, t, -2, sub))
        for x in (adj, fwd)
    ]
    return laps[0], laps[1], rho[t] + row_shift(rho, t, -1, sub) if want_rho else None


def lat_inner(ring, sub, want_rho):
    count = len(ring[0])
    flux = [list(lat_flux(ring, t, sub)) for t in range(count)]
    zero = jnp.zeros_like(ring[0][0])
    for k in range(3):
        flux[0][k] = jnp.where(sub >= 1, flux[0][k], zero)
        flux[-1][k] = jnp.where(sub < SUB - 2, flux[-1][k], zero)
    flux.append([zero] * 3)
    return [lat_terms(flux, t, sub, want_rho) for t in range(count)]


def lat_outer(adj, fwd, buoy, sub):
    ring = ([adj], [fwd], [buoy])
    mask = (sub >= SUB - 2) | (sub < 1)
    flux = [[jnp.where(mask, x, 0.0) for x in lat_flux(ring, 0, sub)]]
    return lat_terms(flux, 0, sub, True)


def places(core, layers):
    return (layers + 3) * (1 - core), (layers + 3) * core


def inner_kernel(*refs):
    fields, from_core = refs[:6], refs[6]
    wide, part, to_first, to_second, to_third = refs[7:]
    layers, rows, lanes = fields[0].shape
    tiles = rows // SUB
    sub, lane = iotas(lanes)
    core = lax.axis_index("rad")
    even = lax.axis_index("lat") % 2 == 0
    near, border = places(core, layers)
    zero = jnp.zeros((SUB, lanes), F32)
    away = (lane >= 3) & (lane < lanes - 3)

    def at(t):
        return pl.ds(t * SUB, SUB)

    for f in range(3):
        for t in range(tiles):
            for layer in range(layers):
                wide[f, layer + 6, t] = fields[f][layer, at(t), :]
            for k in range(6):
                wide[f, (layers + 6) * (1 - core) + k, t] = from_core[6 * f + k, at(t), :]
            for k in range(3):
                wide[f, border + 3 + k, t] = zero

    def send(k, low, high):
        to_first[k] = to_third[k] = jnp.where(even, high, low)
        to_second[k] = jnp.where(even, low, high)

    ends = ((0, True), (tiles - 1, False))
    third = [None, None]
    for layer in range(layers):
        send(
            layers + layer,
            *(pack_three(*(x[layer, at(t), :] for x in fields[:3]), low, sub) for t, low in ends),
        )
        for k, row in enumerate((2, SUB - 3)):
            x = rolled(fields[5][layer, at(ends[k][0]), :], layer - row, 0)
            third[k] = x if layer == 0 else jnp.where(sub == layer, x, third[k])
    send(2 * layers, *third)
    for e in range(3):
        send(
            2 * layers + 1 + e,
            *(pack_three(*(wide[f, near + 3 + e, t] for f in range(3)), low, sub) for t, low in ends),
        )

    start = 6 - 3 * core
    for t in range(tiles):
        terms = radial(
            lambda f, k: wide[f, start + k, t], lambda k: wide[2, start + k, t], layers + 3
        )
        for k, term in enumerate(terms):
            for g in range(3):
                part[g, start - 3 + k, t] = term[g]

    def own(layer, carry):
        here = [[wide[f, layer + 6, t] for t in range(tiles)] for f in range(3)]
        terms = lat_inner(here, sub, True)
        for t in range(tiles):
            lon = lon_terms(*(x[t] for x in here), True)
            for g in range(3):
                part[g, layer + 3, t] += terms[t][g] + jnp.where(away, lon[g], 0.0)
        return carry

    lax.fori_loop(0, layers, own, 0, unroll=2)

    def other(e, carry):
        here = [[wide[f, near + 3 + e, t] for t in range(tiles)] for f in range(3)]
        terms = lat_inner(here, sub, False)
        for t in range(tiles):
            lon = lon_terms(*(x[t] for x in here), False)
            for g in range(2):
                part[g, near + e, t] += terms[t][g] + jnp.where(away, lon[g], 0.0)
        return carry

    lax.fori_loop(0, 3, other, 0, unroll=True)


def turn_kernel(*refs):
    fields, packs, part = refs[:6], refs[6:10], refs[10]
    to_first, to_second, to_third, to_core, edges = refs[14:]
    layers, rows, lanes = fields[0].shape
    tiles = rows // SUB
    sub, lane = iotas(lanes)
    seg = lane % SEGMENT
    core = lax.axis_index("rad")
    even = lax.axis_index("lat") % 2 == 0
    per = lanes // SEGMENT
    groups = packs[0].shape[0]

    def send(k, low, high):
        to_first[k] = to_third[k] = jnp.where(even, high, low)
        to_second[k] = jnp.where(even, low, high)

    def ends(ref, *index):
        low, high = (ref[(*index, pl.ds(t * SUB, SUB), slice(None))] for t in (0, tiles - 1))
        return jnp.where(sub < 4, low, high)

    for k, ref in enumerate(packs):
        to_core[k] = ref[(groups - 1) * (1 - core)]
    halos = []
    for g in range(groups):
        pack = [ends(x, g) for x in packs]
        wins = [windows(*pack, f, seg) for f in range(3)]
        laps, _ = edge_terms(wins, seg, False)
        halos.append(halos_of(wins, seg))
        for s in range(min(per, layers - g * per)):
            layer = g * per + s
            here = [ends(x, layer) for x in fields]
            stiff = here[5] * LAP_SCALE
            made = []
            for f in range(2):
                before = jnp.where(sub < 4, part[f, layer + 3, 0], part[f, layer + 3, tiles - 1])
                lap = before + at_ends(laps[f], s, lane)
                made.append(2.0 * here[f] - here[3 + f] + stiff * lap)
            send(layer, *(pack_three(*made, here[5], low, sub) for low in (True, False)))
    both = [merged([pack_three(*x, low, sub) for x in halos], seg) for low in (True, False)]
    for k, (low, high) in enumerate(zip(*both)):
        send(2 * layers + 4 + k, low, high)
        edges[0, k] = low
        edges[1, k] = high


def middle_kernel(*refs):
    fields, (bulk_in, density_in) = refs[:6], refs[6:8]
    packs, from_core, from_core2, wide, part = refs[8:12], refs[12], refs[13], refs[14], refs[15]
    first, first_pack, stiff_pack, buoy_halo, flux_out, sums, done = refs[16:23]
    first_halo, own_pack, part_last, halo_pack, lap_pack = refs[23:]
    layers, rows, lanes = fields[0].shape
    tiles = rows // SUB
    sub, lane = iotas(lanes)
    seg = lane % SEGMENT
    core = lax.axis_index("rad")
    near, border = places(core, layers)
    per = lanes // SEGMENT
    groups = packs[0].shape[0]
    zero = jnp.zeros((SUB, lanes), F32)
    inside = range(1, tiles - 1)

    def at(t):
        return pl.ds(pl.multiple_of(t * SUB, SUB), SUB)

    def edges_at(t, carry):
        sources = [[x[group, at(t), :] for x in packs] for group in range(groups)]
        sources.append([from_core2[k, at(t), :] for k in range(4)])
        wins = [[windows(*x, f, seg) for f in range(3)] for x in sources]
        halos = [halos_of(x, seg) for x in wins]
        before = [jnp.where(core == 0, 0.0, x) for x in halos[-1]]
        after = [jnp.where(core == 0, x, 0.0) for x in halos[-1]]
        radials = packed_radial([before, *halos[:-1], after], lane)
        terms = [edge_terms(x, seg, k < groups) for k, x in enumerate(wins)]
        own = [x for x, _ in terms]
        own[groups] = [
            jnp.where(core == 0, x, rolled(x, -(per - 3) * SEGMENT, 1)) for x in own[groups]
        ]
        for group in range(groups):
            for f in range(3):
                halo_pack[f, group, t] = halos[group][f]
            for g in range(2):
                lap_pack[g, group, t] = terms[group][1][g] + radials[group][g]
        for group in range(groups + 1):
            for g, x in enumerate(own[group]):
                own_pack[g, group, t] = x
        return carry

    lax.fori_loop(0, tiles, edges_at, 0)
    for group in range(groups):
        halo = [[halo_pack[f, group, t] for t in range(tiles)] for f in range(3)]
        lat = lat_inner(halo, sub, False)
        for t in range(tiles):
            rest = []
            for f in range(3, 6):
                offset = OFFSETS[f]
                mask = (seg >= offset) & (seg < offset + WIDTHS[f])
                x = jnp.where(mask, packs[0][group, at(t), :], packs[1][group, at(t), :])
                rest.append(rolled(x, 3 - offset, 1))
            stiff = rest[2] * LAP_SCALE
            stiff_pack[group, t] = stiff
            for g in range(2):
                lap = lap_pack[g, group, t] + lat[t][g]
                first_pack[g, group, t] = 2.0 * halo[g][t] - rest[g] + stiff * lap
    for g in range(2):
        for k in range(3):
            for t in range(tiles):
                first[g, border + k, t] = zero

    def first_at(t, carry):
        for layer in range(layers):
            group, s = divmod(layer, per)
            buoy_halo[layer, t] = spread(halo_pack[2, group, t], s)
            stiff = fields[5][layer, at(t), :] * LAP_SCALE
            here = [wide[f, layer + 6, t] for f in range(2)]
            for g in range(2):
                first_halo[g, layer, t] = spread(first_pack[g, group, t], s)
                lap = part[g, layer + 3, t] + at_ends(own_pack[g, group, t], s, lane)
                update = stiff * lap
                first[g, layer + 3, t] = 2.0 * here[g] - fields[3 + g][layer, at(t), :] + update
            sums[0, layer, t] = bulk_in[layer, at(t), :] + here[0] * update
            rho = part[2, layer + 3, t] + at_ends(own_pack[2, group, t], s, lane)
            sums[1, layer, t] = density_in[layer, at(t), :] + RHO_SCALE * rho
        for e in range(3):
            stiff = from_core[24 + e, at(t), :] * LAP_SCALE
            for g in range(2):
                lap = part[g, near + e, t] + at_ends(own_pack[g, groups, t], e, lane)
                past = from_core[18 + 3 * g + e, at(t), :]
                first[g, near + e, t] = 2.0 * wide[g, near + 3 + e, t] - past + stiff * lap
        return carry

    lax.fori_loop(0, tiles, first_at, 0)

    for t in inside:
        terms = radial(lambda f, k: first[f, 3 + k, t], lambda k: wide[2, 6 + k, t], layers)
        for k, term in enumerate(terms):
            for g in range(3):
                part_last[g, k, t - 1] = term[g]

    def last(layer, carry):
        here = [[first[f, layer + 3, t] for t in range(tiles)] for f in range(2)]
        here.append([wide[2, layer + 6, t] for t in range(tiles)])
        flux = [lat_flux(here, t, sub) for t in range(tiles)]
        for k in range(3):
            for n, t in enumerate((1, tiles - 2)):
                flux_out[k, n, layer] = flux[t][k]
        for t in inside:
            lat = lat_terms(flux, t, sub, True)
            there = [first_halo[0, layer, t], first_halo[1, layer, t], buoy_halo[layer, t]]
            laps, rho = longitudinal([x[t] for x in here], there, lane, False, True)
            stiff = fields[5][layer, at(t), :] * LAP_SCALE
            for g in range(2):
                update = stiff * (part_last[g, layer, t - 1] + lat[g] + laps[0][g])
                done[2 * g, layer, at(t - 1), :] = (
                    2.0 * here[g][t] - fields[g][layer, at(t), :] + update
                )
                done[2 * g + 1, layer, at(t - 1), :] = here[g][t]
            done[4, layer, at(t - 1), :] = sums[0, layer, t] + here[0][t] * update
            done[5, layer, at(t - 1), :] = sums[1, layer, t] + RHO_SCALE * (
                part_last[2, layer, t - 1] + lat[2] + rho
            )
        return carry

    lax.fori_loop(0, layers, last, 0, unroll=4)


def last_kernel(*refs):
    fields, from_core = refs[:6], refs[6]
    wide, first, first_pack, stiff_pack, buoy_halo, flux_in, sums, done = refs[7:15]
    edges, from_first, from_second, from_third = refs[15:19]
    outs = refs[19:25]
    fixed, fixed_halo, ring_buoy, part, made, sems = refs[25:]
    layers, rows, lanes = fields[0].shape
    tiles = rows // SUB
    sub, lane = iotas(lanes)
    core = lax.axis_index("rad")
    place, count = lax.axis_index("lat"), lax.axis_size("lat")
    even = place % 2 == 0
    near, border = places(core, layers)
    zero = jnp.zeros((SUB, lanes), F32)
    ends = ((0, sub < 3), (tiles - 1, sub >= SUB - 3))
    copies = [
        pltpu.make_async_copy(done.at[k], out.at[:, pl.ds(SUB, rows - 2 * SUB), :], sems.at[k, 0])
        for k, out in enumerate(outs)
    ]
    for copy in copies:
        copy.start()

    def at(t):
        return pl.ds(t * SUB, SUB)

    def received(k):
        one = jnp.where(place % 4 < 2, from_first[k], from_third[k])
        two = from_second[k]
        behind, ahead = jnp.where(even, two, one), jnp.where(even, one, two)
        return jnp.where(place > 0, behind, 0.0), jnp.where(place < count - 1, ahead, 0.0)

    def join(behind, ahead):
        return jnp.where(sub < 4, ahead, behind)

    def three(k):
        behind, ahead = received(k)
        return list(zip(unpack_three(behind, False), unpack_three(ahead, True)))

    def outer(own, halos):
        low = [jnp.where(sub < 4, x[0], h[0]) for x, h in zip(own, halos)]
        high = [jnp.where(sub < 4, h[1], x[1]) for x, h in zip(own, halos)]
        return lat_outer(*low, sub), lat_outer(*high, sub)

    for g in range(2):
        for k in range(3):
            for n in range(2):
                fixed[g, border + k, n] = zero

    per = lanes // SEGMENT
    for group in range(stiff_pack.shape[0]):
        if group % 2 == 0:
            k = group // 2
            mine = list(zip(unpack_three(edges[0, k], True), unpack_three(edges[1, k], False)))
            side = outer(mine, three(2 * layers + 4 + k))
        for n, (t, mask) in enumerate(ends):
            for g in range(2):
                lap = jnp.where(mask, unmerged(side[n][g], group), 0.0)
                x = first_pack[g, group, t] + stiff_pack[group, t] * lap
                for s in range(min(per, layers - group * per)):
                    fixed_halo[g, group * per + s, n] = spread(x, s)

    for e in range(3):
        halos = three(2 * layers + 1 + e)
        mine = [(wide[f, near + 3 + e, 0], wide[f, near + 3 + e, tiles - 1]) for f in range(3)]
        side = outer(mine, halos)
        for n, (t, mask) in enumerate(ends):
            stiff = from_core[24 + e, at(t), :] * LAP_SCALE
            for g in range(2):
                lap = jnp.where(mask, side[n][g], 0.0)
                fixed[g, near + e, n] = first[g, near + e, t] + stiff * lap

    third = received(2 * layers)
    for layer in range(layers):
        halos = three(layers + layer)
        mine = [(x[layer, at(0), :], x[layer, at(tiles - 1), :]) for x in fields[:3]]
        side = outer(mine, halos)
        for n, (t, mask) in enumerate(ends):
            stiff = fields[5][layer, at(t), :] * LAP_SCALE
            for g in range(2):
                update = stiff * jnp.where(mask, side[n][g], 0.0)
                fixed[g, layer + 3, n] = first[g, layer + 3, t] + update
            made[4, layer, n] = sums[0, layer, t] + mine[0][n] * update
            made[5, layer, n] = sums[1, layer, t] + RHO_SCALE * jnp.where(mask, side[n][2], 0.0)
        adj, fwd, stiff = three(layer)
        low, high = (rolled(third[k], row - layer, 0) for k, row in enumerate((SUB - 3, 2)))
        stiff = jnp.where(
            sub < 4,
            jnp.where(sub == 2, high, stiff[1]),
            jnp.where(sub == SUB - 3, low, stiff[0]),
        )
        for g, x in enumerate((adj, fwd)):
            lap = join(side[0][g], side[1][g])
            fixed[g, layer + 3, 2] = join(*x) + stiff * LAP_SCALE * lap
        ring_buoy[layer] = join(*halos[2])

    for n, (t, _) in enumerate(ends):
        terms = radial(lambda f, k: fixed[f, 3 + k, n], lambda k: wide[2, 6 + k, t], layers)
        for k, term in enumerate(terms):
            for g in range(3):
                part[g, k, n] = term[g]

    def last(layer, carry):
        buoys = [wide[2, layer + 6, t] for t in (0, 1, tiles - 2, tiles - 1)]
        rings = [
            [fixed[f, layer + 3, 2], fixed[f, layer + 3, 0], first[f, layer + 3, 1]]
            + [first[f, layer + 3, tiles - 2], fixed[f, layer + 3, 1]]
            for f in range(2)
        ] + [[ring_buoy[layer], *buoys]]
        flux = [None] * 5
        for t in (0, 1, 4):
            flux[t] = lat_flux(rings, t, sub)
        for n in range(2):
            flux[2 + n] = [flux_in[k, n, layer] for k in range(3)]
        for n, (t, _) in enumerate(ends):
            k = (1, 4)[n]
            here = [x[k] for x in rings]
            lat = lat_terms(flux, k, sub, True)
            there = [fixed_halo[0, layer, n], fixed_halo[1, layer, n], buoy_halo[layer, t]]
            laps, rho = longitudinal(here, there, lane, False, True)
            stiff = fields[5][layer, at(t), :] * LAP_SCALE
            for g in range(2):
                update = stiff * (part[g, layer, n] + lat[g] + laps[0][g])
                made[2 * g, layer, n] = 2.0 * here[g] - fields[g][layer, at(t), :] + update
                made[2 * g + 1, layer, n] = here[g]
            made[4, layer, n] += here[0] * update
            made[5, layer, n] += RHO_SCALE * (part[2, layer, n] + lat[2] + rho)
        return carry

    lax.fori_loop(0, layers, last, 0, unroll=True)
    for k, out in enumerate(outs):
        for n, (t, _) in enumerate(ends):
            copy = pltpu.make_async_copy(made.at[k, :, n], out.at[:, at(t), :], sems.at[k, 1 + n])
            copy.start()
            copies.append(copy)
    for copy in copies:
        copy.wait()


def pairs(count, start, step):
    partner = {i: i for i in range(count)}
    for i in range(start, count - 1, step):
        partner[i], partner[i + 1] = i + 1, i
    return [
        (2 * i + core, 2 * j + (core if i != j else 1 - core))
        for i, j in partner.items()
        for core in range(2)
    ]


def call(kernel, out_shape, args, in_specs=None, out_specs=None, **more):
    return pl.pallas_call(
        kernel,
        out_shape=out_shape,
        in_specs=in_specs or [VMEM] * len(args),
        out_specs=out_specs or (VMEM,) * len(out_shape),
        compiler_params=PARAMS,
        **more,
    )(*args)


def shards(
    adj_now, adj_next, fwd_now, fwd_next, stiffness, buoyancy, kernel_bulk_in, kernel_density_in
):
    layers, rows, lanes = adj_now.shape
    tiles = rows // SUB
    fields = (adj_now, fwd_now, buoyancy, adj_next, fwd_next, stiffness)
    groups = -(-layers // (lanes // SEGMENT))
    around, count = lax.axis_size("lon"), lax.axis_size("lat")
    ring = [(i, (i + 1) % around) for i in range(around)]
    swap = [(0, 1), (1, 0)]

    def made(*shape):
        return pltpu.VMEM(shape, F32)

    block = (layers, rows, lanes)
    edge = made(groups, rows, lanes)
    hbm = pl.BlockSpec(memory_space=pltpu.HBM)
    *fields, to_right, to_left, to_core = call(
        edges_kernel,
        (made(*block),) * 6 + (edge, edge, made(sum(WIDTHS), rows, lanes)),
        [pltpu.with_memory_space_constraint(x, pltpu.HBM) for x in fields],
        in_specs=[hbm] * 6,
        scratch_shapes=[pltpu.SemaphoreType.DMA((6,))],
    )
    from_left = lax.ppermute(to_right, "lon", ring)
    from_right = lax.ppermute(to_left, "lon", [(b, a) for a, b in ring])
    from_core = lax.ppermute(to_core, "rad", swap)
    pairs_of_groups = -(-groups // 2)
    lat_edge = made(2 * layers + 4 + pairs_of_groups, SUB, lanes)
    packs = [from_left, from_right, to_left, to_right]
    wide, part, to_first, to_second, to_third = call(
        inner_kernel,
        (
            made(3, layers + 12, tiles, SUB, lanes),
            made(3, layers + 6, tiles, SUB, lanes),
            lat_edge,
            lat_edge,
            lat_edge,
        ),
        [*fields, from_core],
    )
    to_first, to_second, to_third, to_core, edges = call(
        turn_kernel,
        (lat_edge, lat_edge, lat_edge, made(4, rows, lanes), made(2, pairs_of_groups, SUB, lanes)),
        [*fields, *packs, part, to_first, to_second, to_third],
        input_output_aliases={11: 0, 12: 1, 13: 2},
    )
    from_first = lax.ppermute(to_first, ("lat", "rad"), pairs(count, 0, 4))
    from_second = lax.ppermute(to_second, ("lat", "rad"), pairs(count, 1, 2))
    from_third = lax.ppermute(to_third, ("lat", "rad"), pairs(count, 2, 4))
    from_core2 = lax.ppermute(to_core, "rad", swap)
    first, first_pack, stiff_pack, buoy_halo, flux, sums, done = call(
        middle_kernel,
        (
            made(2, layers + 6, tiles, SUB, lanes),
            made(2, groups, tiles, SUB, lanes),
            made(groups, tiles, SUB, lanes),
            made(layers, tiles, SUB, lanes),
            made(3, 2, layers, SUB, lanes),
            made(2, layers, tiles, SUB, lanes),
            made(6, layers, rows - 2 * SUB, lanes),
        ),
        [
            *fields,
            kernel_bulk_in,
            kernel_density_in,
            *packs,
            from_core,
            from_core2,
            wide,
            part,
        ],
        cost_estimate=HEAVY,
        scratch_shapes=[
            made(2, layers, tiles, SUB, lanes),
            made(3, groups + 1, tiles, SUB, lanes),
            made(3, layers, tiles - 2, SUB, lanes),
            made(3, groups, tiles, SUB, lanes),
            made(2, groups, tiles, SUB, lanes),
        ],
    )
    return call(
        last_kernel,
        (jax.ShapeDtypeStruct(block, F32),) * 6,
        [
            *fields,
            from_core,
            wide,
            first,
            first_pack,
            stiff_pack,
            buoy_halo,
            flux,
            sums,
            done,
            edges,
            from_first,
            from_second,
            from_third,
        ],
        out_specs=(hbm,) * 6,
        scratch_shapes=[
            made(2, layers + 6, 3, SUB, lanes),
            made(2, layers, 2, SUB, lanes),
            made(layers, SUB, lanes),
            made(3, layers, 2, SUB, lanes),
            made(6, layers, 2, SUB, lanes),
            pltpu.SemaphoreType.DMA((6, 3)),
        ],
    )


def solution(mesh):
    spec = P("rad", "lat", "lon")
    return jax.shard_map(
        shards, mesh=mesh, in_specs=(spec,) * 8, out_specs=(spec,) * 6, check_vma=False
    )
```

```python
import jax
import jax.numpy as jnp
from jax import lax
from jax.experimental import pallas as pl
from jax.experimental.pallas import tpu as pltpu
from jax.sharding import PartitionSpec as P

F32 = jnp.float32
SUB = 8
LAP_SCALE = 1.0 / 1152.0
RHO_SCALE = 1.0 / 2304.0
WIDTHS = (6, 6, 6, 3, 3, 3)
OFFSETS = (0, 6, 12, 21, 24, 27)
SEGMENT = 32
VMEM = pl.BlockSpec(memory_space=pltpu.VMEM)
PARAMS = pltpu.CompilerParams(vmem_limit_bytes=24 * 1024 * 1024)
HEAVY = pl.CostEstimate(flops=4000000000, bytes_accessed=1000000, transcendentals=0)


def iotas(lanes):
    return (
        lax.broadcasted_iota(jnp.int32, (SUB, lanes), 0),
        lax.broadcasted_iota(jnp.int32, (SUB, lanes), 1),
    )


def rolled(x, shift, axis):
    size = x.shape[axis]
    shift = shift % size
    return x if shift == 0 else pltpu.roll(x, shift, axis)


def lane_shift(here, there, by, lane):
    size = here.shape[1]
    if by > 0:
        return rolled(jnp.where(lane < by, there, here), size - by, 1)
    return rolled(jnp.where(lane >= size + by, there, here), -by, 1)


def row_shift(tiles, t, by, sub):
    if by > 0:
        return rolled(jnp.where(sub < by, tiles[(t + 1) % len(tiles)], tiles[t]), SUB - by, 0)
    return rolled(jnp.where(sub >= SUB + by, tiles[t - 1], tiles[t]), -by, 0)


def slope(ahead, here, ahead2, behind):
    return 27.0 * (ahead - here) - (ahead2 - behind)


def pack_three(a, b, c, low, sub):
    if low:
        return jnp.where(sub < 3, a, jnp.where(sub < 6, rolled(b, 3, 0), rolled(c, 6, 0)))
    return jnp.where(sub >= 5, a, jnp.where(sub >= 2, rolled(b, -3, 0), rolled(c, -6, 0)))


def unpack_three(x, low):
    sign = -1 if low else 1
    return x, rolled(x, 3 * sign, 0), rolled(x, 6 * sign, 0)


def edges_kernel(*refs):
    sources, fields, (to_right, to_left, to_core), sems = refs[:6], refs[6:12], refs[12:15], refs[15]
    copies = [pltpu.make_async_copy(x, y, sems.at[k]) for k, (x, y) in enumerate(zip(sources, fields))]
    for copy in copies:
        copy.start()
    layers, rows, lanes = fields[0].shape
    _, lane = iotas(lanes)
    core = lax.axis_index("rad")
    per = lanes // SEGMENT
    row = 0
    packed = {}
    for f, (width, offset) in enumerate(zip(WIDTHS, OFFSETS)):
        copies[f].wait()
        for layer in range(layers):
            group, s = divmod(layer, per)
            first = s * SEGMENT + offset
            second = first + width
            mask = lane >= second
            if second + width > lanes:
                mask = mask | (lane < second + width - lanes)
            mine = (lane >= first) & (lane < second)
            theirs = mask & (lane < second + width) if second + width <= lanes else mask
            for t in range(rows // SUB):
                x = rolled(fields[f][layer, pl.ds(t * SUB, SUB), :], second, 1)
                right, left = packed.get((group, t), (x, x))
                packed[group, t] = jnp.where(mine, x, right), jnp.where(theirs, x, left)
        to_core[row : row + width] = fields[f][pl.ds((layers - width) * (1 - core), width)]
        row += width
    for (group, t), (right, left) in packed.items():
        to_right[group, pl.ds(t * SUB, SUB), :] = right
        to_left[group, pl.ds(t * SUB, SUB), :] = left


def radial(p_at, b_at, layers):
    flux, rho = [], []
    p = [[p_at(f, k) for k in range(-3, layers + 3)] for f in range(2)]
    b = [b_at(k) for k in range(-2, layers + 2)]
    for k in range(layers + 3):
        buoy = b[k] + b[k + 1]
        grads = [slope(x[k + 2], x[k + 1], x[k + 3], x[k]) for x in p]
        flux.append([buoy * g for g in grads])
        rho.append(flux[k][0] * grads[1])
    out = []
    for k in range(layers):
        laps = [slope(flux[k + 2][f], flux[k + 1][f], flux[k + 3][f], flux[k][f]) for f in range(2)]
        out.append((laps[0], laps[1], rho[k + 1] + rho[k + 2]))
    return out


def longitudinal(here, there, lane, want_there, want_rho):
    flux, rho = [], []
    for x, y in ((here, there), (there, here)):
        buoy = x[2] + lane_shift(x[2], y[2], 1, lane)
        grads = [
            slope(
                lane_shift(x[f], y[f], 1, lane),
                x[f],
                lane_shift(x[f], y[f], 2, lane),
                lane_shift(x[f], y[f], -1, lane),
            )
            for f in range(2)
        ]
        flux.append([buoy * g for g in grads])
        rho.append(flux[-1][0] * grads[1])
    laps = []
    for x, y in ((0, 1), (1, 0))[: 2 if want_there else 1]:
        laps.append(
            [
                slope(
                    flux[x][f],
                    lane_shift(flux[x][f], flux[y][f], -1, lane),
                    lane_shift(flux[x][f], flux[y][f], 1, lane),
                    lane_shift(flux[x][f], flux[y][f], -2, lane),
                )
                for f in range(2)
            ]
        )
    density = rho[0] + lane_shift(rho[0], rho[1], -1, lane) if want_rho else None
    return laps, density


def windows(from_left, from_right, to_left, to_right, f, seg):
    offset = OFFSETS[f]
    mask = (seg >= offset) & (seg < offset + WIDTHS[f])
    return jnp.where(mask, from_left, to_left), jnp.where(mask, to_right, from_right)


def lon_flux(fields, offsets):
    def shift(f, by):
        return rolled(fields[f], -offsets[f] - by, 1)

    face = shift(2, 0) + shift(2, 1)
    grads = [slope(shift(f, 1), shift(f, 0), shift(f, 2), shift(f, -1)) for f in range(2)]
    flux = [face * g for g in grads]
    return flux[0], flux[1], flux[0] * grads[1]


def lon_terms(fields, want_rho, offsets=(0, 0, 0)):
    flux = lon_flux(fields, offsets)
    terms = [slope(x, rolled(x, 1, 1), rolled(x, -1, 1), rolled(x, 2, 1)) for x in flux[:2]]
    return terms + [flux[2] + rolled(flux[2], 1, 1)] if want_rho else terms


def edge_terms(wins, seg, want_rho, offsets):
    left = lon_terms([x[0] for x in wins], want_rho, offsets)
    right = lon_terms([x[1] for x in wins], want_rho, offsets)
    valid = (seg >= 3) & (seg < 9)
    own = [jnp.where(valid, jnp.where(seg < 6, y, x), 0.0) for x, y in zip(left, right)]
    return own, [jnp.where(seg < 6, x, y) for x, y in zip(left[:2], right[:2])]


def halos_of(wins, seg):
    return [jnp.where(seg < 6, x, y) for x, y in wins]


def aligned(wins):
    return [tuple(rolled(x, -offset, 1) for x in win) for win, offset in zip(wins, OFFSETS)]


def spread(x, s):
    return rolled(x, -s * SEGMENT - 6, 1)


def at_ends(x, s, lane):
    return jnp.where((lane < 3) | (lane >= x.shape[1] - 3), spread(x, s), 0.0)


def merged(tiles, seg):
    half = SEGMENT // 2
    out = []
    for k in range(0, len(tiles), 2):
        x = tiles[k]
        if k + 1 < len(tiles):
            x = jnp.where(seg < half, x, rolled(tiles[k + 1], half, 1))
        out.append(x)
    return out


def unmerged(x, group):
    return rolled(x, -(SEGMENT // 2) * (group % 2), 1)


def packed_radial(groups, lane):
    size = lane.shape[1]

    def shift(x, i, by):
        step = by * SEGMENT
        if by > 0:
            return rolled(jnp.where(lane < step, x[min(i + 1, len(x) - 1)], x[i]), -step, 1)
        return rolled(jnp.where(lane >= size + step, x[max(i - 1, 0)], x[i]), -step, 1)

    adj, fwd, buoy = ([x[f] for x in groups] for f in range(3))
    flux = ([], [])
    for i in range(len(groups)):
        face = buoy[i] + shift(buoy, i, 1)
        for f, x in enumerate((adj, fwd)):
            flux[f].append(face * slope(shift(x, i, 1), x[i], shift(x, i, 2), shift(x, i, -1)))
    return [
        [slope(x[i], shift(x, i, -1), shift(x, i, 1), shift(x, i, -2)) for x in flux]
        for i in range(1, len(groups) - 1)
    ]


def lat_flux(ring, t, sub):
    adj, fwd, buoy = ring
    face = buoy[t] + row_shift(buoy, t, 1, sub)
    grads = [
        slope(row_shift(x, t, 1, sub), x[t], row_shift(x, t, 2, sub), row_shift(x, t, -1, sub))
        for x in (adj, fwd)
    ]
    flux = [face * g for g in grads]
    return flux[0], flux[1], flux[0] * grads[1]


def lat_terms(flux, t, sub, want_rho):
    adj, fwd, rho = ([x[k] for x in flux] for k in range(3))
    laps = [
        slope(x[t], row_shift(x, t, -1, sub), row_shift(x, t, 1, sub), row_shift(x, t, -2, sub))
        for x in (adj, fwd)
    ]
    return laps[0], laps[1], rho[t] + row_shift(rho, t, -1, sub) if want_rho else None


def lat_inner(ring, sub, want_rho):
    count = len(ring[0])
    flux = [list(lat_flux(ring, t, sub)) for t in range(count)]
    zero = jnp.zeros_like(ring[0][0])
    for k in range(3):
        flux[0][k] = jnp.where(sub >= 1, flux[0][k], zero)
        flux[-1][k] = jnp.where(sub < SUB - 2, flux[-1][k], zero)
    flux.append([zero] * 3)
    return [lat_terms(flux, t, sub, want_rho) for t in range(count)]


def lat_outer(adj, fwd, buoy, sub):
    ring = ([adj], [fwd], [buoy])
    mask = (sub >= SUB - 2) | (sub < 1)
    flux = [[jnp.where(mask, x, 0.0) for x in lat_flux(ring, 0, sub)]]
    return lat_terms(flux, 0, sub, True)


def places(core, layers):
    return (layers + 3) * (1 - core), (layers + 3) * core


def inner_kernel(*refs):
    fields, from_core = refs[:6], refs[6]
    wide, part, to_first, to_second, to_third = refs[7:]
    layers, rows, lanes = fields[0].shape
    tiles = rows // SUB
    sub, lane = iotas(lanes)
    core = lax.axis_index("rad")
    even = lax.axis_index("lat") % 2 == 0
    near, border = places(core, layers)
    zero = jnp.zeros((SUB, lanes), F32)
    away = (lane >= 3) & (lane < lanes - 3)

    def at(t):
        return pl.ds(t * SUB, SUB)

    for f in range(3):
        for t in range(tiles):
            for layer in range(layers):
                wide[f, layer + 6, t] = fields[f][layer, at(t), :]
            for k in range(6):
                wide[f, (layers + 6) * (1 - core) + k, t] = from_core[6 * f + k, at(t), :]
            for k in range(3):
                wide[f, border + 3 + k, t] = zero

    def send(k, low, high):
        to_first[k] = to_third[k] = jnp.where(even, high, low)
        to_second[k] = jnp.where(even, low, high)

    ends = ((0, True), (tiles - 1, False))
    third = [None, None]
    for layer in range(layers):
        send(
            layers + layer,
            *(pack_three(*(x[layer, at(t), :] for x in fields[:3]), low, sub) for t, low in ends),
        )
        for k, row in enumerate((2, SUB - 3)):
            x = rolled(fields[5][layer, at(ends[k][0]), :], layer - row, 0)
            third[k] = x if layer == 0 else jnp.where(sub == layer, x, third[k])
    send(2 * layers, *third)
    for e in range(3):
        send(
            2 * layers + 1 + e,
            *(pack_three(*(wide[f, near + 3 + e, t] for f in range(3)), low, sub) for t, low in ends),
        )

    start = 6 - 3 * core
    for t in range(tiles):
        terms = radial(
            lambda f, k: wide[f, start + k, t], lambda k: wide[2, start + k, t], layers + 3
        )
        for k, term in enumerate(terms):
            for g in range(3):
                part[g, start - 3 + k, t] = term[g]

    def own(layer, carry):
        here = [[wide[f, layer + 6, t] for t in range(tiles)] for f in range(3)]
        terms = lat_inner(here, sub, True)
        for t in range(tiles):
            lon = lon_terms([x[t] for x in here], True)
            for g in range(3):
                part[g, layer + 3, t] += terms[t][g] + jnp.where(away, lon[g], 0.0)
        return carry

    lax.fori_loop(0, layers, own, 0, unroll=2)

    def other(e, carry):
        here = [[wide[f, near + 3 + e, t] for t in range(tiles)] for f in range(3)]
        terms = lat_inner(here, sub, False)
        for t in range(tiles):
            lon = lon_terms([x[t] for x in here], False)
            for g in range(2):
                part[g, near + e, t] += terms[t][g] + jnp.where(away, lon[g], 0.0)
        return carry

    lax.fori_loop(0, 3, other, 0, unroll=True)


def turn_kernel(*refs):
    fields, packs, part = refs[:6], refs[6:10], refs[10]
    to_first, to_second, to_third, to_core, edges = refs[14:]
    layers, rows, lanes = fields[0].shape
    tiles = rows // SUB
    sub, lane = iotas(lanes)
    seg = lane % SEGMENT
    core = lax.axis_index("rad")
    even = lax.axis_index("lat") % 2 == 0
    per = lanes // SEGMENT
    groups = packs[0].shape[0]

    def send(k, low, high):
        to_first[k] = to_third[k] = jnp.where(even, high, low)
        to_second[k] = jnp.where(even, low, high)

    def ends(ref, *index):
        low, high = (ref[(*index, pl.ds(t * SUB, SUB), slice(None))] for t in (0, tiles - 1))
        return jnp.where(sub < 4, low, high)

    for k, ref in enumerate(packs):
        to_core[k] = ref[(groups - 1) * (1 - core)]
    halos = []
    for g in range(groups):
        pack = [ends(x, g) for x in packs]
        wins = [windows(*pack, f, seg) for f in range(3)]
        laps, _ = edge_terms(wins, seg, False, OFFSETS)
        halos.append(halos_of(aligned(wins), seg))
        for s in range(min(per, layers - g * per)):
            layer = g * per + s
            here = [ends(x, layer) for x in fields]
            stiff = here[5] * LAP_SCALE
            made = []
            for f in range(2):
                before = jnp.where(sub < 4, part[f, layer + 3, 0], part[f, layer + 3, tiles - 1])
                lap = before + at_ends(laps[f], s, lane)
                made.append(2.0 * here[f] - here[3 + f] + stiff * lap)
            send(layer, *(pack_three(*made, here[5], low, sub) for low in (True, False)))
    both = [merged([pack_three(*x, low, sub) for x in halos], seg) for low in (True, False)]
    for k, (low, high) in enumerate(zip(*both)):
        send(2 * layers + 4 + k, low, high)
        edges[0, k] = low
        edges[1, k] = high


def middle_kernel(*refs):
    fields, (bulk_in, density_in) = refs[:6], refs[6:8]
    packs, from_core, from_core2, wide, part = refs[8:12], refs[12], refs[13], refs[14], refs[15]
    first, first_pack, stiff_pack, buoy_halo, flux_out, sums, done = refs[16:23]
    first_halo, own_pack, part_last, halo_pack, lap_pack = refs[23:]
    layers, rows, lanes = fields[0].shape
    tiles = rows // SUB
    sub, lane = iotas(lanes)
    seg = lane % SEGMENT
    core = lax.axis_index("rad")
    near, border = places(core, layers)
    per = lanes // SEGMENT
    groups = packs[0].shape[0]
    zero = jnp.zeros((SUB, lanes), F32)
    inside = range(1, tiles - 1)

    def at(t):
        return pl.ds(pl.multiple_of(t * SUB, SUB), SUB)

    def edges_at(t, carry):
        sources = [[x[group, at(t), :] for x in packs] for group in range(groups)]
        sources.append([from_core2[k, at(t), :] for k in range(4)])
        wins = [aligned([windows(*x, f, seg) for f in range(3)]) for x in sources]
        halos = [halos_of(x, seg) for x in wins]
        before = [jnp.where(core == 0, 0.0, x) for x in halos[-1]]
        after = [jnp.where(core == 0, x, 0.0) for x in halos[-1]]
        radials = packed_radial([before, *halos[:-1], after], lane)
        terms = [edge_terms(x, seg, True, (0, 0, 0)) for x in wins[:-1]]
        own = [x for x, _ in terms]
        for group in range(groups):
            for f, x in enumerate(halos[group]):
                halo_pack[f, group, t] = x
            for g in range(2):
                lap_pack[g, group, t] = terms[group][1][g] + radials[group][g]
        for group in range(groups):
            for g, x in enumerate(own[group]):
                own_pack[g, group, t] = x
        return carry

    def other_at(t, carry):
        other = [from_core2[k, at(t), :] for k in range(4)]
        wins = aligned([windows(*other, f, seg) for f in range(3)])
        own, _ = edge_terms(wins, seg, False, (0, 0, 0))
        for g in range(2):
            own_pack[g, groups, t] = jnp.where(core == 0, own[g], rolled(own[g], -(per - 3) * SEGMENT, 1))
        return carry

    lax.fori_loop(0, tiles, edges_at, 0, unroll=2)
    lax.fori_loop(0, tiles, other_at, 0, unroll=True)
    for group in range(groups):
        halo = [[halo_pack[f, group, t] for t in range(tiles)] for f in range(3)]
        lat = lat_inner(halo, sub, False)
        for t in range(tiles):
            rest = []
            for f in range(3, 6):
                offset = OFFSETS[f]
                mask = (seg >= offset) & (seg < offset + WIDTHS[f])
                x = jnp.where(mask, packs[0][group, at(t), :], packs[1][group, at(t), :])
                rest.append(rolled(x, 3 - offset, 1))
            stiff = rest[2] * LAP_SCALE
            stiff_pack[group, t] = stiff
            for g in range(2):
                lap = lap_pack[g, group, t] + lat[t][g]
                first_pack[g, group, t] = 2.0 * halo[g][t] - rest[g] + stiff * lap
    for g in range(2):
        for k in range(3):
            for t in range(tiles):
                first[g, border + k, t] = zero

    def first_at(t, carry):
        for layer in range(layers):
            group, s = divmod(layer, per)
            buoy_halo[layer, t] = spread(halo_pack[2, group, t], s)
            stiff = fields[5][layer, at(t), :] * LAP_SCALE
            here = [wide[f, layer + 6, t] for f in range(2)]
            for g in range(2):
                first_halo[g, layer, t] = spread(first_pack[g, group, t], s)
                lap = part[g, layer + 3, t] + at_ends(own_pack[g, group, t], s, lane)
                update = stiff * lap
                first[g, layer + 3, t] = 2.0 * here[g] - fields[3 + g][layer, at(t), :] + update
            sums[0, layer, t] = bulk_in[layer, at(t), :] + here[0] * update
            rho = part[2, layer + 3, t] + at_ends(own_pack[2, group, t], s, lane)
            sums[1, layer, t] = density_in[layer, at(t), :] + RHO_SCALE * rho
        for e in range(3):
            stiff = from_core[24 + e, at(t), :] * LAP_SCALE
            for g in range(2):
                lap = part[g, near + e, t] + at_ends(own_pack[g, groups, t], e, lane)
                past = from_core[18 + 3 * g + e, at(t), :]
                first[g, near + e, t] = 2.0 * wide[g, near + 3 + e, t] - past + stiff * lap
        return carry

    lax.fori_loop(0, tiles, first_at, 0, unroll=2)

    for t in inside:
        terms = radial(lambda f, k: first[f, 3 + k, t], lambda k: wide[2, 6 + k, t], layers)
        for k, term in enumerate(terms):
            for g in range(3):
                part_last[g, k, t - 1] = term[g]

    def last(layer, carry):
        here = [[first[f, layer + 3, t] for t in range(tiles)] for f in range(2)]
        here.append([wide[2, layer + 6, t] for t in range(tiles)])
        flux = [lat_flux(here, t, sub) for t in range(tiles)]
        for k in range(3):
            for n, t in enumerate((1, tiles - 2)):
                flux_out[k, n, layer] = flux[t][k]
        for t in inside:
            lat = lat_terms(flux, t, sub, True)
            there = [first_halo[0, layer, t], first_halo[1, layer, t], buoy_halo[layer, t]]
            laps, rho = longitudinal([x[t] for x in here], there, lane, False, True)
            stiff = fields[5][layer, at(t), :] * LAP_SCALE
            for g in range(2):
                update = stiff * (part_last[g, layer, t - 1] + lat[g] + laps[0][g])
                done[2 * g, layer, at(t - 1), :] = (
                    2.0 * here[g][t] - fields[g][layer, at(t), :] + update
                )
                done[2 * g + 1, layer, at(t - 1), :] = here[g][t]
            done[4, layer, at(t - 1), :] = sums[0, layer, t] + here[0][t] * update
            done[5, layer, at(t - 1), :] = sums[1, layer, t] + RHO_SCALE * (
                part_last[2, layer, t - 1] + lat[2] + rho
            )
        return carry

    lax.fori_loop(0, layers, last, 0, unroll=4)


def last_kernel(*refs):
    fields, from_core = refs[:6], refs[6]
    wide, first, first_pack, stiff_pack, buoy_halo, flux_in, sums, done = refs[7:15]
    edges, from_first, from_second, from_third = refs[15:19]
    outs = refs[19:25]
    fixed, fixed_halo, ring_buoy, part, made, sems = refs[25:]
    layers, rows, lanes = fields[0].shape
    tiles = rows // SUB
    sub, lane = iotas(lanes)
    core = lax.axis_index("rad")
    place, count = lax.axis_index("lat"), lax.axis_size("lat")
    even = place % 2 == 0
    near, border = places(core, layers)
    zero = jnp.zeros((SUB, lanes), F32)
    ends = ((0, sub < 3), (tiles - 1, sub >= SUB - 3))
    copies = [
        pltpu.make_async_copy(done.at[k], out.at[:, pl.ds(SUB, rows - 2 * SUB), :], sems.at[k, 0])
        for k, out in enumerate(outs)
    ]
    for copy in copies:
        copy.start()

    def at(t):
        return pl.ds(t * SUB, SUB)

    def received(k):
        one = jnp.where(place % 4 < 2, from_first[k], from_third[k])
        two = from_second[k]
        behind, ahead = jnp.where(even, two, one), jnp.where(even, one, two)
        return jnp.where(place > 0, behind, 0.0), jnp.where(place < count - 1, ahead, 0.0)

    def join(behind, ahead):
        return jnp.where(sub < 4, ahead, behind)

    def three(k):
        behind, ahead = received(k)
        return list(zip(unpack_three(behind, False), unpack_three(ahead, True)))

    def outer(own, halos):
        low = [jnp.where(sub < 4, x[0], h[0]) for x, h in zip(own, halos)]
        high = [jnp.where(sub < 4, h[1], x[1]) for x, h in zip(own, halos)]
        return lat_outer(*low, sub), lat_outer(*high, sub)

    for g in range(2):
        for k in range(3):
            for n in range(2):
                fixed[g, border + k, n] = zero

    per = lanes // SEGMENT
    for group in range(stiff_pack.shape[0]):
        if group % 2 == 0:
            k = group // 2
            mine = list(zip(unpack_three(edges[0, k], True), unpack_three(edges[1, k], False)))
            side = outer(mine, three(2 * layers + 4 + k))
        for n, (t, mask) in enumerate(ends):
            for g in range(2):
                lap = jnp.where(mask, unmerged(side[n][g], group), 0.0)
                x = first_pack[g, group, t] + stiff_pack[group, t] * lap
                for s in range(min(per, layers - group * per)):
                    fixed_halo[g, group * per + s, n] = spread(x, s)

    for e in range(3):
        halos = three(2 * layers + 1 + e)
        mine = [(wide[f, near + 3 + e, 0], wide[f, near + 3 + e, tiles - 1]) for f in range(3)]
        side = outer(mine, halos)
        for n, (t, mask) in enumerate(ends):
            stiff = from_core[24 + e, at(t), :] * LAP_SCALE
            for g in range(2):
                lap = jnp.where(mask, side[n][g], 0.0)
                fixed[g, near + e, n] = first[g, near + e, t] + stiff * lap

    third = received(2 * layers)
    for layer in range(layers):
        halos = three(layers + layer)
        mine = [(x[layer, at(0), :], x[layer, at(tiles - 1), :]) for x in fields[:3]]
        side = outer(mine, halos)
        for n, (t, mask) in enumerate(ends):
            stiff = fields[5][layer, at(t), :] * LAP_SCALE
            for g in range(2):
                update = stiff * jnp.where(mask, side[n][g], 0.0)
                fixed[g, layer + 3, n] = first[g, layer + 3, t] + update
            made[4, layer, n] = sums[0, layer, t] + mine[0][n] * update
            made[5, layer, n] = sums[1, layer, t] + RHO_SCALE * jnp.where(mask, side[n][2], 0.0)
        adj, fwd, stiff = three(layer)
        low, high = (rolled(third[k], row - layer, 0) for k, row in enumerate((SUB - 3, 2)))
        stiff = jnp.where(
            sub < 4,
            jnp.where(sub == 2, high, stiff[1]),
            jnp.where(sub == SUB - 3, low, stiff[0]),
        )
        for g, x in enumerate((adj, fwd)):
            lap = join(side[0][g], side[1][g])
            fixed[g, layer + 3, 2] = join(*x) + stiff * LAP_SCALE * lap
        ring_buoy[layer] = join(*halos[2])

    for n, (t, _) in enumerate(ends):
        terms = radial(lambda f, k: fixed[f, 3 + k, n], lambda k: wide[2, 6 + k, t], layers)
        for k, term in enumerate(terms):
            for g in range(3):
                part[g, k, n] = term[g]

    def last(layer, carry):
        buoys = [wide[2, layer + 6, t] for t in (0, 1, tiles - 2, tiles - 1)]
        rings = [
            [fixed[f, layer + 3, 2], fixed[f, layer + 3, 0], first[f, layer + 3, 1]]
            + [first[f, layer + 3, tiles - 2], fixed[f, layer + 3, 1]]
            for f in range(2)
        ] + [[ring_buoy[layer], *buoys]]
        flux = [None] * 5
        for t in (0, 1, 4):
            flux[t] = lat_flux(rings, t, sub)
        for n in range(2):
            flux[2 + n] = [flux_in[k, n, layer] for k in range(3)]
        for n, (t, _) in enumerate(ends):
            k = (1, 4)[n]
            here = [x[k] for x in rings]
            lat = lat_terms(flux, k, sub, True)
            there = [fixed_halo[0, layer, n], fixed_halo[1, layer, n], buoy_halo[layer, t]]
            laps, rho = longitudinal(here, there, lane, False, True)
            stiff = fields[5][layer, at(t), :] * LAP_SCALE
            for g in range(2):
                update = stiff * (part[g, layer, n] + lat[g] + laps[0][g])
                made[2 * g, layer, n] = 2.0 * here[g] - fields[g][layer, at(t), :] + update
                made[2 * g + 1, layer, n] = here[g]
            made[4, layer, n] += here[0] * update
            made[5, layer, n] += RHO_SCALE * (part[2, layer, n] + lat[2] + rho)
        return carry

    lax.fori_loop(0, layers, last, 0, unroll=True)
    for k, out in enumerate(outs):
        for n, (t, _) in enumerate(ends):
            copy = pltpu.make_async_copy(made.at[k, :, n], out.at[:, at(t), :], sems.at[k, 1 + n])
            copy.start()
            copies.append(copy)
    for copy in copies:
        copy.wait()


def pairs(count, start, step):
    partner = {i: i for i in range(count)}
    for i in range(start, count - 1, step):
        partner[i], partner[i + 1] = i + 1, i
    return [
        (2 * i + core, 2 * j + (core if i != j else 1 - core))
        for i, j in partner.items()
        for core in range(2)
    ]


def call(kernel, out_shape, args, in_specs=None, out_specs=None, **more):
    return pl.pallas_call(
        kernel,
        out_shape=out_shape,
        in_specs=in_specs or [VMEM] * len(args),
        out_specs=out_specs or (VMEM,) * len(out_shape),
        compiler_params=PARAMS,
        **more,
    )(*args)


def shards(
    adj_now, adj_next, fwd_now, fwd_next, stiffness, buoyancy, kernel_bulk_in, kernel_density_in
):
    layers, rows, lanes = adj_now.shape
    tiles = rows // SUB
    fields = (adj_now, fwd_now, buoyancy, adj_next, fwd_next, stiffness)
    groups = -(-layers // (lanes // SEGMENT))
    around, count = lax.axis_size("lon"), lax.axis_size("lat")
    ring = [(i, (i + 1) % around) for i in range(around)]
    swap = [(0, 1), (1, 0)]

    def made(*shape):
        return pltpu.VMEM(shape, F32)

    block = (layers, rows, lanes)
    edge = made(groups, rows, lanes)
    hbm = pl.BlockSpec(memory_space=pltpu.HBM)
    *fields, to_right, to_left, to_core = call(
        edges_kernel,
        (made(*block),) * 6 + (edge, edge, made(sum(WIDTHS), rows, lanes)),
        [pltpu.with_memory_space_constraint(x, pltpu.HBM) for x in fields],
        in_specs=[hbm] * 6,
        scratch_shapes=[pltpu.SemaphoreType.DMA((6,))],
    )
    from_left = lax.ppermute(to_right, "lon", ring)
    from_right = lax.ppermute(to_left, "lon", [(b, a) for a, b in ring])
    from_core = lax.ppermute(to_core, "rad", swap)
    pairs_of_groups = -(-groups // 2)
    lat_edge = made(2 * layers + 4 + pairs_of_groups, SUB, lanes)
    packs = [from_left, from_right, to_left, to_right]
    wide, part, to_first, to_second, to_third = call(
        inner_kernel,
        (
            made(3, layers + 12, tiles, SUB, lanes),
            made(3, layers + 6, tiles, SUB, lanes),
            lat_edge,
            lat_edge,
            lat_edge,
        ),
        [*fields, from_core],
    )
    to_first, to_second, to_third, to_core, edges = call(
        turn_kernel,
        (lat_edge, lat_edge, lat_edge, made(4, rows, lanes), made(2, pairs_of_groups, SUB, lanes)),
        [*fields, *packs, part, to_first, to_second, to_third],
        input_output_aliases={11: 0, 12: 1, 13: 2},
    )
    from_first = lax.ppermute(to_first, ("lat", "rad"), pairs(count, 0, 4))
    from_second = lax.ppermute(to_second, ("lat", "rad"), pairs(count, 1, 2))
    from_third = lax.ppermute(to_third, ("lat", "rad"), pairs(count, 2, 4))
    from_core2 = lax.ppermute(to_core, "rad", swap)
    first, first_pack, stiff_pack, buoy_halo, flux, sums, done = call(
        middle_kernel,
        (
            made(2, layers + 6, tiles, SUB, lanes),
            made(2, groups, tiles, SUB, lanes),
            made(groups, tiles, SUB, lanes),
            made(layers, tiles, SUB, lanes),
            made(3, 2, layers, SUB, lanes),
            made(2, layers, tiles, SUB, lanes),
            made(6, layers, rows - 2 * SUB, lanes),
        ),
        [
            *fields,
            kernel_bulk_in,
            kernel_density_in,
            *packs,
            from_core,
            from_core2,
            wide,
            part,
        ],
        cost_estimate=HEAVY,
        scratch_shapes=[
            made(2, layers, tiles, SUB, lanes),
            made(3, groups + 1, tiles, SUB, lanes),
            made(3, layers, tiles - 2, SUB, lanes),
            made(3, groups, tiles, SUB, lanes),
            made(2, groups, tiles, SUB, lanes),
        ],
    )
    return call(
        last_kernel,
        (jax.ShapeDtypeStruct(block, F32),) * 6,
        [
            *fields,
            from_core,
            wide,
            first,
            first_pack,
            stiff_pack,
            buoy_halo,
            flux,
            sums,
            done,
            edges,
            from_first,
            from_second,
            from_third,
        ],
        out_specs=(hbm,) * 6,
        scratch_shapes=[
            made(2, layers + 6, 3, SUB, lanes),
            made(2, layers, 2, SUB, lanes),
            made(layers, SUB, lanes),
            made(3, layers, 2, SUB, lanes),
            made(6, layers, 2, SUB, lanes),
            pltpu.SemaphoreType.DMA((6, 3)),
        ],
    )


def solution(mesh):
    spec = P("rad", "lat", "lon")
    return jax.shard_map(
        shards, mesh=mesh, in_specs=(spec,) * 8, out_specs=(spec,) * 6, check_vma=False
    )
```

```python
import jax
import jax.numpy as jnp
from jax import lax
from jax.experimental import pallas as pl
from jax.experimental.pallas import tpu as pltpu
from jax.sharding import PartitionSpec as P

F32 = jnp.float32
SUB = 8
LAP_SCALE = 1.0 / 1152.0
RHO_SCALE = 1.0 / 2304.0
WIDTHS = (6, 6, 6, 3, 3, 3)
OFFSETS = (0, 6, 12, 21, 24, 27)
SEGMENT = 32
VMEM = pl.BlockSpec(memory_space=pltpu.VMEM)
PARAMS = pltpu.CompilerParams(vmem_limit_bytes=24 * 1024 * 1024)
HEAVY = pl.CostEstimate(flops=4000000000, bytes_accessed=1000000, transcendentals=0)


def iotas(lanes):
    return (
        lax.broadcasted_iota(jnp.int32, (SUB, lanes), 0),
        lax.broadcasted_iota(jnp.int32, (SUB, lanes), 1),
    )


def rolled(x, shift, axis):
    size = x.shape[axis]
    shift = shift % size
    return x if shift == 0 else pltpu.roll(x, shift, axis)


def lane_shift(here, there, by, lane):
    size = here.shape[1]
    if by > 0:
        return rolled(jnp.where(lane < by, there, here), size - by, 1)
    return rolled(jnp.where(lane >= size + by, there, here), -by, 1)


def row_shift(tiles, t, by, sub):
    if by > 0:
        return rolled(jnp.where(sub < by, tiles[(t + 1) % len(tiles)], tiles[t]), SUB - by, 0)
    return rolled(jnp.where(sub >= SUB + by, tiles[t - 1], tiles[t]), -by, 0)


def slope(ahead, here, ahead2, behind):
    return 27.0 * (ahead - here) - (ahead2 - behind)


def pack_three(a, b, c, low, sub):
    if low:
        return jnp.where(sub < 3, a, jnp.where(sub < 6, rolled(b, 3, 0), rolled(c, 6, 0)))
    return jnp.where(sub >= 5, a, jnp.where(sub >= 2, rolled(b, -3, 0), rolled(c, -6, 0)))


def unpack_three(x, low):
    sign = -1 if low else 1
    return x, rolled(x, 3 * sign, 0), rolled(x, 6 * sign, 0)


def edges_kernel(*refs):
    sources, fields, (to_right, to_left, to_core), sems = refs[:6], refs[6:12], refs[12:15], refs[15]
    copies = [pltpu.make_async_copy(x, y, sems.at[k]) for k, (x, y) in enumerate(zip(sources, fields))]
    for copy in copies:
        copy.start()
    layers, rows, lanes = fields[0].shape
    _, lane = iotas(lanes)
    core = lax.axis_index("rad")
    per = lanes // SEGMENT
    row = 0
    packed = {}
    for f, (width, offset) in enumerate(zip(WIDTHS, OFFSETS)):
        copies[f].wait()
        for layer in range(layers):
            group, s = divmod(layer, per)
            first = s * SEGMENT + offset
            second = first + width
            mask = lane >= second
            if second + width > lanes:
                mask = mask | (lane < second + width - lanes)
            mine = (lane >= first) & (lane < second)
            theirs = mask & (lane < second + width) if second + width <= lanes else mask
            for t in range(rows // SUB):
                x = rolled(fields[f][layer, pl.ds(t * SUB, SUB), :], second, 1)
                right, left = packed.get((group, t), (x, x))
                packed[group, t] = jnp.where(mine, x, right), jnp.where(theirs, x, left)
        to_core[row : row + width] = fields[f][pl.ds((layers - width) * (1 - core), width)]
        row += width
    for (group, t), (right, left) in packed.items():
        to_right[group, pl.ds(t * SUB, SUB), :] = right
        to_left[group, pl.ds(t * SUB, SUB), :] = left


def radial(p_at, b_at, layers):
    flux, rho = [], []
    p = [[p_at(f, k) for k in range(-3, layers + 3)] for f in range(2)]
    b = [b_at(k) for k in range(-2, layers + 2)]
    for k in range(layers + 3):
        buoy = b[k] + b[k + 1]
        grads = [slope(x[k + 2], x[k + 1], x[k + 3], x[k]) for x in p]
        flux.append([buoy * g for g in grads])
        rho.append(flux[k][0] * grads[1])
    out = []
    for k in range(layers):
        laps = [slope(flux[k + 2][f], flux[k + 1][f], flux[k + 3][f], flux[k][f]) for f in range(2)]
        out.append((laps[0], laps[1], rho[k + 1] + rho[k + 2]))
    return out


def longitudinal(here, there, lane, want_there, want_rho):
    flux, rho = [], []
    for x, y in ((here, there), (there, here)):
        buoy = x[2] + lane_shift(x[2], y[2], 1, lane)
        grads = [
            slope(
                lane_shift(x[f], y[f], 1, lane),
                x[f],
                lane_shift(x[f], y[f], 2, lane),
                lane_shift(x[f], y[f], -1, lane),
            )
            for f in range(2)
        ]
        flux.append([buoy * g for g in grads])
        rho.append(flux[-1][0] * grads[1])
    laps = []
    for x, y in ((0, 1), (1, 0))[: 2 if want_there else 1]:
        laps.append(
            [
                slope(
                    flux[x][f],
                    lane_shift(flux[x][f], flux[y][f], -1, lane),
                    lane_shift(flux[x][f], flux[y][f], 1, lane),
                    lane_shift(flux[x][f], flux[y][f], -2, lane),
                )
                for f in range(2)
            ]
        )
    density = rho[0] + lane_shift(rho[0], rho[1], -1, lane) if want_rho else None
    return laps, density


def windows(from_left, from_right, to_left, to_right, f, seg):
    offset = OFFSETS[f]
    mask = (seg >= offset) & (seg < offset + WIDTHS[f])
    return jnp.where(mask, from_left, to_left), jnp.where(mask, to_right, from_right)


def lon_flux(fields, offsets):
    def shift(f, by):
        return rolled(fields[f], -offsets[f] - by, 1)

    face = shift(2, 0) + shift(2, 1)
    grads = [slope(shift(f, 1), shift(f, 0), shift(f, 2), shift(f, -1)) for f in range(2)]
    flux = [face * g for g in grads]
    return flux[0], flux[1], flux[0] * grads[1]


def lon_terms(fields, want_rho, offsets=(0, 0, 0)):
    flux = lon_flux(fields, offsets)
    terms = [slope(x, rolled(x, 1, 1), rolled(x, -1, 1), rolled(x, 2, 1)) for x in flux[:2]]
    return terms + [flux[2] + rolled(flux[2], 1, 1)] if want_rho else terms


def edge_terms(wins, seg, want_rho, offsets):
    left = lon_terms([x[0] for x in wins], want_rho, offsets)
    right = lon_terms([x[1] for x in wins], want_rho, offsets)
    valid = (seg >= 3) & (seg < 9)
    own = [jnp.where(valid, jnp.where(seg < 6, y, x), 0.0) for x, y in zip(left, right)]
    return own, [jnp.where(seg < 6, x, y) for x, y in zip(left[:2], right[:2])]


def halos_of(wins, seg):
    return [jnp.where(seg < 6, x, y) for x, y in wins]


def aligned(wins):
    return [tuple(rolled(x, -offset, 1) for x in win) for win, offset in zip(wins, OFFSETS)]


def spread(x, s):
    return rolled(x, -s * SEGMENT - 6, 1)


def at_ends(x, s, lane):
    return jnp.where((lane < 3) | (lane >= x.shape[1] - 3), spread(x, s), 0.0)


def merged(tiles, seg):
    half = SEGMENT // 2
    out = []
    for k in range(0, len(tiles), 2):
        x = tiles[k]
        if k + 1 < len(tiles):
            x = jnp.where(seg < half, x, rolled(tiles[k + 1], half, 1))
        out.append(x)
    return out


def unmerged(x, group):
    return rolled(x, -(SEGMENT // 2) * (group % 2), 1)


def packed_radial(groups, lane):
    size = lane.shape[1]

    def shift(x, i, by):
        step = by * SEGMENT
        if by > 0:
            return rolled(jnp.where(lane < step, x[min(i + 1, len(x) - 1)], x[i]), -step, 1)
        return rolled(jnp.where(lane >= size + step, x[max(i - 1, 0)], x[i]), -step, 1)

    adj, fwd, buoy = ([x[f] for x in groups] for f in range(3))
    flux = ([], [])
    for i in range(len(groups)):
        face = buoy[i] + shift(buoy, i, 1)
        for f, x in enumerate((adj, fwd)):
            flux[f].append(face * slope(shift(x, i, 1), x[i], shift(x, i, 2), shift(x, i, -1)))
    return [
        [slope(x[i], shift(x, i, -1), shift(x, i, 1), shift(x, i, -2)) for x in flux]
        for i in range(1, len(groups) - 1)
    ]


def lat_flux(ring, t, sub):
    adj, fwd, buoy = ring
    face = buoy[t] + row_shift(buoy, t, 1, sub)
    grads = [
        slope(row_shift(x, t, 1, sub), x[t], row_shift(x, t, 2, sub), row_shift(x, t, -1, sub))
        for x in (adj, fwd)
    ]
    flux = [face * g for g in grads]
    return flux[0], flux[1], flux[0] * grads[1]


def lat_terms(flux, t, sub, want_rho):
    adj, fwd, rho = ([x[k] for x in flux] for k in range(3))
    laps = [
        slope(x[t], row_shift(x, t, -1, sub), row_shift(x, t, 1, sub), row_shift(x, t, -2, sub))
        for x in (adj, fwd)
    ]
    return laps[0], laps[1], rho[t] + row_shift(rho, t, -1, sub) if want_rho else None


def lat_inner(ring, sub, want_rho):
    count = len(ring[0])
    flux = [list(lat_flux(ring, t, sub)) for t in range(count)]
    zero = jnp.zeros_like(ring[0][0])
    for k in range(3):
        flux[0][k] = jnp.where(sub >= 1, flux[0][k], zero)
        flux[-1][k] = jnp.where(sub < SUB - 2, flux[-1][k], zero)
    flux.append([zero] * 3)
    return [lat_terms(flux, t, sub, want_rho) for t in range(count)]


def lat_outer(adj, fwd, buoy, sub):
    ring = ([adj], [fwd], [buoy])
    mask = (sub >= SUB - 2) | (sub < 1)
    flux = [[jnp.where(mask, x, 0.0) for x in lat_flux(ring, 0, sub)]]
    return lat_terms(flux, 0, sub, True)


def places(core, layers):
    return (layers + 3) * (1 - core), (layers + 3) * core


def inner_kernel(*refs):
    fields, from_core = refs[:6], refs[6]
    wide, part, to_first, to_second, to_third = refs[7:]
    layers, rows, lanes = fields[0].shape
    tiles = rows // SUB
    sub, lane = iotas(lanes)
    core = lax.axis_index("rad")
    even = lax.axis_index("lat") % 2 == 0
    near, border = places(core, layers)
    zero = jnp.zeros((SUB, lanes), F32)
    away = (lane >= 3) & (lane < lanes - 3)

    def at(t):
        return pl.ds(t * SUB, SUB)

    for f in range(3):
        for t in range(tiles):
            for layer in range(layers):
                wide[f, layer + 6, t] = fields[f][layer, at(t), :]
            for k in range(6):
                wide[f, (layers + 6) * (1 - core) + k, t] = from_core[6 * f + k, at(t), :]
            for k in range(3):
                wide[f, border + 3 + k, t] = zero

    def send(k, low, high):
        to_first[k] = to_third[k] = jnp.where(even, high, low)
        to_second[k] = jnp.where(even, low, high)

    ends = ((0, True), (tiles - 1, False))
    third = [None, None]
    for layer in range(layers):
        send(
            layers + layer,
            *(pack_three(*(x[layer, at(t), :] for x in fields[:3]), low, sub) for t, low in ends),
        )
        for k, row in enumerate((2, SUB - 3)):
            x = rolled(fields[5][layer, at(ends[k][0]), :], layer - row, 0)
            third[k] = x if layer == 0 else jnp.where(sub == layer, x, third[k])
    send(2 * layers, *third)
    for e in range(3):
        send(
            2 * layers + 1 + e,
            *(pack_three(*(wide[f, near + 3 + e, t] for f in range(3)), low, sub) for t, low in ends),
        )

    start = 6 - 3 * core
    for t in range(tiles):
        terms = radial(
            lambda f, k: wide[f, start + k, t], lambda k: wide[2, start + k, t], layers + 3
        )
        for k, term in enumerate(terms):
            for g in range(3):
                part[g, start - 3 + k, t] = term[g]

    def own(layer, carry):
        here = [[wide[f, layer + 6, t] for t in range(tiles)] for f in range(3)]
        terms = lat_inner(here, sub, True)
        for t in range(tiles):
            lon = lon_terms([x[t] for x in here], True)
            for g in range(3):
                part[g, layer + 3, t] += terms[t][g] + jnp.where(away, lon[g], 0.0)
        return carry

    lax.fori_loop(0, layers, own, 0, unroll=2)

    def other(e, carry):
        here = [[wide[f, near + 3 + e, t] for t in range(tiles)] for f in range(3)]
        terms = lat_inner(here, sub, False)
        for t in range(tiles):
            lon = lon_terms([x[t] for x in here], False)
            for g in range(2):
                part[g, near + e, t] += terms[t][g] + jnp.where(away, lon[g], 0.0)
        return carry

    lax.fori_loop(0, 3, other, 0, unroll=True)


def turn_kernel(*refs):
    fields, packs, part = refs[:6], refs[6:10], refs[10]
    to_first, to_second, to_third, to_core, edges = refs[14:]
    layers, rows, lanes = fields[0].shape
    tiles = rows // SUB
    sub, lane = iotas(lanes)
    seg = lane % SEGMENT
    core = lax.axis_index("rad")
    even = lax.axis_index("lat") % 2 == 0
    per = lanes // SEGMENT
    groups = packs[0].shape[0]

    def send(k, low, high):
        to_first[k] = to_third[k] = jnp.where(even, high, low)
        to_second[k] = jnp.where(even, low, high)

    def ends(ref, *index):
        low, high = (ref[(*index, pl.ds(t * SUB, SUB), slice(None))] for t in (0, tiles - 1))
        return jnp.where(sub < 4, low, high)

    for k, ref in enumerate(packs):
        to_core[k] = ref[(groups - 1) * (1 - core)]
    halos = []
    for g in range(groups):
        pack = [ends(x, g) for x in packs]
        wins = [windows(*pack, f, seg) for f in range(3)]
        laps, _ = edge_terms(wins, seg, False, OFFSETS)
        halos.append(halos_of(aligned(wins), seg))
        for s in range(min(per, layers - g * per)):
            layer = g * per + s
            here = [ends(x, layer) for x in fields]
            stiff = here[5] * LAP_SCALE
            made = []
            for f in range(2):
                before = jnp.where(sub < 4, part[f, layer + 3, 0], part[f, layer + 3, tiles - 1])
                lap = before + at_ends(laps[f], s, lane)
                made.append(2.0 * here[f] - here[3 + f] + stiff * lap)
            send(layer, *(pack_three(*made, here[5], low, sub) for low in (True, False)))
    both = [merged([pack_three(*x, low, sub) for x in halos], seg) for low in (True, False)]
    for k, (low, high) in enumerate(zip(*both)):
        send(2 * layers + 4 + k, low, high)
        edges[0, k] = low
        edges[1, k] = high


def middle_kernel(*refs):
    fields, (bulk_in, density_in) = refs[:6], refs[6:8]
    packs, from_core, from_core2, wide, part = refs[8:12], refs[12], refs[13], refs[14], refs[15]
    first, first_pack, stiff_pack, buoy_halo, flux_out, sums, done = refs[16:23]
    first_halo, own_pack, part_last, halo_pack, lap_pack = refs[23:]
    layers, rows, lanes = fields[0].shape
    tiles = rows // SUB
    sub, lane = iotas(lanes)
    seg = lane % SEGMENT
    core = lax.axis_index("rad")
    near, border = places(core, layers)
    per = lanes // SEGMENT
    groups = packs[0].shape[0]
    zero = jnp.zeros((SUB, lanes), F32)
    inside = range(1, tiles - 1)

    def at(t):
        return pl.ds(pl.multiple_of(t * SUB, SUB), SUB)

    def edges_at(t, carry):
        sources = [[x[group, at(t), :] for x in packs] for group in range(groups)]
        sources.append([from_core2[k, at(t), :] for k in range(4)])
        wins = [aligned([windows(*x, f, seg) for f in range(3)]) for x in sources]
        halos = [halos_of(x, seg) for x in wins]
        before = [jnp.where(core == 0, 0.0, x) for x in halos[-1]]
        after = [jnp.where(core == 0, x, 0.0) for x in halos[-1]]
        radials = packed_radial([before, *halos[:-1], after], lane)
        terms = [edge_terms(x, seg, True, (0, 0, 0)) for x in wins[:-1]]
        own = [x for x, _ in terms]
        for group in range(groups):
            for f, x in enumerate(halos[group]):
                halo_pack[f, group, t] = x
            for g in range(2):
                lap_pack[g, group, t] = terms[group][1][g] + radials[group][g]
        for group in range(groups):
            for g, x in enumerate(own[group]):
                own_pack[g, group, t] = x
        return carry

    def other_at(t, carry):
        other = [from_core2[k, at(t), :] for k in range(4)]
        wins = aligned([windows(*other, f, seg) for f in range(3)])
        own, _ = edge_terms(wins, seg, False, (0, 0, 0))
        for g in range(2):
            own_pack[g, groups, t] = jnp.where(core == 0, own[g], rolled(own[g], -(per - 3) * SEGMENT, 1))
        return carry

    lax.fori_loop(0, tiles, edges_at, 0, unroll=2)
    lax.fori_loop(0, tiles, other_at, 0, unroll=True)
    for group in range(groups):
        halo = [[halo_pack[f, group, t] for t in range(tiles)] for f in range(3)]
        lat = lat_inner(halo, sub, False)
        for t in range(tiles):
            rest = []
            for f in range(3, 6):
                offset = OFFSETS[f]
                mask = (seg >= offset) & (seg < offset + WIDTHS[f])
                x = jnp.where(mask, packs[0][group, at(t), :], packs[1][group, at(t), :])
                rest.append(rolled(x, 3 - offset, 1))
            stiff = rest[2] * LAP_SCALE
            stiff_pack[group, t] = stiff
            for g in range(2):
                lap = lap_pack[g, group, t] + lat[t][g]
                first_pack[g, group, t] = 2.0 * halo[g][t] - rest[g] + stiff * lap
    for g in range(2):
        for k in range(3):
            for t in range(tiles):
                first[g, border + k, t] = zero

    def first_at(t, carry):
        for layer in range(layers):
            group, s = divmod(layer, per)
            buoy_halo[layer, t] = spread(halo_pack[2, group, t], s)
            stiff = fields[5][layer, at(t), :] * LAP_SCALE
            here = [wide[f, layer + 6, t] for f in range(2)]
            for g in range(2):
                first_halo[g, layer, t] = spread(first_pack[g, group, t], s)
                lap = part[g, layer + 3, t] + at_ends(own_pack[g, group, t], s, lane)
                update = stiff * lap
                first[g, layer + 3, t] = 2.0 * here[g] - fields[3 + g][layer, at(t), :] + update
            sums[0, layer, t] = bulk_in[layer, at(t), :] + here[0] * update
            rho = part[2, layer + 3, t] + at_ends(own_pack[2, group, t], s, lane)
            sums[1, layer, t] = density_in[layer, at(t), :] + RHO_SCALE * rho
        for e in range(3):
            stiff = from_core[24 + e, at(t), :] * LAP_SCALE
            for g in range(2):
                lap = part[g, near + e, t] + at_ends(own_pack[g, groups, t], e, lane)
                past = from_core[18 + 3 * g + e, at(t), :]
                first[g, near + e, t] = 2.0 * wide[g, near + 3 + e, t] - past + stiff * lap
        return carry

    lax.fori_loop(0, tiles, first_at, 0, unroll=2)

    for t in inside:
        terms = radial(lambda f, k: first[f, 3 + k, t], lambda k: wide[2, 6 + k, t], layers)
        for k, term in enumerate(terms):
            for g in range(3):
                part_last[g, k, t - 1] = term[g]

    def last(layer, carry):
        here = [[first[f, layer + 3, t] for t in range(tiles)] for f in range(2)]
        here.append([wide[2, layer + 6, t] for t in range(tiles)])
        flux = [lat_flux(here, t, sub) for t in range(tiles)]
        for k in range(3):
            for n, t in enumerate((1, tiles - 2)):
                flux_out[k, n, layer] = flux[t][k]
        for t in inside:
            lat = lat_terms(flux, t, sub, True)
            there = [first_halo[0, layer, t], first_halo[1, layer, t], buoy_halo[layer, t]]
            laps, rho = longitudinal([x[t] for x in here], there, lane, False, True)
            stiff = fields[5][layer, at(t), :] * LAP_SCALE
            for g in range(2):
                update = stiff * (part_last[g, layer, t - 1] + lat[g] + laps[0][g])
                done[2 * g, layer, at(t - 1), :] = (
                    2.0 * here[g][t] - fields[g][layer, at(t), :] + update
                )
                done[2 * g + 1, layer, at(t - 1), :] = here[g][t]
            done[4, layer, at(t - 1), :] = sums[0, layer, t] + here[0][t] * update
            done[5, layer, at(t - 1), :] = sums[1, layer, t] + RHO_SCALE * (
                part_last[2, layer, t - 1] + lat[2] + rho
            )
        return carry

    lax.fori_loop(0, layers, last, 0, unroll=4)


def last_kernel(*refs):
    fields, from_core = refs[:6], refs[6]
    wide, first, first_pack, stiff_pack, buoy_halo, flux_in, sums, done = refs[7:15]
    edges, from_first, from_second, from_third = refs[15:19]
    outs = refs[19:25]
    fixed, fixed_halo, ring_buoy, part, made, sems = refs[25:]
    layers, rows, lanes = fields[0].shape
    tiles = rows // SUB
    sub, lane = iotas(lanes)
    core = lax.axis_index("rad")
    place, count = lax.axis_index("lat"), lax.axis_size("lat")
    even = place % 2 == 0
    near, border = places(core, layers)
    zero = jnp.zeros((SUB, lanes), F32)
    ends = ((0, sub < 3), (tiles - 1, sub >= SUB - 3))
    copies = [
        pltpu.make_async_copy(done.at[k], out.at[:, pl.ds(SUB, rows - 2 * SUB), :], sems.at[k, 0])
        for k, out in enumerate(outs)
    ]
    for copy in copies:
        copy.start()

    def at(t):
        return pl.ds(t * SUB, SUB)

    def received(k):
        one = jnp.where(place % 4 < 2, from_first[k], from_third[k])
        two = from_second[k]
        behind, ahead = jnp.where(even, two, one), jnp.where(even, one, two)
        return jnp.where(place > 0, behind, 0.0), jnp.where(place < count - 1, ahead, 0.0)

    def join(behind, ahead):
        return jnp.where(sub < 4, ahead, behind)

    def three(k):
        behind, ahead = received(k)
        return list(zip(unpack_three(behind, False), unpack_three(ahead, True)))

    def outer(own, halos):
        low = [jnp.where(sub < 4, x[0], h[0]) for x, h in zip(own, halos)]
        high = [jnp.where(sub < 4, h[1], x[1]) for x, h in zip(own, halos)]
        return lat_outer(*low, sub), lat_outer(*high, sub)

    for g in range(2):
        for k in range(3):
            for n in range(2):
                fixed[g, border + k, n] = zero

    per = lanes // SEGMENT
    for group in range(stiff_pack.shape[0]):
        if group % 2 == 0:
            k = group // 2
            mine = list(zip(unpack_three(edges[0, k], True), unpack_three(edges[1, k], False)))
            side = outer(mine, three(2 * layers + 4 + k))
        for n, (t, mask) in enumerate(ends):
            for g in range(2):
                lap = jnp.where(mask, unmerged(side[n][g], group), 0.0)
                x = first_pack[g, group, t] + stiff_pack[group, t] * lap
                for s in range(min(per, layers - group * per)):
                    fixed_halo[g, group * per + s, n] = spread(x, s)

    for e in range(3):
        halos = three(2 * layers + 1 + e)
        mine = [(wide[f, near + 3 + e, 0], wide[f, near + 3 + e, tiles - 1]) for f in range(3)]
        side = outer(mine, halos)
        for n, (t, mask) in enumerate(ends):
            stiff = from_core[24 + e, at(t), :] * LAP_SCALE
            for g in range(2):
                lap = jnp.where(mask, side[n][g], 0.0)
                fixed[g, near + e, n] = first[g, near + e, t] + stiff * lap

    third = received(2 * layers)
    for layer in range(layers):
        halos = three(layers + layer)
        mine = [(x[layer, at(0), :], x[layer, at(tiles - 1), :]) for x in fields[:3]]
        side = outer(mine, halos)
        for n, (t, mask) in enumerate(ends):
            stiff = fields[5][layer, at(t), :] * LAP_SCALE
            for g in range(2):
                update = stiff * jnp.where(mask, side[n][g], 0.0)
                fixed[g, layer + 3, n] = first[g, layer + 3, t] + update
            made[4, layer, n] = sums[0, layer, t] + mine[0][n] * update
            made[5, layer, n] = sums[1, layer, t] + RHO_SCALE * jnp.where(mask, side[n][2], 0.0)
        adj, fwd, stiff = three(layer)
        low, high = (rolled(third[k], row - layer, 0) for k, row in enumerate((SUB - 3, 2)))
        stiff = jnp.where(
            sub < 4,
            jnp.where(sub == 2, high, stiff[1]),
            jnp.where(sub == SUB - 3, low, stiff[0]),
        )
        for g, x in enumerate((adj, fwd)):
            lap = join(side[0][g], side[1][g])
            fixed[g, layer + 3, 2] = join(*x) + stiff * LAP_SCALE * lap
        ring_buoy[layer] = join(*halos[2])

    for n, (t, _) in enumerate(ends):
        terms = radial(lambda f, k: fixed[f, 3 + k, n], lambda k: wide[2, 6 + k, t], layers)
        for k, term in enumerate(terms):
            for g in range(3):
                part[g, k, n] = term[g]

    def last(layer, n):
        t = ends[n][0]
        rings = [[fixed[f, layer + 3, 2], fixed[f, layer + 3, n]] for f in range(2)]
        rings.append([ring_buoy[layer], wide[2, layer + 6, t]])
        beside = [first[f, layer + 3, (1, tiles - 2)[n]] for f in range(2)]
        beside.append(wide[2, layer + 6, (1, tiles - 2)[n]])
        rings = [[x[0], x[1], y] if n == 0 else [y, x[1], x[0]] for x, y in zip(rings, beside)]
        flux = [None] * 3
        flux[1] = lat_flux(rings, 1, sub)
        flux[2 * n] = lat_flux(rings, 2 * n, sub)
        flux[2 - 2 * n] = [flux_in[k, n, layer] for k in range(3)]
        here = [x[1] for x in rings]
        lat = lat_terms(flux, 1, sub, True)
        there = [fixed_halo[0, layer, n], fixed_halo[1, layer, n], buoy_halo[layer, t]]
        laps, rho = longitudinal(here, there, lane, False, True)
        stiff = fields[5][layer, at(t), :] * LAP_SCALE
        for g in range(2):
            update = stiff * (part[g, layer, n] + lat[g] + laps[0][g])
            made[2 * g, layer, n] = 2.0 * here[g] - fields[g][layer, at(t), :] + update
            made[2 * g + 1, layer, n] = here[g]
        made[4, layer, n] += here[0] * update
        made[5, layer, n] += RHO_SCALE * (part[2, layer, n] + lat[2] + rho)

    for n, (t, _) in enumerate(ends):
        for layer in range(layers):
            last(layer, n)
        for k, out in enumerate(outs):
            copy = pltpu.make_async_copy(made.at[k, :, n], out.at[:, at(t), :], sems.at[k, 1 + n])
            copy.start()
            copies.append(copy)
    for copy in copies:
        copy.wait()


def pairs(count, start, step):
    partner = {i: i for i in range(count)}
    for i in range(start, count - 1, step):
        partner[i], partner[i + 1] = i + 1, i
    return [
        (2 * i + core, 2 * j + (core if i != j else 1 - core))
        for i, j in partner.items()
        for core in range(2)
    ]


def call(kernel, out_shape, args, in_specs=None, out_specs=None, **more):
    return pl.pallas_call(
        kernel,
        out_shape=out_shape,
        in_specs=in_specs or [VMEM] * len(args),
        out_specs=out_specs or (VMEM,) * len(out_shape),
        compiler_params=PARAMS,
        **more,
    )(*args)


def shards(
    adj_now, adj_next, fwd_now, fwd_next, stiffness, buoyancy, kernel_bulk_in, kernel_density_in
):
    layers, rows, lanes = adj_now.shape
    tiles = rows // SUB
    fields = (adj_now, fwd_now, buoyancy, adj_next, fwd_next, stiffness)
    groups = -(-layers // (lanes // SEGMENT))
    around, count = lax.axis_size("lon"), lax.axis_size("lat")
    ring = [(i, (i + 1) % around) for i in range(around)]
    swap = [(0, 1), (1, 0)]

    def made(*shape):
        return pltpu.VMEM(shape, F32)

    block = (layers, rows, lanes)
    edge = made(groups, rows, lanes)
    hbm = pl.BlockSpec(memory_space=pltpu.HBM)
    *fields, to_right, to_left, to_core = call(
        edges_kernel,
        (made(*block),) * 6 + (edge, edge, made(sum(WIDTHS), rows, lanes)),
        [pltpu.with_memory_space_constraint(x, pltpu.HBM) for x in fields],
        in_specs=[hbm] * 6,
        scratch_shapes=[pltpu.SemaphoreType.DMA((6,))],
    )
    from_left = lax.ppermute(to_right, "lon", ring)
    from_right = lax.ppermute(to_left, "lon", [(b, a) for a, b in ring])
    from_core = lax.ppermute(to_core, "rad", swap)
    pairs_of_groups = -(-groups // 2)
    lat_edge = made(2 * layers + 4 + pairs_of_groups, SUB, lanes)
    packs = [from_left, from_right, to_left, to_right]
    wide, part, to_first, to_second, to_third = call(
        inner_kernel,
        (
            made(3, layers + 12, tiles, SUB, lanes),
            made(3, layers + 6, tiles, SUB, lanes),
            lat_edge,
            lat_edge,
            lat_edge,
        ),
        [*fields, from_core],
    )
    to_first, to_second, to_third, to_core, edges = call(
        turn_kernel,
        (lat_edge, lat_edge, lat_edge, made(4, rows, lanes), made(2, pairs_of_groups, SUB, lanes)),
        [*fields, *packs, part, to_first, to_second, to_third],
        input_output_aliases={11: 0, 12: 1, 13: 2},
    )
    from_first = lax.ppermute(to_first, ("lat", "rad"), pairs(count, 0, 4))
    from_second = lax.ppermute(to_second, ("lat", "rad"), pairs(count, 1, 2))
    from_third = lax.ppermute(to_third, ("lat", "rad"), pairs(count, 2, 4))
    from_core2 = lax.ppermute(to_core, "rad", swap)
    first, first_pack, stiff_pack, buoy_halo, flux, sums, done = call(
        middle_kernel,
        (
            made(2, layers + 6, tiles, SUB, lanes),
            made(2, groups, tiles, SUB, lanes),
            made(groups, tiles, SUB, lanes),
            made(layers, tiles, SUB, lanes),
            made(3, 2, layers, SUB, lanes),
            made(2, layers, tiles, SUB, lanes),
            made(6, layers, rows - 2 * SUB, lanes),
        ),
        [
            *fields,
            kernel_bulk_in,
            kernel_density_in,
            *packs,
            from_core,
            from_core2,
            wide,
            part,
        ],
        cost_estimate=HEAVY,
        scratch_shapes=[
            made(2, layers, tiles, SUB, lanes),
            made(3, groups + 1, tiles, SUB, lanes),
            made(3, layers, tiles - 2, SUB, lanes),
            made(3, groups, tiles, SUB, lanes),
            made(2, groups, tiles, SUB, lanes),
        ],
    )
    return call(
        last_kernel,
        (jax.ShapeDtypeStruct(block, F32),) * 6,
        [
            *fields,
            from_core,
            wide,
            first,
            first_pack,
            stiff_pack,
            buoy_halo,
            flux,
            sums,
            done,
            edges,
            from_first,
            from_second,
            from_third,
        ],
        out_specs=(hbm,) * 6,
        scratch_shapes=[
            made(2, layers + 6, 3, SUB, lanes),
            made(2, layers, 2, SUB, lanes),
            made(layers, SUB, lanes),
            made(3, layers, 2, SUB, lanes),
            made(6, layers, 2, SUB, lanes),
            pltpu.SemaphoreType.DMA((6, 3)),
        ],
    )


def solution(mesh):
    spec = P("rad", "lat", "lon")
    return jax.shard_map(
        shards, mesh=mesh, in_specs=(spec,) * 8, out_specs=(spec,) * 6, check_vma=False
    )
```

```python
import jax
import jax.numpy as jnp
from jax import lax
from jax.experimental import pallas as pl
from jax.experimental.pallas import tpu as pltpu
from jax.sharding import PartitionSpec as P

F32 = jnp.float32
SUB = 8
LAP_SCALE = 1.0 / 1152.0
RHO_SCALE = 1.0 / 2304.0
WIDTHS = (6, 6, 6, 3, 3, 3)
OFFSETS = (0, 6, 12, 21, 24, 27)
SEGMENT = 32
VMEM = pl.BlockSpec(memory_space=pltpu.VMEM)
PARAMS = pltpu.CompilerParams(vmem_limit_bytes=24 * 1024 * 1024)
HEAVY = pl.CostEstimate(flops=4000000000, bytes_accessed=1000000, transcendentals=0)


def iotas(lanes):
    return (
        lax.broadcasted_iota(jnp.int32, (SUB, lanes), 0),
        lax.broadcasted_iota(jnp.int32, (SUB, lanes), 1),
    )


def rolled(x, shift, axis):
    size = x.shape[axis]
    shift = shift % size
    return x if shift == 0 else pltpu.roll(x, shift, axis)


def lane_shift(here, there, by, lane):
    size = here.shape[1]
    if by > 0:
        return rolled(jnp.where(lane < by, there, here), size - by, 1)
    return rolled(jnp.where(lane >= size + by, there, here), -by, 1)


def row_shift(tiles, t, by, sub):
    if by > 0:
        return rolled(jnp.where(sub < by, tiles[(t + 1) % len(tiles)], tiles[t]), SUB - by, 0)
    return rolled(jnp.where(sub >= SUB + by, tiles[t - 1], tiles[t]), -by, 0)


def slope(ahead, here, ahead2, behind):
    return 27.0 * (ahead - here) - (ahead2 - behind)


def pack_three(a, b, c, low, sub):
    if low:
        return jnp.where(sub < 3, a, jnp.where(sub < 6, rolled(b, 3, 0), rolled(c, 6, 0)))
    return jnp.where(sub >= 5, a, jnp.where(sub >= 2, rolled(b, -3, 0), rolled(c, -6, 0)))


def unpack_three(x, low):
    sign = -1 if low else 1
    return x, rolled(x, 3 * sign, 0), rolled(x, 6 * sign, 0)


def edges_kernel(*refs):
    sources, fields, (to_right, to_left, to_core), sems = refs[:6], refs[6:12], refs[12:15], refs[15]
    copies = [pltpu.make_async_copy(x, y, sems.at[k]) for k, (x, y) in enumerate(zip(sources, fields))]
    for copy in copies:
        copy.start()
    layers, rows, lanes = fields[0].shape
    _, lane = iotas(lanes)
    core = lax.axis_index("rad")
    per = lanes // SEGMENT
    for copy in copies:
        copy.wait()
    for group in range(to_right.shape[0]):
        for t in range(rows // SUB):
            at = pl.ds(t * SUB, SUB)
            right = left = None
            for layer in range(group * per, min(layers, (group + 1) * per)):
                for f, (width, offset) in enumerate(zip(WIDTHS, OFFSETS)):
                    first = (layer - group * per) * SEGMENT + offset
                    second = first + width
                    x = rolled(fields[f][layer, at, :], second, 1)
                    mask = lane >= second
                    if second + width > lanes:
                        mask = mask | (lane < second + width - lanes)
                    right = x if right is None else jnp.where(lane >= first, x, right)
                    left = x if left is None else jnp.where(mask, x, left)
            to_right[group, at, :] = right
            to_left[group, at, :] = left
    row = 0
    for f, width in enumerate(WIDTHS):
        to_core[row : row + width] = fields[f][pl.ds((layers - width) * (1 - core), width)]
        row += width


def radial(p_at, b_at, layers):
    flux, rho = [], []
    p = [[p_at(f, k) for k in range(-3, layers + 3)] for f in range(2)]
    b = [b_at(k) for k in range(-2, layers + 2)]
    for k in range(layers + 3):
        buoy = b[k] + b[k + 1]
        grads = [slope(x[k + 2], x[k + 1], x[k + 3], x[k]) for x in p]
        flux.append([buoy * g for g in grads])
        rho.append(flux[k][0] * grads[1])
    out = []
    for k in range(layers):
        laps = [slope(flux[k + 2][f], flux[k + 1][f], flux[k + 3][f], flux[k][f]) for f in range(2)]
        out.append((laps[0], laps[1], rho[k + 1] + rho[k + 2]))
    return out


def longitudinal(here, there, lane, want_there, want_rho):
    flux, rho = [], []
    for x, y in ((here, there), (there, here)):
        buoy = x[2] + lane_shift(x[2], y[2], 1, lane)
        grads = [
            slope(
                lane_shift(x[f], y[f], 1, lane),
                x[f],
                lane_shift(x[f], y[f], 2, lane),
                lane_shift(x[f], y[f], -1, lane),
            )
            for f in range(2)
        ]
        flux.append([buoy * g for g in grads])
        rho.append(flux[-1][0] * grads[1])
    laps = []
    for x, y in ((0, 1), (1, 0))[: 2 if want_there else 1]:
        laps.append(
            [
                slope(
                    flux[x][f],
                    lane_shift(flux[x][f], flux[y][f], -1, lane),
                    lane_shift(flux[x][f], flux[y][f], 1, lane),
                    lane_shift(flux[x][f], flux[y][f], -2, lane),
                )
                for f in range(2)
            ]
        )
    density = rho[0] + lane_shift(rho[0], rho[1], -1, lane) if want_rho else None
    return laps, density


def windows(from_left, from_right, to_left, to_right, f, seg):
    offset = OFFSETS[f]
    mask = (seg >= offset) & (seg < offset + WIDTHS[f])
    return jnp.where(mask, from_left, to_left), jnp.where(mask, to_right, from_right)


def lon_flux(fields, offsets):
    def shift(f, by):
        return rolled(fields[f], -offsets[f] - by, 1)

    face = shift(2, 0) + shift(2, 1)
    grads = [slope(shift(f, 1), shift(f, 0), shift(f, 2), shift(f, -1)) for f in range(2)]
    flux = [face * g for g in grads]
    return flux[0], flux[1], flux[0] * grads[1]


def lon_terms(fields, want_rho, offsets=(0, 0, 0)):
    flux = lon_flux(fields, offsets)
    terms = [slope(x, rolled(x, 1, 1), rolled(x, -1, 1), rolled(x, 2, 1)) for x in flux[:2]]
    return terms + [flux[2] + rolled(flux[2], 1, 1)] if want_rho else terms


def edge_terms(wins, seg, want_rho, offsets):
    left = lon_terms([x[0] for x in wins], want_rho, offsets)
    right = lon_terms([x[1] for x in wins], want_rho, offsets)
    valid = (seg >= 3) & (seg < 9)
    own = [jnp.where(valid, jnp.where(seg < 6, y, x), 0.0) for x, y in zip(left, right)]
    return own, [jnp.where(seg < 6, x, y) for x, y in zip(left[:2], right[:2])]


def halos_of(wins, seg):
    return [jnp.where(seg < 6, x, y) for x, y in wins]


def aligned(wins):
    return [tuple(rolled(x, -offset, 1) for x in win) for win, offset in zip(wins, OFFSETS)]


def spread(x, s):
    return rolled(x, -s * SEGMENT - 6, 1)


def at_ends(x, s, lane):
    return jnp.where((lane < 3) | (lane >= x.shape[1] - 3), spread(x, s), 0.0)


def merged(tiles, seg):
    half = SEGMENT // 2
    out = []
    for k in range(0, len(tiles), 2):
        x = tiles[k]
        if k + 1 < len(tiles):
            x = jnp.where(seg < half, x, rolled(tiles[k + 1], half, 1))
        out.append(x)
    return out


def unmerged(x, group):
    return rolled(x, -(SEGMENT // 2) * (group % 2), 1)


def packed_radial(groups, lane):
    size = lane.shape[1]

    def shift(x, i, by):
        step = by * SEGMENT
        if by > 0:
            return rolled(jnp.where(lane < step, x[min(i + 1, len(x) - 1)], x[i]), -step, 1)
        return rolled(jnp.where(lane >= size + step, x[max(i - 1, 0)], x[i]), -step, 1)

    adj, fwd, buoy = ([x[f] for x in groups] for f in range(3))
    flux = ([], [])
    for i in range(len(groups)):
        face = buoy[i] + shift(buoy, i, 1)
        for f, x in enumerate((adj, fwd)):
            flux[f].append(face * slope(shift(x, i, 1), x[i], shift(x, i, 2), shift(x, i, -1)))
    return [
        [slope(x[i], shift(x, i, -1), shift(x, i, 1), shift(x, i, -2)) for x in flux]
        for i in range(1, len(groups) - 1)
    ]


def lat_flux(ring, t, sub):
    adj, fwd, buoy = ring
    face = buoy[t] + row_shift(buoy, t, 1, sub)
    grads = [
        slope(row_shift(x, t, 1, sub), x[t], row_shift(x, t, 2, sub), row_shift(x, t, -1, sub))
        for x in (adj, fwd)
    ]
    flux = [face * g for g in grads]
    return flux[0], flux[1], flux[0] * grads[1]


def lat_terms(flux, t, sub, want_rho):
    adj, fwd, rho = ([x[k] for x in flux] for k in range(3))
    laps = [
        slope(x[t], row_shift(x, t, -1, sub), row_shift(x, t, 1, sub), row_shift(x, t, -2, sub))
        for x in (adj, fwd)
    ]
    return laps[0], laps[1], rho[t] + row_shift(rho, t, -1, sub) if want_rho else None


def lat_inner(ring, sub, want_rho):
    count = len(ring[0])
    flux = [list(lat_flux(ring, t, sub)) for t in range(count)]
    zero = jnp.zeros_like(ring[0][0])
    for k in range(3):
        flux[0][k] = jnp.where(sub >= 1, flux[0][k], zero)
        flux[-1][k] = jnp.where(sub < SUB - 2, flux[-1][k], zero)
    flux.append([zero] * 3)
    return [lat_terms(flux, t, sub, want_rho) for t in range(count)]


def lat_outer(adj, fwd, buoy, sub):
    ring = ([adj], [fwd], [buoy])
    mask = (sub >= SUB - 2) | (sub < 1)
    flux = [[jnp.where(mask, x, 0.0) for x in lat_flux(ring, 0, sub)]]
    return lat_terms(flux, 0, sub, True)


def places(core, layers):
    return (layers + 3) * (1 - core), (layers + 3) * core


def inner_kernel(*refs):
    fields, from_core = refs[:6], refs[6]
    wide, part, to_first, to_second, to_third = refs[7:]
    layers, rows, lanes = fields[0].shape
    tiles = rows // SUB
    sub, lane = iotas(lanes)
    core = lax.axis_index("rad")
    even = lax.axis_index("lat") % 2 == 0
    near, border = places(core, layers)
    zero = jnp.zeros((SUB, lanes), F32)
    away = (lane >= 3) & (lane < lanes - 3)

    def at(t):
        return pl.ds(t * SUB, SUB)

    for f in range(3):
        for t in range(tiles):
            for layer in range(layers):
                wide[f, layer + 6, t] = fields[f][layer, at(t), :]
            for k in range(6):
                wide[f, (layers + 6) * (1 - core) + k, t] = from_core[6 * f + k, at(t), :]
            for k in range(3):
                wide[f, border + 3 + k, t] = zero

    def send(k, low, high):
        to_first[k] = to_third[k] = jnp.where(even, high, low)
        to_second[k] = jnp.where(even, low, high)

    ends = ((0, True), (tiles - 1, False))
    third = [None, None]
    for layer in range(layers):
        send(
            layers + layer,
            *(pack_three(*(x[layer, at(t), :] for x in fields[:3]), low, sub) for t, low in ends),
        )
        for k, row in enumerate((2, SUB - 3)):
            x = rolled(fields[5][layer, at(ends[k][0]), :], layer - row, 0)
            third[k] = x if layer == 0 else jnp.where(sub == layer, x, third[k])
    send(2 * layers, *third)
    for e in range(3):
        send(
            2 * layers + 1 + e,
            *(pack_three(*(wide[f, near + 3 + e, t] for f in range(3)), low, sub) for t, low in ends),
        )

    start = 6 - 3 * core
    for t in range(tiles):
        terms = radial(
            lambda f, k: wide[f, start + k, t], lambda k: wide[2, start + k, t], layers + 3
        )
        for k, term in enumerate(terms):
            for g in range(3):
                part[g, start - 3 + k, t] = term[g]

    def own(layer, carry):
        here = [[wide[f, layer + 6, t] for t in range(tiles)] for f in range(3)]
        terms = lat_inner(here, sub, True)
        for t in range(tiles):
            lon = lon_terms([x[t] for x in here], True)
            for g in range(3):
                part[g, layer + 3, t] += terms[t][g] + jnp.where(away, lon[g], 0.0)
        return carry

    lax.fori_loop(0, layers, own, 0, unroll=2)

    def other(e, carry):
        here = [[wide[f, near + 3 + e, t] for t in range(tiles)] for f in range(3)]
        terms = lat_inner(here, sub, False)
        for t in range(tiles):
            lon = lon_terms([x[t] for x in here], False)
            for g in range(2):
                part[g, near + e, t] += terms[t][g] + jnp.where(away, lon[g], 0.0)
        return carry

    lax.fori_loop(0, 3, other, 0, unroll=True)


def turn_kernel(*refs):
    fields, packs, part = refs[:6], refs[6:10], refs[10]
    to_first, to_second, to_third, to_core, edges = refs[14:]
    layers, rows, lanes = fields[0].shape
    tiles = rows // SUB
    sub, lane = iotas(lanes)
    seg = lane % SEGMENT
    core = lax.axis_index("rad")
    even = lax.axis_index("lat") % 2 == 0
    per = lanes // SEGMENT
    groups = packs[0].shape[0]

    def send(k, low, high):
        to_first[k] = to_third[k] = jnp.where(even, high, low)
        to_second[k] = jnp.where(even, low, high)

    def ends(ref, *index):
        low, high = (ref[(*index, pl.ds(t * SUB, SUB), slice(None))] for t in (0, tiles - 1))
        return jnp.where(sub < 4, low, high)

    for k, ref in enumerate(packs):
        to_core[k] = ref[(groups - 1) * (1 - core)]
    halos = []
    for g in range(groups):
        pack = [ends(x, g) for x in packs]
        wins = [windows(*pack, f, seg) for f in range(3)]
        laps, _ = edge_terms(wins, seg, False, OFFSETS)
        halos.append(halos_of(aligned(wins), seg))
        for s in range(min(per, layers - g * per)):
            layer = g * per + s
            here = [ends(x, layer) for x in fields]
            stiff = here[5] * LAP_SCALE
            made = []
            for f in range(2):
                before = jnp.where(sub < 4, part[f, layer + 3, 0], part[f, layer + 3, tiles - 1])
                lap = before + at_ends(laps[f], s, lane)
                made.append(2.0 * here[f] - here[3 + f] + stiff * lap)
            send(layer, *(pack_three(*made, here[5], low, sub) for low in (True, False)))
    both = [merged([pack_three(*x, low, sub) for x in halos], seg) for low in (True, False)]
    for k, (low, high) in enumerate(zip(*both)):
        send(2 * layers + 4 + k, low, high)
        edges[0, k] = low
        edges[1, k] = high


def middle_kernel(*refs):
    fields, (bulk_in, density_in) = refs[:6], refs[6:8]
    packs, from_core, from_core2, wide, part = refs[8:12], refs[12], refs[13], refs[14], refs[15]
    first, first_pack, stiff_pack, buoy_halo, flux_out, sums, done = refs[16:23]
    first_halo, own_pack, part_last, halo_pack, lap_pack = refs[23:]
    layers, rows, lanes = fields[0].shape
    tiles = rows // SUB
    sub, lane = iotas(lanes)
    seg = lane % SEGMENT
    core = lax.axis_index("rad")
    near, border = places(core, layers)
    per = lanes // SEGMENT
    groups = packs[0].shape[0]
    zero = jnp.zeros((SUB, lanes), F32)
    inside = range(1, tiles - 1)

    def at(t):
        return pl.ds(pl.multiple_of(t * SUB, SUB), SUB)

    def edges_at(t, carry):
        sources = [[x[group, at(t), :] for x in packs] for group in range(groups)]
        sources.append([from_core2[k, at(t), :] for k in range(4)])
        wins = [aligned([windows(*x, f, seg) for f in range(3)]) for x in sources]
        halos = [halos_of(x, seg) for x in wins]
        before = [jnp.where(core == 0, 0.0, x) for x in halos[-1]]
        after = [jnp.where(core == 0, x, 0.0) for x in halos[-1]]
        radials = packed_radial([before, *halos[:-1], after], lane)
        terms = [edge_terms(x, seg, True, (0, 0, 0)) for x in wins[:-1]]
        own = [x for x, _ in terms]
        for group in range(groups):
            for f, x in enumerate(halos[group]):
                halo_pack[f, group, t] = x
            for g in range(2):
                lap_pack[g, group, t] = terms[group][1][g] + radials[group][g]
        for group in range(groups):
            for g, x in enumerate(own[group]):
                own_pack[g, group, t] = x
        return carry

    def other_at(t, carry):
        other = [from_core2[k, at(t), :] for k in range(4)]
        wins = aligned([windows(*other, f, seg) for f in range(3)])
        own, _ = edge_terms(wins, seg, False, (0, 0, 0))
        for g in range(2):
            own_pack[g, groups, t] = jnp.where(core == 0, own[g], rolled(own[g], -(per - 3) * SEGMENT, 1))
        return carry

    lax.fori_loop(0, tiles, edges_at, 0, unroll=2)
    lax.fori_loop(0, tiles, other_at, 0, unroll=True)
    for group in range(groups):
        halo = [[halo_pack[f, group, t] for t in range(tiles)] for f in range(3)]
        lat = lat_inner(halo, sub, False)
        for t in range(tiles):
            rest = []
            for f in range(3, 6):
                offset = OFFSETS[f]
                mask = (seg >= offset) & (seg < offset + WIDTHS[f])
                x = jnp.where(mask, packs[0][group, at(t), :], packs[1][group, at(t), :])
                rest.append(rolled(x, 3 - offset, 1))
            stiff = rest[2] * LAP_SCALE
            stiff_pack[group, t] = stiff
            for g in range(2):
                lap = lap_pack[g, group, t] + lat[t][g]
                first_pack[g, group, t] = 2.0 * halo[g][t] - rest[g] + stiff * lap
    for g in range(2):
        for k in range(3):
            for t in range(tiles):
                first[g, border + k, t] = zero

    def first_at(t, carry):
        for layer in range(layers):
            group, s = divmod(layer, per)
            buoy_halo[layer, t] = spread(halo_pack[2, group, t], s)
            stiff = fields[5][layer, at(t), :] * LAP_SCALE
            here = [wide[f, layer + 6, t] for f in range(2)]
            for g in range(2):
                first_halo[g, layer, t] = spread(first_pack[g, group, t], s)
                lap = part[g, layer + 3, t] + at_ends(own_pack[g, group, t], s, lane)
                update = stiff * lap
                first[g, layer + 3, t] = 2.0 * here[g] - fields[3 + g][layer, at(t), :] + update
            sums[0, layer, t] = bulk_in[layer, at(t), :] + here[0] * update
            rho = part[2, layer + 3, t] + at_ends(own_pack[2, group, t], s, lane)
            sums[1, layer, t] = density_in[layer, at(t), :] + RHO_SCALE * rho
        for e in range(3):
            stiff = from_core[24 + e, at(t), :] * LAP_SCALE
            for g in range(2):
                lap = part[g, near + e, t] + at_ends(own_pack[g, groups, t], e, lane)
                past = from_core[18 + 3 * g + e, at(t), :]
                first[g, near + e, t] = 2.0 * wide[g, near + 3 + e, t] - past + stiff * lap
        return carry

    lax.fori_loop(0, tiles, first_at, 0, unroll=2)

    for t in inside:
        terms = radial(lambda f, k: first[f, 3 + k, t], lambda k: wide[2, 6 + k, t], layers)
        for k, term in enumerate(terms):
            for g in range(3):
                part_last[g, k, t - 1] = term[g]

    def last(layer, carry):
        here = [[first[f, layer + 3, t] for t in range(tiles)] for f in range(2)]
        here.append([wide[2, layer + 6, t] for t in range(tiles)])
        flux = [lat_flux(here, t, sub) for t in range(tiles)]
        for k in range(3):
            for n, t in enumerate((1, tiles - 2)):
                flux_out[k, n, layer] = flux[t][k]
        for t in inside:
            lat = lat_terms(flux, t, sub, True)
            there = [first_halo[0, layer, t], first_halo[1, layer, t], buoy_halo[layer, t]]
            laps, rho = longitudinal([x[t] for x in here], there, lane, False, True)
            stiff = fields[5][layer, at(t), :] * LAP_SCALE
            for g in range(2):
                update = stiff * (part_last[g, layer, t - 1] + lat[g] + laps[0][g])
                done[2 * g, layer, at(t - 1), :] = (
                    2.0 * here[g][t] - fields[g][layer, at(t), :] + update
                )
                done[2 * g + 1, layer, at(t - 1), :] = here[g][t]
            done[4, layer, at(t - 1), :] = sums[0, layer, t] + here[0][t] * update
            done[5, layer, at(t - 1), :] = sums[1, layer, t] + RHO_SCALE * (
                part_last[2, layer, t - 1] + lat[2] + rho
            )
        return carry

    lax.fori_loop(0, layers, last, 0, unroll=4)


def last_kernel(*refs):
    fields, from_core = refs[:6], refs[6]
    wide, first, first_pack, stiff_pack, buoy_halo, flux_in, sums, done = refs[7:15]
    edges, from_first, from_second, from_third = refs[15:19]
    outs = refs[19:25]
    fixed, fixed_halo, ring_buoy, part, made, sems = refs[25:]
    layers, rows, lanes = fields[0].shape
    tiles = rows // SUB
    sub, lane = iotas(lanes)
    core = lax.axis_index("rad")
    place, count = lax.axis_index("lat"), lax.axis_size("lat")
    even = place % 2 == 0
    near, border = places(core, layers)
    zero = jnp.zeros((SUB, lanes), F32)
    ends = ((0, sub < 3), (tiles - 1, sub >= SUB - 3))
    copies = [
        pltpu.make_async_copy(done.at[k], out.at[:, pl.ds(SUB, rows - 2 * SUB), :], sems.at[k, 0])
        for k, out in enumerate(outs)
    ]
    for copy in copies:
        copy.start()

    def at(t):
        return pl.ds(t * SUB, SUB)

    def received(k):
        one = jnp.where(place % 4 < 2, from_first[k], from_third[k])
        two = from_second[k]
        behind, ahead = jnp.where(even, two, one), jnp.where(even, one, two)
        return jnp.where(place > 0, behind, 0.0), jnp.where(place < count - 1, ahead, 0.0)

    def join(behind, ahead):
        return jnp.where(sub < 4, ahead, behind)

    def three(k):
        behind, ahead = received(k)
        return list(zip(unpack_three(behind, False), unpack_three(ahead, True)))

    def outer(own, halos):
        low = [jnp.where(sub < 4, x[0], h[0]) for x, h in zip(own, halos)]
        high = [jnp.where(sub < 4, h[1], x[1]) for x, h in zip(own, halos)]
        return lat_outer(*low, sub), lat_outer(*high, sub)

    for g in range(2):
        for k in range(3):
            for n in range(2):
                fixed[g, border + k, n] = zero

    per = lanes // SEGMENT
    for group in range(stiff_pack.shape[0]):
        if group % 2 == 0:
            k = group // 2
            mine = list(zip(unpack_three(edges[0, k], True), unpack_three(edges[1, k], False)))
            side = outer(mine, three(2 * layers + 4 + k))
        for n, (t, mask) in enumerate(ends):
            for g in range(2):
                lap = jnp.where(mask, unmerged(side[n][g], group), 0.0)
                x = first_pack[g, group, t] + stiff_pack[group, t] * lap
                for s in range(min(per, layers - group * per)):
                    fixed_halo[g, group * per + s, n] = spread(x, s)

    for e in range(3):
        halos = three(2 * layers + 1 + e)
        mine = [(wide[f, near + 3 + e, 0], wide[f, near + 3 + e, tiles - 1]) for f in range(3)]
        side = outer(mine, halos)
        for n, (t, mask) in enumerate(ends):
            stiff = from_core[24 + e, at(t), :] * LAP_SCALE
            for g in range(2):
                lap = jnp.where(mask, side[n][g], 0.0)
                fixed[g, near + e, n] = first[g, near + e, t] + stiff * lap

    third = received(2 * layers)
    for layer in range(layers):
        halos = three(layers + layer)
        mine = [(x[layer, at(0), :], x[layer, at(tiles - 1), :]) for x in fields[:3]]
        side = outer(mine, halos)
        for n, (t, mask) in enumerate(ends):
            stiff = fields[5][layer, at(t), :] * LAP_SCALE
            for g in range(2):
                update = stiff * jnp.where(mask, side[n][g], 0.0)
                fixed[g, layer + 3, n] = first[g, layer + 3, t] + update
            made[4, layer, n] = sums[0, layer, t] + mine[0][n] * update
            made[5, layer, n] = sums[1, layer, t] + RHO_SCALE * jnp.where(mask, side[n][2], 0.0)
        adj, fwd, stiff = three(layer)
        low, high = (rolled(third[k], row - layer, 0) for k, row in enumerate((SUB - 3, 2)))
        stiff = jnp.where(
            sub < 4,
            jnp.where(sub == 2, high, stiff[1]),
            jnp.where(sub == SUB - 3, low, stiff[0]),
        )
        for g, x in enumerate((adj, fwd)):
            lap = join(side[0][g], side[1][g])
            fixed[g, layer + 3, 2] = join(*x) + stiff * LAP_SCALE * lap
        ring_buoy[layer] = join(*halos[2])

    for n, (t, _) in enumerate(ends):
        terms = radial(lambda f, k: fixed[f, 3 + k, n], lambda k: wide[2, 6 + k, t], layers)
        for k, term in enumerate(terms):
            for g in range(3):
                part[g, k, n] = term[g]

    def last(layer, n):
        t = ends[n][0]
        rings = [[fixed[f, layer + 3, 2], fixed[f, layer + 3, n]] for f in range(2)]
        rings.append([ring_buoy[layer], wide[2, layer + 6, t]])
        beside = [first[f, layer + 3, (1, tiles - 2)[n]] for f in range(2)]
        beside.append(wide[2, layer + 6, (1, tiles - 2)[n]])
        rings = [[x[0], x[1], y] if n == 0 else [y, x[1], x[0]] for x, y in zip(rings, beside)]
        flux = [None] * 3
        flux[1] = lat_flux(rings, 1, sub)
        flux[2 * n] = lat_flux(rings, 2 * n, sub)
        flux[2 - 2 * n] = [flux_in[k, n, layer] for k in range(3)]
        here = [x[1] for x in rings]
        lat = lat_terms(flux, 1, sub, True)
        there = [fixed_halo[0, layer, n], fixed_halo[1, layer, n], buoy_halo[layer, t]]
        laps, rho = longitudinal(here, there, lane, False, True)
        stiff = fields[5][layer, at(t), :] * LAP_SCALE
        for g in range(2):
            update = stiff * (part[g, layer, n] + lat[g] + laps[0][g])
            made[2 * g, layer, n] = 2.0 * here[g] - fields[g][layer, at(t), :] + update
            made[2 * g + 1, layer, n] = here[g]
        made[4, layer, n] += here[0] * update
        made[5, layer, n] += RHO_SCALE * (part[2, layer, n] + lat[2] + rho)

    for n, (t, _) in enumerate(ends):
        for layer in range(layers):
            last(layer, n)
        for k, out in enumerate(outs):
            copy = pltpu.make_async_copy(made.at[k, :, n], out.at[:, at(t), :], sems.at[k, 1 + n])
            copy.start()
            copies.append(copy)
    for copy in copies:
        copy.wait()


def pairs(count, start, step):
    partner = {i: i for i in range(count)}
    for i in range(start, count - 1, step):
        partner[i], partner[i + 1] = i + 1, i
    return [
        (2 * i + core, 2 * j + (core if i != j else 1 - core))
        for i, j in partner.items()
        for core in range(2)
    ]


def call(kernel, out_shape, args, in_specs=None, out_specs=None, **more):
    return pl.pallas_call(
        kernel,
        out_shape=out_shape,
        in_specs=in_specs or [VMEM] * len(args),
        out_specs=out_specs or (VMEM,) * len(out_shape),
        compiler_params=PARAMS,
        **more,
    )(*args)


def shards(
    adj_now, adj_next, fwd_now, fwd_next, stiffness, buoyancy, kernel_bulk_in, kernel_density_in
):
    layers, rows, lanes = adj_now.shape
    tiles = rows // SUB
    fields = (adj_now, fwd_now, buoyancy, adj_next, fwd_next, stiffness)
    groups = -(-layers // (lanes // SEGMENT))
    around, count = lax.axis_size("lon"), lax.axis_size("lat")
    ring = [(i, (i + 1) % around) for i in range(around)]
    swap = [(0, 1), (1, 0)]

    def made(*shape):
        return pltpu.VMEM(shape, F32)

    block = (layers, rows, lanes)
    edge = made(groups, rows, lanes)
    hbm = pl.BlockSpec(memory_space=pltpu.HBM)
    *fields, to_right, to_left, to_core = call(
        edges_kernel,
        (made(*block),) * 6 + (edge, edge, made(sum(WIDTHS), rows, lanes)),
        [pltpu.with_memory_space_constraint(x, pltpu.HBM) for x in fields],
        in_specs=[hbm] * 6,
        scratch_shapes=[pltpu.SemaphoreType.DMA((6,))],
    )
    from_left = lax.ppermute(to_right, "lon", ring)
    from_right = lax.ppermute(to_left, "lon", [(b, a) for a, b in ring])
    from_core = lax.ppermute(to_core, "rad", swap)
    pairs_of_groups = -(-groups // 2)
    lat_edge = made(2 * layers + 4 + pairs_of_groups, SUB, lanes)
    packs = [from_left, from_right, to_left, to_right]
    wide, part, to_first, to_second, to_third = call(
        inner_kernel,
        (
            made(3, layers + 12, tiles, SUB, lanes),
            made(3, layers + 6, tiles, SUB, lanes),
            lat_edge,
            lat_edge,
            lat_edge,
        ),
        [*fields, from_core],
    )
    to_first, to_second, to_third, to_core, edges = call(
        turn_kernel,
        (lat_edge, lat_edge, lat_edge, made(4, rows, lanes), made(2, pairs_of_groups, SUB, lanes)),
        [*fields, *packs, part, to_first, to_second, to_third],
        input_output_aliases={11: 0, 12: 1, 13: 2},
    )
    from_first = lax.ppermute(to_first, ("lat", "rad"), pairs(count, 0, 4))
    from_second = lax.ppermute(to_second, ("lat", "rad"), pairs(count, 1, 2))
    from_third = lax.ppermute(to_third, ("lat", "rad"), pairs(count, 2, 4))
    from_core2 = lax.ppermute(to_core, "rad", swap)
    first, first_pack, stiff_pack, buoy_halo, flux, sums, done = call(
        middle_kernel,
        (
            made(2, layers + 6, tiles, SUB, lanes),
            made(2, groups, tiles, SUB, lanes),
            made(groups, tiles, SUB, lanes),
            made(layers, tiles, SUB, lanes),
            made(3, 2, layers, SUB, lanes),
            made(2, layers, tiles, SUB, lanes),
            made(6, layers, rows - 2 * SUB, lanes),
        ),
        [
            *fields,
            kernel_bulk_in,
            kernel_density_in,
            *packs,
            from_core,
            from_core2,
            wide,
            part,
        ],
        cost_estimate=HEAVY,
        scratch_shapes=[
            made(2, layers, tiles, SUB, lanes),
            made(3, groups + 1, tiles, SUB, lanes),
            made(3, layers, tiles - 2, SUB, lanes),
            made(3, groups, tiles, SUB, lanes),
            made(2, groups, tiles, SUB, lanes),
        ],
    )
    return call(
        last_kernel,
        (jax.ShapeDtypeStruct(block, F32),) * 6,
        [
            *fields,
            from_core,
            wide,
            first,
            first_pack,
            stiff_pack,
            buoy_halo,
            flux,
            sums,
            done,
            edges,
            from_first,
            from_second,
            from_third,
        ],
        out_specs=(hbm,) * 6,
        scratch_shapes=[
            made(2, layers + 6, 3, SUB, lanes),
            made(2, layers, 2, SUB, lanes),
            made(layers, SUB, lanes),
            made(3, layers, 2, SUB, lanes),
            made(6, layers, 2, SUB, lanes),
            pltpu.SemaphoreType.DMA((6, 3)),
        ],
    )


def solution(mesh):
    spec = P("rad", "lat", "lon")
    return jax.shard_map(
        shards, mesh=mesh, in_specs=(spec,) * 8, out_specs=(spec,) * 6, check_vma=False
    )
```

```python
import jax
import jax.numpy as jnp
from jax import lax
from jax.experimental import pallas as pl
from jax.experimental.pallas import tpu as pltpu
from jax.sharding import PartitionSpec as P

F32 = jnp.float32
SUB = 8
LAP_SCALE = 1.0 / 1152.0
RHO_SCALE = 1.0 / 2304.0
WIDTHS = (6, 6, 6, 3, 3, 3)
OFFSETS = (0, 6, 12, 21, 24, 27)
SEGMENT = 32
VMEM = pl.BlockSpec(memory_space=pltpu.VMEM)
PARAMS = pltpu.CompilerParams(vmem_limit_bytes=24 * 1024 * 1024)
HEAVY = pl.CostEstimate(flops=4000000000, bytes_accessed=1000000, transcendentals=0)


def iotas(lanes):
    return (
        lax.broadcasted_iota(jnp.int32, (SUB, lanes), 0),
        lax.broadcasted_iota(jnp.int32, (SUB, lanes), 1),
    )


def rolled(x, shift, axis):
    size = x.shape[axis]
    shift = shift % size
    return x if shift == 0 else pltpu.roll(x, shift, axis)


def lane_shift(here, there, by, lane):
    size = here.shape[1]
    if by > 0:
        return rolled(jnp.where(lane < by, there, here), size - by, 1)
    return rolled(jnp.where(lane >= size + by, there, here), -by, 1)


def row_shift(tiles, t, by, sub):
    if by > 0:
        return rolled(jnp.where(sub < by, tiles[(t + 1) % len(tiles)], tiles[t]), SUB - by, 0)
    return rolled(jnp.where(sub >= SUB + by, tiles[t - 1], tiles[t]), -by, 0)


def slope(ahead, here, ahead2, behind):
    return 27.0 * (ahead - here) - (ahead2 - behind)


def pack_three(a, b, c, low, sub):
    if low:
        return jnp.where(sub < 3, a, jnp.where(sub < 6, rolled(b, 3, 0), rolled(c, 6, 0)))
    return jnp.where(sub >= 5, a, jnp.where(sub >= 2, rolled(b, -3, 0), rolled(c, -6, 0)))


def unpack_three(x, low):
    sign = -1 if low else 1
    return x, rolled(x, 3 * sign, 0), rolled(x, 6 * sign, 0)


def edges_kernel(*refs):
    sources, fields, (to_right, to_left, to_core), sems = refs[:6], refs[6:12], refs[12:15], refs[15]
    copies = [pltpu.make_async_copy(x, y, sems.at[k]) for k, (x, y) in enumerate(zip(sources, fields))]
    for copy in copies:
        copy.start()
    layers, rows, lanes = fields[0].shape
    _, lane = iotas(lanes)
    core = lax.axis_index("rad")
    per = lanes // SEGMENT
    for copy in copies:
        copy.wait()
    for group in range(to_right.shape[0]):
        for t in range(rows // SUB):
            at = pl.ds(t * SUB, SUB)
            right = left = None
            for layer in range(group * per, min(layers, (group + 1) * per)):
                for f, (width, offset) in enumerate(zip(WIDTHS, OFFSETS)):
                    first = (layer - group * per) * SEGMENT + offset
                    second = first + width
                    x = rolled(fields[f][layer, at, :], second, 1)
                    mask = lane >= second
                    if second + width > lanes:
                        mask = mask | (lane < second + width - lanes)
                    right = x if right is None else jnp.where(lane >= first, x, right)
                    left = x if left is None else jnp.where(mask, x, left)
            to_right[group, at, :] = right
            to_left[group, at, :] = left
    row = 0
    for f, width in enumerate(WIDTHS):
        to_core[row : row + width] = fields[f][pl.ds((layers - width) * (1 - core), width)]
        row += width


def radial(p_at, b_at, layers):
    flux, rho = [], []
    p = [[p_at(f, k) for k in range(-3, layers + 3)] for f in range(2)]
    b = [b_at(k) for k in range(-2, layers + 2)]
    for k in range(layers + 3):
        buoy = b[k] + b[k + 1]
        grads = [slope(x[k + 2], x[k + 1], x[k + 3], x[k]) for x in p]
        flux.append([buoy * g for g in grads])
        rho.append(flux[k][0] * grads[1])
    out = []
    for k in range(layers):
        laps = [slope(flux[k + 2][f], flux[k + 1][f], flux[k + 3][f], flux[k][f]) for f in range(2)]
        out.append((laps[0], laps[1], rho[k + 1] + rho[k + 2]))
    return out


def longitudinal(here, there, lane, want_there, want_rho):
    flux, rho = [], []
    for x, y in ((here, there), (there, here)):
        buoy = x[2] + lane_shift(x[2], y[2], 1, lane)
        grads = [
            slope(
                lane_shift(x[f], y[f], 1, lane),
                x[f],
                lane_shift(x[f], y[f], 2, lane),
                lane_shift(x[f], y[f], -1, lane),
            )
            for f in range(2)
        ]
        flux.append([buoy * g for g in grads])
        rho.append(flux[-1][0] * grads[1])
    laps = []
    for x, y in ((0, 1), (1, 0))[: 2 if want_there else 1]:
        laps.append(
            [
                slope(
                    flux[x][f],
                    lane_shift(flux[x][f], flux[y][f], -1, lane),
                    lane_shift(flux[x][f], flux[y][f], 1, lane),
                    lane_shift(flux[x][f], flux[y][f], -2, lane),
                )
                for f in range(2)
            ]
        )
    density = rho[0] + lane_shift(rho[0], rho[1], -1, lane) if want_rho else None
    return laps, density


def windows(from_left, from_right, to_left, to_right, f, seg):
    offset = OFFSETS[f]
    mask = (seg >= offset) & (seg < offset + WIDTHS[f])
    return jnp.where(mask, from_left, to_left), jnp.where(mask, to_right, from_right)


def lon_flux(fields, offsets):
    def shift(f, by):
        return rolled(fields[f], -offsets[f] - by, 1)

    face = shift(2, 0) + shift(2, 1)
    grads = [slope(shift(f, 1), shift(f, 0), shift(f, 2), shift(f, -1)) for f in range(2)]
    flux = [face * g for g in grads]
    return flux[0], flux[1], flux[0] * grads[1]


def lon_terms(fields, want_rho, offsets=(0, 0, 0)):
    flux = lon_flux(fields, offsets)
    terms = [slope(x, rolled(x, 1, 1), rolled(x, -1, 1), rolled(x, 2, 1)) for x in flux[:2]]
    return terms + [flux[2] + rolled(flux[2], 1, 1)] if want_rho else terms


def edge_terms(wins, seg, want_rho, offsets):
    left = lon_terms([x[0] for x in wins], want_rho, offsets)
    right = lon_terms([x[1] for x in wins], want_rho, offsets)
    valid = (seg >= 3) & (seg < 9)
    own = [jnp.where(valid, jnp.where(seg < 6, y, x), 0.0) for x, y in zip(left, right)]
    return own, [jnp.where(seg < 6, x, y) for x, y in zip(left[:2], right[:2])]


def halos_of(wins, seg):
    return [jnp.where(seg < 6, x, y) for x, y in wins]


def aligned(wins):
    return [tuple(rolled(x, -offset, 1) for x in win) for win, offset in zip(wins, OFFSETS)]


def spread(x, s):
    return rolled(x, -s * SEGMENT - 6, 1)


def at_ends(x, s, lane):
    return jnp.where((lane < 3) | (lane >= x.shape[1] - 3), spread(x, s), 0.0)


def merged(tiles, seg):
    half = SEGMENT // 2
    out = []
    for k in range(0, len(tiles), 2):
        x = tiles[k]
        if k + 1 < len(tiles):
            x = jnp.where(seg < half, x, rolled(tiles[k + 1], half, 1))
        out.append(x)
    return out


def unmerged(x, group):
    return rolled(x, -(SEGMENT // 2) * (group % 2), 1)


def packed_radial(groups, lane):
    size = lane.shape[1]

    def shift(x, i, by):
        step = by * SEGMENT
        if by > 0:
            return rolled(jnp.where(lane < step, x[min(i + 1, len(x) - 1)], x[i]), -step, 1)
        return rolled(jnp.where(lane >= size + step, x[max(i - 1, 0)], x[i]), -step, 1)

    adj, fwd, buoy = ([x[f] for x in groups] for f in range(3))
    flux = ([], [])
    for i in range(len(groups)):
        face = buoy[i] + shift(buoy, i, 1)
        for f, x in enumerate((adj, fwd)):
            flux[f].append(face * slope(shift(x, i, 1), x[i], shift(x, i, 2), shift(x, i, -1)))
    return [
        [slope(x[i], shift(x, i, -1), shift(x, i, 1), shift(x, i, -2)) for x in flux]
        for i in range(1, len(groups) - 1)
    ]


def lat_flux(ring, t, sub):
    adj, fwd, buoy = ring
    face = buoy[t] + row_shift(buoy, t, 1, sub)
    grads = [
        slope(row_shift(x, t, 1, sub), x[t], row_shift(x, t, 2, sub), row_shift(x, t, -1, sub))
        for x in (adj, fwd)
    ]
    flux = [face * g for g in grads]
    return flux[0], flux[1], flux[0] * grads[1]


def lat_terms(flux, t, sub, want_rho):
    adj, fwd, rho = ([x[k] for x in flux] for k in range(3))
    laps = [
        slope(x[t], row_shift(x, t, -1, sub), row_shift(x, t, 1, sub), row_shift(x, t, -2, sub))
        for x in (adj, fwd)
    ]
    return laps[0], laps[1], rho[t] + row_shift(rho, t, -1, sub) if want_rho else None


def lat_inner(ring, sub, want_rho):
    count = len(ring[0])
    flux = [list(lat_flux(ring, t, sub)) for t in range(count)]
    zero = jnp.zeros_like(ring[0][0])
    for k in range(3):
        flux[0][k] = jnp.where(sub >= 1, flux[0][k], zero)
        flux[-1][k] = jnp.where(sub < SUB - 2, flux[-1][k], zero)
    flux.append([zero] * 3)
    return [lat_terms(flux, t, sub, want_rho) for t in range(count)]


def lat_outer(adj, fwd, buoy, sub):
    ring = ([adj], [fwd], [buoy])
    mask = (sub >= SUB - 2) | (sub < 1)
    flux = [[jnp.where(mask, x, 0.0) for x in lat_flux(ring, 0, sub)]]
    return lat_terms(flux, 0, sub, True)


def places(core, layers):
    return (layers + 3) * (1 - core), (layers + 3) * core


def inner_kernel(*refs):
    fields, (bulk_in, density_in), from_core = refs[:6], refs[6:8], refs[8]
    wide, part, base, to_first, to_second, to_third = refs[9:]
    layers, rows, lanes = fields[0].shape
    tiles = rows // SUB
    sub, lane = iotas(lanes)
    core = lax.axis_index("rad")
    even = lax.axis_index("lat") % 2 == 0
    near, border = places(core, layers)
    zero = jnp.zeros((SUB, lanes), F32)
    away = (lane >= 3) & (lane < lanes - 3)

    def at(t):
        return pl.ds(t * SUB, SUB)

    for f in range(3):
        for t in range(tiles):
            for layer in range(layers):
                wide[f, layer + 6, t] = fields[f][layer, at(t), :]
            for k in range(6):
                wide[f, (layers + 6) * (1 - core) + k, t] = from_core[6 * f + k, at(t), :]
            for k in range(3):
                wide[f, border + 3 + k, t] = zero

    def send(k, low, high):
        to_first[k] = to_third[k] = jnp.where(even, high, low)
        to_second[k] = jnp.where(even, low, high)

    ends = ((0, True), (tiles - 1, False))
    third = [None, None]
    for layer in range(layers):
        send(
            layers + layer,
            *(pack_three(*(x[layer, at(t), :] for x in fields[:3]), low, sub) for t, low in ends),
        )
        for k, row in enumerate((2, SUB - 3)):
            x = rolled(fields[5][layer, at(ends[k][0]), :], layer - row, 0)
            third[k] = x if layer == 0 else jnp.where(sub == layer, x, third[k])
    send(2 * layers, *third)
    for e in range(3):
        send(
            2 * layers + 1 + e,
            *(pack_three(*(wide[f, near + 3 + e, t] for f in range(3)), low, sub) for t, low in ends),
        )

    start = 6 - 3 * core
    for t in range(tiles):
        terms = radial(
            lambda f, k: wide[f, start + k, t], lambda k: wide[2, start + k, t], layers + 3
        )
        for k, term in enumerate(terms):
            for g in range(3):
                part[g, start - 3 + k, t] = term[g]

    def own(layer, carry):
        here = [[wide[f, layer + 6, t] for t in range(tiles)] for f in range(3)]
        terms = lat_inner(here, sub, True)
        for t in range(tiles):
            lon = lon_terms([x[t] for x in here], True)
            total = [
                part[g, layer + 3, t] + terms[t][g] + jnp.where(away, lon[g], 0.0) for g in range(3)
            ]
            stiff = fields[5][layer, at(t), :] * LAP_SCALE
            for g in range(2):
                part[g, layer + 3, t] = total[g]
                update = stiff * total[g]
                base[g, layer, t] = 2.0 * here[g][t] - fields[3 + g][layer, at(t), :] + update
            base[2, layer, t] = bulk_in[layer, at(t), :] + here[0][t] * update
            base[3, layer, t] = density_in[layer, at(t), :] + RHO_SCALE * total[2]
        return carry

    lax.fori_loop(0, layers, own, 0, unroll=2)

    def other(e, carry):
        here = [[wide[f, near + 3 + e, t] for t in range(tiles)] for f in range(3)]
        terms = lat_inner(here, sub, False)
        for t in range(tiles):
            lon = lon_terms([x[t] for x in here], False)
            for g in range(2):
                part[g, near + e, t] += terms[t][g] + jnp.where(away, lon[g], 0.0)
        return carry

    lax.fori_loop(0, 3, other, 0, unroll=True)


def turn_kernel(*refs):
    fields, packs, part = refs[:6], refs[6:10], refs[10]
    to_first, to_second, to_third, to_core, edges = refs[14:]
    layers, rows, lanes = fields[0].shape
    tiles = rows // SUB
    sub, lane = iotas(lanes)
    seg = lane % SEGMENT
    core = lax.axis_index("rad")
    even = lax.axis_index("lat") % 2 == 0
    per = lanes // SEGMENT
    groups = packs[0].shape[0]

    def send(k, low, high):
        to_first[k] = to_third[k] = jnp.where(even, high, low)
        to_second[k] = jnp.where(even, low, high)

    def ends(ref, *index):
        low, high = (ref[(*index, pl.ds(t * SUB, SUB), slice(None))] for t in (0, tiles - 1))
        return jnp.where(sub < 4, low, high)

    for k, ref in enumerate(packs):
        to_core[k] = ref[(groups - 1) * (1 - core)]
    halos = []
    for g in range(groups):
        pack = [ends(x, g) for x in packs]
        wins = [windows(*pack, f, seg) for f in range(3)]
        laps, _ = edge_terms(wins, seg, False, OFFSETS)
        halos.append(halos_of(aligned(wins), seg))
        for s in range(min(per, layers - g * per)):
            layer = g * per + s
            here = [ends(x, layer) for x in fields]
            stiff = here[5] * LAP_SCALE
            made = []
            for f in range(2):
                before = jnp.where(sub < 4, part[f, layer + 3, 0], part[f, layer + 3, tiles - 1])
                lap = before + at_ends(laps[f], s, lane)
                made.append(2.0 * here[f] - here[3 + f] + stiff * lap)
            send(layer, *(pack_three(*made, here[5], low, sub) for low in (True, False)))
    both = [merged([pack_three(*x, low, sub) for x in halos], seg) for low in (True, False)]
    for k, (low, high) in enumerate(zip(*both)):
        send(2 * layers + 4 + k, low, high)
        edges[0, k] = low
        edges[1, k] = high


def middle_kernel(*refs):
    fields, base = refs[:6], refs[6]
    packs, from_core, from_core2, wide, part = refs[7:11], refs[11], refs[12], refs[13], refs[14]
    first, first_pack, stiff_pack, buoy_halo, flux_out, sums, done = refs[15:22]
    first_halo, own_pack, part_last, halo_pack, lap_pack = refs[22:]
    layers, rows, lanes = fields[0].shape
    tiles = rows // SUB
    sub, lane = iotas(lanes)
    seg = lane % SEGMENT
    core = lax.axis_index("rad")
    near, border = places(core, layers)
    per = lanes // SEGMENT
    groups = packs[0].shape[0]
    zero = jnp.zeros((SUB, lanes), F32)
    inside = range(1, tiles - 1)

    def at(t):
        return pl.ds(pl.multiple_of(t * SUB, SUB), SUB)

    def edges_at(t, carry):
        sources = [[x[group, at(t), :] for x in packs] for group in range(groups)]
        sources.append([from_core2[k, at(t), :] for k in range(4)])
        wins = [aligned([windows(*x, f, seg) for f in range(3)]) for x in sources]
        halos = [halos_of(x, seg) for x in wins]
        before = [jnp.where(core == 0, 0.0, x) for x in halos[-1]]
        after = [jnp.where(core == 0, x, 0.0) for x in halos[-1]]
        radials = packed_radial([before, *halos[:-1], after], lane)
        terms = [edge_terms(x, seg, True, (0, 0, 0)) for x in wins[:-1]]
        own = [x for x, _ in terms]
        for group in range(groups):
            for f, x in enumerate(halos[group]):
                halo_pack[f, group, t] = x
            for g in range(2):
                lap_pack[g, group, t] = terms[group][1][g] + radials[group][g]
        for group in range(groups):
            for g, x in enumerate(own[group]):
                own_pack[g, group, t] = x
        return carry

    def other_at(t, carry):
        other = [from_core2[k, at(t), :] for k in range(4)]
        wins = aligned([windows(*other, f, seg) for f in range(3)])
        own, _ = edge_terms(wins, seg, False, (0, 0, 0))
        for g in range(2):
            own_pack[g, groups, t] = jnp.where(core == 0, own[g], rolled(own[g], -(per - 3) * SEGMENT, 1))
        return carry

    lax.fori_loop(0, tiles, edges_at, 0, unroll=2)
    lax.fori_loop(0, tiles, other_at, 0, unroll=True)
    for group in range(groups):
        halo = [[halo_pack[f, group, t] for t in range(tiles)] for f in range(3)]
        lat = lat_inner(halo, sub, False)
        for t in range(tiles):
            rest = []
            for f in range(3, 6):
                offset = OFFSETS[f]
                mask = (seg >= offset) & (seg < offset + WIDTHS[f])
                x = jnp.where(mask, packs[0][group, at(t), :], packs[1][group, at(t), :])
                rest.append(rolled(x, 3 - offset, 1))
            stiff = rest[2] * LAP_SCALE
            stiff_pack[group, t] = stiff
            for g in range(2):
                lap = lap_pack[g, group, t] + lat[t][g]
                first_pack[g, group, t] = 2.0 * halo[g][t] - rest[g] + stiff * lap
    for g in range(2):
        for k in range(3):
            for t in range(tiles):
                first[g, border + k, t] = zero

    def first_at(t, carry):
        for layer in range(layers):
            group, s = divmod(layer, per)
            buoy_halo[layer, t] = spread(halo_pack[2, group, t], s)
            stiff = fields[5][layer, at(t), :] * LAP_SCALE
            for g in range(2):
                first_halo[g, layer, t] = spread(first_pack[g, group, t], s)
                update = stiff * at_ends(own_pack[g, group, t], s, lane)
                first[g, layer + 3, t] = base[g, layer, t] + update
            sums[0, layer, t] = base[2, layer, t] + wide[0, layer + 6, t] * update
            rho = at_ends(own_pack[2, group, t], s, lane)
            sums[1, layer, t] = base[3, layer, t] + RHO_SCALE * rho
        for e in range(3):
            stiff = from_core[24 + e, at(t), :] * LAP_SCALE
            for g in range(2):
                lap = part[g, near + e, t] + at_ends(own_pack[g, groups, t], e, lane)
                past = from_core[18 + 3 * g + e, at(t), :]
                first[g, near + e, t] = 2.0 * wide[g, near + 3 + e, t] - past + stiff * lap
        return carry

    lax.fori_loop(0, tiles, first_at, 0, unroll=2)

    for t in inside:
        terms = radial(lambda f, k: first[f, 3 + k, t], lambda k: wide[2, 6 + k, t], layers)
        for k, term in enumerate(terms):
            for g in range(3):
                part_last[g, k, t - 1] = term[g]

    def last(layer, carry):
        here = [[first[f, layer + 3, t] for t in range(tiles)] for f in range(2)]
        here.append([wide[2, layer + 6, t] for t in range(tiles)])
        flux = [lat_flux(here, t, sub) for t in range(tiles)]
        for k in range(3):
            for n, t in enumerate((1, tiles - 2)):
                flux_out[k, n, layer] = flux[t][k]
        for t in inside:
            lat = lat_terms(flux, t, sub, True)
            there = [first_halo[0, layer, t], first_halo[1, layer, t], buoy_halo[layer, t]]
            laps, rho = longitudinal([x[t] for x in here], there, lane, False, True)
            stiff = fields[5][layer, at(t), :] * LAP_SCALE
            for g in range(2):
                update = stiff * (part_last[g, layer, t - 1] + lat[g] + laps[0][g])
                done[2 * g, layer, at(t - 1), :] = (
                    2.0 * here[g][t] - fields[g][layer, at(t), :] + update
                )
                done[2 * g + 1, layer, at(t - 1), :] = here[g][t]
            done[4, layer, at(t - 1), :] = sums[0, layer, t] + here[0][t] * update
            done[5, layer, at(t - 1), :] = sums[1, layer, t] + RHO_SCALE * (
                part_last[2, layer, t - 1] + lat[2] + rho
            )
        return carry

    lax.fori_loop(0, layers, last, 0, unroll=4)


def last_kernel(*refs):
    fields, from_core = refs[:6], refs[6]
    wide, first, first_pack, stiff_pack, buoy_halo, flux_in, sums, done = refs[7:15]
    edges, from_first, from_second, from_third = refs[15:19]
    outs = refs[19:25]
    fixed, fixed_halo, ring_buoy, part, made, sems = refs[25:]
    layers, rows, lanes = fields[0].shape
    tiles = rows // SUB
    sub, lane = iotas(lanes)
    core = lax.axis_index("rad")
    place, count = lax.axis_index("lat"), lax.axis_size("lat")
    even = place % 2 == 0
    near, border = places(core, layers)
    zero = jnp.zeros((SUB, lanes), F32)
    ends = ((0, sub < 3), (tiles - 1, sub >= SUB - 3))
    copies = [
        pltpu.make_async_copy(done.at[k], out.at[:, pl.ds(SUB, rows - 2 * SUB), :], sems.at[k, 0])
        for k, out in enumerate(outs)
    ]
    for copy in copies:
        copy.start()

    def at(t):
        return pl.ds(t * SUB, SUB)

    def received(k):
        one = jnp.where(place % 4 < 2, from_first[k], from_third[k])
        two = from_second[k]
        behind, ahead = jnp.where(even, two, one), jnp.where(even, one, two)
        return jnp.where(place > 0, behind, 0.0), jnp.where(place < count - 1, ahead, 0.0)

    def join(behind, ahead):
        return jnp.where(sub < 4, ahead, behind)

    def three(k):
        behind, ahead = received(k)
        return list(zip(unpack_three(behind, False), unpack_three(ahead, True)))

    def outer(own, halos):
        low = [jnp.where(sub < 4, x[0], h[0]) for x, h in zip(own, halos)]
        high = [jnp.where(sub < 4, h[1], x[1]) for x, h in zip(own, halos)]
        return lat_outer(*low, sub), lat_outer(*high, sub)

    for g in range(2):
        for k in range(3):
            for n in range(2):
                fixed[g, border + k, n] = zero

    per = lanes // SEGMENT
    for group in range(stiff_pack.shape[0]):
        if group % 2 == 0:
            k = group // 2
            mine = list(zip(unpack_three(edges[0, k], True), unpack_three(edges[1, k], False)))
            side = outer(mine, three(2 * layers + 4 + k))
        for n, (t, mask) in enumerate(ends):
            for g in range(2):
                lap = jnp.where(mask, unmerged(side[n][g], group), 0.0)
                x = first_pack[g, group, t] + stiff_pack[group, t] * lap
                for s in range(min(per, layers - group * per)):
                    fixed_halo[g, group * per + s, n] = spread(x, s)

    for e in range(3):
        halos = three(2 * layers + 1 + e)
        mine = [(wide[f, near + 3 + e, 0], wide[f, near + 3 + e, tiles - 1]) for f in range(3)]
        side = outer(mine, halos)
        for n, (t, mask) in enumerate(ends):
            stiff = from_core[24 + e, at(t), :] * LAP_SCALE
            for g in range(2):
                lap = jnp.where(mask, side[n][g], 0.0)
                fixed[g, near + e, n] = first[g, near + e, t] + stiff * lap

    third = received(2 * layers)
    for layer in range(layers):
        halos = three(layers + layer)
        mine = [(x[layer, at(0), :], x[layer, at(tiles - 1), :]) for x in fields[:3]]
        side = outer(mine, halos)
        for n, (t, mask) in enumerate(ends):
            stiff = fields[5][layer, at(t), :] * LAP_SCALE
            for g in range(2):
                update = stiff * jnp.where(mask, side[n][g], 0.0)
                fixed[g, layer + 3, n] = first[g, layer + 3, t] + update
            made[4, layer, n] = sums[0, layer, t] + mine[0][n] * update
            made[5, layer, n] = sums[1, layer, t] + RHO_SCALE * jnp.where(mask, side[n][2], 0.0)
        adj, fwd, stiff = three(layer)
        low, high = (rolled(third[k], row - layer, 0) for k, row in enumerate((SUB - 3, 2)))
        stiff = jnp.where(
            sub < 4,
            jnp.where(sub == 2, high, stiff[1]),
            jnp.where(sub == SUB - 3, low, stiff[0]),
        )
        for g, x in enumerate((adj, fwd)):
            lap = join(side[0][g], side[1][g])
            fixed[g, layer + 3, 2] = join(*x) + stiff * LAP_SCALE * lap
        ring_buoy[layer] = join(*halos[2])

    for n, (t, _) in enumerate(ends):
        terms = radial(lambda f, k: fixed[f, 3 + k, n], lambda k: wide[2, 6 + k, t], layers)
        for k, term in enumerate(terms):
            for g in range(3):
                part[g, k, n] = term[g]

    def last(layer, n):
        t = ends[n][0]
        rings = [[fixed[f, layer + 3, 2], fixed[f, layer + 3, n]] for f in range(2)]
        rings.append([ring_buoy[layer], wide[2, layer + 6, t]])
        beside = [first[f, layer + 3, (1, tiles - 2)[n]] for f in range(2)]
        beside.append(wide[2, layer + 6, (1, tiles - 2)[n]])
        rings = [[x[0], x[1], y] if n == 0 else [y, x[1], x[0]] for x, y in zip(rings, beside)]
        flux = [None] * 3
        flux[1] = lat_flux(rings, 1, sub)
        flux[2 * n] = lat_flux(rings, 2 * n, sub)
        flux[2 - 2 * n] = [flux_in[k, n, layer] for k in range(3)]
        here = [x[1] for x in rings]
        lat = lat_terms(flux, 1, sub, True)
        there = [fixed_halo[0, layer, n], fixed_halo[1, layer, n], buoy_halo[layer, t]]
        laps, rho = longitudinal(here, there, lane, False, True)
        stiff = fields[5][layer, at(t), :] * LAP_SCALE
        for g in range(2):
            update = stiff * (part[g, layer, n] + lat[g] + laps[0][g])
            made[2 * g, layer, n] = 2.0 * here[g] - fields[g][layer, at(t), :] + update
            made[2 * g + 1, layer, n] = here[g]
        made[4, layer, n] += here[0] * update
        made[5, layer, n] += RHO_SCALE * (part[2, layer, n] + lat[2] + rho)

    for n, (t, _) in enumerate(ends):
        for layer in range(layers):
            last(layer, n)
        for k, out in enumerate(outs):
            copy = pltpu.make_async_copy(made.at[k, :, n], out.at[:, at(t), :], sems.at[k, 1 + n])
            copy.start()
            copies.append(copy)
    for copy in copies:
        copy.wait()


def pairs(count, start, step):
    partner = {i: i for i in range(count)}
    for i in range(start, count - 1, step):
        partner[i], partner[i + 1] = i + 1, i
    return [
        (2 * i + core, 2 * j + (core if i != j else 1 - core))
        for i, j in partner.items()
        for core in range(2)
    ]


def call(kernel, out_shape, args, in_specs=None, out_specs=None, **more):
    return pl.pallas_call(
        kernel,
        out_shape=out_shape,
        in_specs=in_specs or [VMEM] * len(args),
        out_specs=out_specs or (VMEM,) * len(out_shape),
        compiler_params=PARAMS,
        **more,
    )(*args)


def shards(
    adj_now, adj_next, fwd_now, fwd_next, stiffness, buoyancy, kernel_bulk_in, kernel_density_in
):
    layers, rows, lanes = adj_now.shape
    tiles = rows // SUB
    fields = (adj_now, fwd_now, buoyancy, adj_next, fwd_next, stiffness)
    groups = -(-layers // (lanes // SEGMENT))
    around, count = lax.axis_size("lon"), lax.axis_size("lat")
    ring = [(i, (i + 1) % around) for i in range(around)]
    swap = [(0, 1), (1, 0)]

    def made(*shape):
        return pltpu.VMEM(shape, F32)

    block = (layers, rows, lanes)
    edge = made(groups, rows, lanes)
    hbm = pl.BlockSpec(memory_space=pltpu.HBM)
    *fields, to_right, to_left, to_core = call(
        edges_kernel,
        (made(*block),) * 6 + (edge, edge, made(sum(WIDTHS), rows, lanes)),
        [pltpu.with_memory_space_constraint(x, pltpu.HBM) for x in fields],
        in_specs=[hbm] * 6,
        scratch_shapes=[pltpu.SemaphoreType.DMA((6,))],
    )
    from_left = lax.ppermute(to_right, "lon", ring)
    from_right = lax.ppermute(to_left, "lon", [(b, a) for a, b in ring])
    from_core = lax.ppermute(to_core, "rad", swap)
    pairs_of_groups = -(-groups // 2)
    lat_edge = made(2 * layers + 4 + pairs_of_groups, SUB, lanes)
    packs = [from_left, from_right, to_left, to_right]
    wide, part, base, to_first, to_second, to_third = call(
        inner_kernel,
        (
            made(3, layers + 12, tiles, SUB, lanes),
            made(3, layers + 6, tiles, SUB, lanes),
            made(4, layers, tiles, SUB, lanes),
            lat_edge,
            lat_edge,
            lat_edge,
        ),
        [*fields, kernel_bulk_in, kernel_density_in, from_core],
    )
    to_first, to_second, to_third, to_core, edges = call(
        turn_kernel,
        (lat_edge, lat_edge, lat_edge, made(4, rows, lanes), made(2, pairs_of_groups, SUB, lanes)),
        [*fields, *packs, part, to_first, to_second, to_third],
        input_output_aliases={11: 0, 12: 1, 13: 2},
    )
    from_first = lax.ppermute(to_first, ("lat", "rad"), pairs(count, 0, 4))
    from_second = lax.ppermute(to_second, ("lat", "rad"), pairs(count, 1, 2))
    from_third = lax.ppermute(to_third, ("lat", "rad"), pairs(count, 2, 4))
    from_core2 = lax.ppermute(to_core, "rad", swap)
    first, first_pack, stiff_pack, buoy_halo, flux, sums, done = call(
        middle_kernel,
        (
            made(2, layers + 6, tiles, SUB, lanes),
            made(2, groups, tiles, SUB, lanes),
            made(groups, tiles, SUB, lanes),
            made(layers, tiles, SUB, lanes),
            made(3, 2, layers, SUB, lanes),
            made(2, layers, tiles, SUB, lanes),
            made(6, layers, rows - 2 * SUB, lanes),
        ),
        [
            *fields,
            base,
            *packs,
            from_core,
            from_core2,
            wide,
            part,
        ],
        cost_estimate=HEAVY,
        scratch_shapes=[
            made(2, layers, tiles, SUB, lanes),
            made(3, groups + 1, tiles, SUB, lanes),
            made(3, layers, tiles - 2, SUB, lanes),
            made(3, groups, tiles, SUB, lanes),
            made(2, groups, tiles, SUB, lanes),
        ],
    )
    return call(
        last_kernel,
        (jax.ShapeDtypeStruct(block, F32),) * 6,
        [
            *fields,
            from_core,
            wide,
            first,
            first_pack,
            stiff_pack,
            buoy_halo,
            flux,
            sums,
            done,
            edges,
            from_first,
            from_second,
            from_third,
        ],
        out_specs=(hbm,) * 6,
        scratch_shapes=[
            made(2, layers + 6, 3, SUB, lanes),
            made(2, layers, 2, SUB, lanes),
            made(layers, SUB, lanes),
            made(3, layers, 2, SUB, lanes),
            made(6, layers, 2, SUB, lanes),
            pltpu.SemaphoreType.DMA((6, 3)),
        ],
    )


def solution(mesh):
    spec = P("rad", "lat", "lon")
    return jax.shard_map(
        shards, mesh=mesh, in_specs=(spec,) * 8, out_specs=(spec,) * 6, check_vma=False
    )
```

```python
import jax
import jax.numpy as jnp
from jax import lax
from jax.experimental import pallas as pl
from jax.experimental.pallas import tpu as pltpu
from jax.sharding import PartitionSpec as P

F32 = jnp.float32
SUB = 8
LAP_SCALE = 1.0 / 1152.0
RHO_SCALE = 1.0 / 2304.0
WIDTHS = (6, 6, 6, 3, 3, 3)
OFFSETS = (0, 6, 12, 21, 24, 27)
SEGMENT = 32
VMEM = pl.BlockSpec(memory_space=pltpu.VMEM)
PARAMS = pltpu.CompilerParams(vmem_limit_bytes=24 * 1024 * 1024)
HEAVY = pl.CostEstimate(flops=4000000000, bytes_accessed=1000000, transcendentals=0)


def iotas(lanes):
    return (
        lax.broadcasted_iota(jnp.int32, (SUB, lanes), 0),
        lax.broadcasted_iota(jnp.int32, (SUB, lanes), 1),
    )


def rolled(x, shift, axis):
    size = x.shape[axis]
    shift = shift % size
    return x if shift == 0 else pltpu.roll(x, shift, axis)


def lane_shift(here, there, by, lane):
    size = here.shape[1]
    if by > 0:
        return rolled(jnp.where(lane < by, there, here), size - by, 1)
    return rolled(jnp.where(lane >= size + by, there, here), -by, 1)


def row_shift(tiles, t, by, sub):
    if by > 0:
        return rolled(jnp.where(sub < by, tiles[(t + 1) % len(tiles)], tiles[t]), SUB - by, 0)
    return rolled(jnp.where(sub >= SUB + by, tiles[t - 1], tiles[t]), -by, 0)


def slope(ahead, here, ahead2, behind):
    return 27.0 * (ahead - here) - (ahead2 - behind)


def pack_three(a, b, c, low, sub):
    if low:
        return jnp.where(sub < 3, a, jnp.where(sub < 6, rolled(b, 3, 0), rolled(c, 6, 0)))
    return jnp.where(sub >= 5, a, jnp.where(sub >= 2, rolled(b, -3, 0), rolled(c, -6, 0)))


def unpack_three(x, low):
    sign = -1 if low else 1
    return x, rolled(x, 3 * sign, 0), rolled(x, 6 * sign, 0)


def edges_kernel(*refs):
    sources, fields, (to_right, to_left, to_core), sems = refs[:6], refs[6:12], refs[12:15], refs[15]
    copies = [pltpu.make_async_copy(x, y, sems.at[k]) for k, (x, y) in enumerate(zip(sources, fields))]
    for copy in copies:
        copy.start()
    layers, rows, lanes = fields[0].shape
    _, lane = iotas(lanes)
    core = lax.axis_index("rad")
    per = lanes // SEGMENT
    for copy in copies:
        copy.wait()
    for group in range(to_right.shape[0]):
        for t in range(rows // SUB):
            at = pl.ds(t * SUB, SUB)
            right = left = None
            for layer in range(group * per, min(layers, (group + 1) * per)):
                for f, (width, offset) in enumerate(zip(WIDTHS, OFFSETS)):
                    first = (layer - group * per) * SEGMENT + offset
                    second = first + width
                    x = rolled(fields[f][layer, at, :], second, 1)
                    mask = lane >= second
                    if second + width > lanes:
                        mask = mask | (lane < second + width - lanes)
                    right = x if right is None else jnp.where(lane >= first, x, right)
                    left = x if left is None else jnp.where(mask, x, left)
            to_right[group, at, :] = right
            to_left[group, at, :] = left
    row = 0
    for f, width in enumerate(WIDTHS):
        to_core[row : row + width] = fields[f][pl.ds((layers - width) * (1 - core), width)]
        row += width


def radial(p_at, b_at, layers):
    flux, rho = [], []
    p = [[p_at(f, k) for k in range(-3, layers + 3)] for f in range(2)]
    b = [b_at(k) for k in range(-2, layers + 2)]
    for k in range(layers + 3):
        buoy = b[k] + b[k + 1]
        grads = [slope(x[k + 2], x[k + 1], x[k + 3], x[k]) for x in p]
        flux.append([buoy * g for g in grads])
        rho.append(flux[k][0] * grads[1])
    out = []
    for k in range(layers):
        laps = [slope(flux[k + 2][f], flux[k + 1][f], flux[k + 3][f], flux[k][f]) for f in range(2)]
        out.append((laps[0], laps[1], rho[k + 1] + rho[k + 2]))
    return out


def longitudinal(here, there, lane, want_there, want_rho):
    flux, rho = [], []
    for x, y in ((here, there), (there, here)):
        buoy = x[2] + lane_shift(x[2], y[2], 1, lane)
        grads = [
            slope(
                lane_shift(x[f], y[f], 1, lane),
                x[f],
                lane_shift(x[f], y[f], 2, lane),
                lane_shift(x[f], y[f], -1, lane),
            )
            for f in range(2)
        ]
        flux.append([buoy * g for g in grads])
        rho.append(flux[-1][0] * grads[1])
    laps = []
    for x, y in ((0, 1), (1, 0))[: 2 if want_there else 1]:
        laps.append(
            [
                slope(
                    flux[x][f],
                    lane_shift(flux[x][f], flux[y][f], -1, lane),
                    lane_shift(flux[x][f], flux[y][f], 1, lane),
                    lane_shift(flux[x][f], flux[y][f], -2, lane),
                )
                for f in range(2)
            ]
        )
    density = rho[0] + lane_shift(rho[0], rho[1], -1, lane) if want_rho else None
    return laps, density


def windows(from_left, from_right, to_left, to_right, f, seg):
    offset = OFFSETS[f]
    mask = (seg >= offset) & (seg < offset + WIDTHS[f])
    return jnp.where(mask, from_left, to_left), jnp.where(mask, to_right, from_right)


def lon_flux(fields, offsets):
    def shift(f, by):
        return rolled(fields[f], -offsets[f] - by, 1)

    face = shift(2, 0) + shift(2, 1)
    grads = [slope(shift(f, 1), shift(f, 0), shift(f, 2), shift(f, -1)) for f in range(2)]
    flux = [face * g for g in grads]
    return flux[0], flux[1], flux[0] * grads[1]


def lon_terms(fields, want_rho, offsets=(0, 0, 0)):
    flux = lon_flux(fields, offsets)
    terms = [slope(x, rolled(x, 1, 1), rolled(x, -1, 1), rolled(x, 2, 1)) for x in flux[:2]]
    return terms + [flux[2] + rolled(flux[2], 1, 1)] if want_rho else terms


def edge_terms(wins, seg, want_rho, offsets):
    left = lon_terms([x[0] for x in wins], want_rho, offsets)
    right = lon_terms([x[1] for x in wins], want_rho, offsets)
    valid = (seg >= 3) & (seg < 9)
    own = [jnp.where(valid, jnp.where(seg < 6, y, x), 0.0) for x, y in zip(left, right)]
    return own, [jnp.where(seg < 6, x, y) for x, y in zip(left[:2], right[:2])]


def halos_of(wins, seg):
    return [jnp.where(seg < 6, x, y) for x, y in wins]


def aligned(wins):
    return [tuple(rolled(x, -offset, 1) for x in win) for win, offset in zip(wins, OFFSETS)]


def spread(x, s):
    return rolled(x, -s * SEGMENT - 6, 1)


def at_ends(x, s, lane):
    return jnp.where((lane < 3) | (lane >= x.shape[1] - 3), spread(x, s), 0.0)


def merged(tiles, seg):
    half = SEGMENT // 2
    out = []
    for k in range(0, len(tiles), 2):
        x = tiles[k]
        if k + 1 < len(tiles):
            x = jnp.where(seg < half, x, rolled(tiles[k + 1], half, 1))
        out.append(x)
    return out


def unmerged(x, group):
    return rolled(x, -(SEGMENT // 2) * (group % 2), 1)


def packed_radial(groups, lane):
    size = lane.shape[1]

    def shift(x, i, by):
        step = by * SEGMENT
        if by > 0:
            return rolled(jnp.where(lane < step, x[min(i + 1, len(x) - 1)], x[i]), -step, 1)
        return rolled(jnp.where(lane >= size + step, x[max(i - 1, 0)], x[i]), -step, 1)

    adj, fwd, buoy = ([x[f] for x in groups] for f in range(3))
    flux = ([], [])
    for i in range(len(groups)):
        face = buoy[i] + shift(buoy, i, 1)
        for f, x in enumerate((adj, fwd)):
            flux[f].append(face * slope(shift(x, i, 1), x[i], shift(x, i, 2), shift(x, i, -1)))
    return [
        [slope(x[i], shift(x, i, -1), shift(x, i, 1), shift(x, i, -2)) for x in flux]
        for i in range(1, len(groups) - 1)
    ]


def lat_flux(ring, t, sub):
    adj, fwd, buoy = ring
    face = buoy[t] + row_shift(buoy, t, 1, sub)
    grads = [
        slope(row_shift(x, t, 1, sub), x[t], row_shift(x, t, 2, sub), row_shift(x, t, -1, sub))
        for x in (adj, fwd)
    ]
    flux = [face * g for g in grads]
    return flux[0], flux[1], flux[0] * grads[1]


def lat_terms(flux, t, sub, want_rho):
    adj, fwd, rho = ([x[k] for x in flux] for k in range(3))
    laps = [
        slope(x[t], row_shift(x, t, -1, sub), row_shift(x, t, 1, sub), row_shift(x, t, -2, sub))
        for x in (adj, fwd)
    ]
    return laps[0], laps[1], rho[t] + row_shift(rho, t, -1, sub) if want_rho else None


def lat_inner(ring, sub, want_rho):
    count = len(ring[0])
    flux = [list(lat_flux(ring, t, sub)) for t in range(count)]
    zero = jnp.zeros_like(ring[0][0])
    for k in range(3):
        flux[0][k] = jnp.where(sub >= 1, flux[0][k], zero)
        flux[-1][k] = jnp.where(sub < SUB - 2, flux[-1][k], zero)
    flux.append([zero] * 3)
    return [lat_terms(flux, t, sub, want_rho) for t in range(count)]


def lat_outer(adj, fwd, buoy, sub):
    ring = ([adj], [fwd], [buoy])
    mask = (sub >= SUB - 2) | (sub < 1)
    flux = [[jnp.where(mask, x, 0.0) for x in lat_flux(ring, 0, sub)]]
    return lat_terms(flux, 0, sub, True)


def places(core, layers):
    return (layers + 3) * (1 - core), (layers + 3) * core


def inner_kernel(*refs):
    fields, (bulk_in, density_in), from_core = refs[:6], refs[6:8], refs[8]
    wide, part, base, to_first, to_second, to_third = refs[9:]
    layers, rows, lanes = fields[0].shape
    tiles = rows // SUB
    sub, lane = iotas(lanes)
    core = lax.axis_index("rad")
    even = lax.axis_index("lat") % 2 == 0
    near, border = places(core, layers)
    zero = jnp.zeros((SUB, lanes), F32)
    away = (lane >= 3) & (lane < lanes - 3)

    def at(t):
        return pl.ds(t * SUB, SUB)

    for f in range(3):
        for t in range(tiles):
            for layer in range(layers):
                wide[f, layer + 6, t] = fields[f][layer, at(t), :]
            for k in range(6):
                wide[f, (layers + 6) * (1 - core) + k, t] = from_core[6 * f + k, at(t), :]
            for k in range(3):
                wide[f, border + 3 + k, t] = zero

    def send(k, low, high):
        to_first[k] = to_third[k] = jnp.where(even, high, low)
        to_second[k] = jnp.where(even, low, high)

    ends = ((0, True), (tiles - 1, False))
    third = [None, None]
    for layer in range(layers):
        send(
            layers + layer,
            *(pack_three(*(x[layer, at(t), :] for x in fields[:3]), low, sub) for t, low in ends),
        )
        for k, row in enumerate((2, SUB - 3)):
            x = rolled(fields[5][layer, at(ends[k][0]), :], layer - row, 0)
            third[k] = x if layer == 0 else jnp.where(sub == layer, x, third[k])
    send(2 * layers, *third)
    for e in range(3):
        send(
            2 * layers + 1 + e,
            *(pack_three(*(wide[f, near + 3 + e, t] for f in range(3)), low, sub) for t, low in ends),
        )

    start = 6 - 3 * core
    for t in range(tiles):
        terms = radial(
            lambda f, k: wide[f, start + k, t], lambda k: wide[2, start + k, t], layers + 3
        )
        for k, term in enumerate(terms):
            for g in range(3):
                part[g, start - 3 + k, t] = term[g]

    def own(layer, carry):
        here = [[wide[f, layer + 6, t] for t in range(tiles)] for f in range(3)]
        terms = lat_inner(here, sub, True)
        for t in range(tiles):
            lon = lon_terms([x[t] for x in here], True)
            total = [
                part[g, layer + 3, t] + terms[t][g] + jnp.where(away, lon[g], 0.0) for g in range(3)
            ]
            stiff = fields[5][layer, at(t), :] * LAP_SCALE
            for g in range(2):
                part[g, layer + 3, t] = total[g]
                update = stiff * total[g]
                base[g, layer, t] = 2.0 * here[g][t] - fields[3 + g][layer, at(t), :] + update
            base[2, layer, t] = bulk_in[layer, at(t), :] + here[0][t] * update
            base[3, layer, t] = density_in[layer, at(t), :] + RHO_SCALE * total[2]
        return carry

    lax.fori_loop(0, layers, own, 0, unroll=2)

    def other(e, carry):
        here = [[wide[f, near + 3 + e, t] for t in range(tiles)] for f in range(3)]
        terms = lat_inner(here, sub, False)
        for t in range(tiles):
            lon = lon_terms([x[t] for x in here], False)
            for g in range(2):
                part[g, near + e, t] += terms[t][g] + jnp.where(away, lon[g], 0.0)
        return carry

    lax.fori_loop(0, 3, other, 0, unroll=True)


def turn_kernel(*refs):
    fields, packs, part = refs[:6], refs[6:10], refs[10]
    to_first, to_second, to_third, to_core, edges = refs[14:]
    layers, rows, lanes = fields[0].shape
    tiles = rows // SUB
    sub, lane = iotas(lanes)
    seg = lane % SEGMENT
    core = lax.axis_index("rad")
    even = lax.axis_index("lat") % 2 == 0
    per = lanes // SEGMENT
    groups = packs[0].shape[0]

    def send(k, low, high):
        to_first[k] = to_third[k] = jnp.where(even, high, low)
        to_second[k] = jnp.where(even, low, high)

    def ends(ref, *index):
        low, high = (ref[(*index, pl.ds(t * SUB, SUB), slice(None))] for t in (0, tiles - 1))
        return jnp.where(sub < 4, low, high)

    for k, ref in enumerate(packs):
        to_core[k] = ref[(groups - 1) * (1 - core)]
    halos = []
    for g in range(groups):
        pack = [ends(x, g) for x in packs]
        wins = [windows(*pack, f, seg) for f in range(3)]
        laps, _ = edge_terms(wins, seg, False, OFFSETS)
        halos.append(halos_of(aligned(wins), seg))
        for s in range(min(per, layers - g * per)):
            layer = g * per + s
            here = [ends(x, layer) for x in fields]
            stiff = here[5] * LAP_SCALE
            made = []
            for f in range(2):
                before = jnp.where(sub < 4, part[f, layer + 3, 0], part[f, layer + 3, tiles - 1])
                lap = before + at_ends(laps[f], s, lane)
                made.append(2.0 * here[f] - here[3 + f] + stiff * lap)
            send(layer, *(pack_three(*made, here[5], low, sub) for low in (True, False)))
    both = [merged([pack_three(*x, low, sub) for x in halos], seg) for low in (True, False)]
    for k, (low, high) in enumerate(zip(*both)):
        send(2 * layers + 4 + k, low, high)
        edges[0, k] = low
        edges[1, k] = high


def middle_kernel(*refs):
    fields, base = refs[:6], refs[6]
    packs, from_core, from_core2, wide, part = refs[7:11], refs[11], refs[12], refs[13], refs[14]
    first, first_pack, stiff_pack, buoy_halo, flux_out, sums, done = refs[15:22]
    first_halo, own_pack, part_last, halo_pack, lap_pack = refs[22:]
    layers, rows, lanes = fields[0].shape
    tiles = rows // SUB
    sub, lane = iotas(lanes)
    seg = lane % SEGMENT
    core = lax.axis_index("rad")
    near, border = places(core, layers)
    per = lanes // SEGMENT
    groups = packs[0].shape[0]
    zero = jnp.zeros((SUB, lanes), F32)
    inside = range(1, tiles - 1)

    def at(t):
        return pl.ds(pl.multiple_of(t * SUB, SUB), SUB)

    def edges_at(t, carry):
        sources = [[x[group, at(t), :] for x in packs] for group in range(groups)]
        sources.append([from_core2[k, at(t), :] for k in range(4)])
        wins = [aligned([windows(*x, f, seg) for f in range(3)]) for x in sources]
        halos = [halos_of(x, seg) for x in wins]
        before = [jnp.where(core == 0, 0.0, x) for x in halos[-1]]
        after = [jnp.where(core == 0, x, 0.0) for x in halos[-1]]
        radials = packed_radial([before, *halos[:-1], after], lane)
        terms = [edge_terms(x, seg, True, (0, 0, 0)) for x in wins[:-1]]
        own = [x for x, _ in terms]
        for group in range(groups):
            for f, x in enumerate(halos[group]):
                halo_pack[f, group, t] = x
            for g in range(2):
                lap_pack[g, group, t] = terms[group][1][g] + radials[group][g]
        for group in range(groups):
            for g, x in enumerate(own[group]):
                own_pack[g, group, t] = x
        return carry

    def other_at(t, carry):
        other = [from_core2[k, at(t), :] for k in range(4)]
        wins = aligned([windows(*other, f, seg) for f in range(3)])
        own, _ = edge_terms(wins, seg, False, (0, 0, 0))
        for g in range(2):
            own_pack[g, groups, t] = jnp.where(core == 0, own[g], rolled(own[g], -(per - 3) * SEGMENT, 1))
        return carry

    lax.fori_loop(0, tiles, edges_at, 0, unroll=2)
    lax.fori_loop(0, tiles, other_at, 0, unroll=True)
    for group in range(groups):
        halo = [[halo_pack[f, group, t] for t in range(tiles)] for f in range(3)]
        lat = lat_inner(halo, sub, False)
        for t in range(tiles):
            rest = []
            for f in range(3, 6):
                offset = OFFSETS[f]
                mask = (seg >= offset) & (seg < offset + WIDTHS[f])
                x = jnp.where(mask, packs[0][group, at(t), :], packs[1][group, at(t), :])
                rest.append(rolled(x, 3 - offset, 1))
            stiff = rest[2] * LAP_SCALE
            stiff_pack[group, t] = stiff
            for g in range(2):
                lap = lap_pack[g, group, t] + lat[t][g]
                first_pack[g, group, t] = 2.0 * halo[g][t] - rest[g] + stiff * lap
    for g in range(2):
        for k in range(3):
            for t in range(tiles):
                first[g, border + k, t] = zero

    def first_at(t, carry):
        for layer in range(layers):
            group, s = divmod(layer, per)
            buoy_halo[layer, t] = spread(halo_pack[2, group, t], s)
            stiff = fields[5][layer, at(t), :] * LAP_SCALE
            for g in range(2):
                first_halo[g, layer, t] = spread(first_pack[g, group, t], s)
                update = stiff * at_ends(own_pack[g, group, t], s, lane)
                first[g, layer + 3, t] = base[g, layer, t] + update
            sums[0, layer, t] = base[2, layer, t] + wide[0, layer + 6, t] * update
            rho = at_ends(own_pack[2, group, t], s, lane)
            sums[1, layer, t] = base[3, layer, t] + RHO_SCALE * rho
        for e in range(3):
            stiff = from_core[24 + e, at(t), :] * LAP_SCALE
            for g in range(2):
                lap = part[g, near + e, t] + at_ends(own_pack[g, groups, t], e, lane)
                past = from_core[18 + 3 * g + e, at(t), :]
                first[g, near + e, t] = 2.0 * wide[g, near + 3 + e, t] - past + stiff * lap
        return carry

    lax.fori_loop(0, tiles, first_at, 0, unroll=2)

    for t in inside:
        terms = radial(lambda f, k: first[f, 3 + k, t], lambda k: wide[2, 6 + k, t], layers)
        for k, term in enumerate(terms):
            for g in range(3):
                part_last[g, k, t - 1] = term[g]

    def last(layer, carry):
        here = [[first[f, layer + 3, t] for t in range(tiles)] for f in range(2)]
        here.append([wide[2, layer + 6, t] for t in range(tiles)])
        flux = [lat_flux(here, t, sub) for t in range(tiles)]
        for k in range(3):
            for n, t in enumerate((1, tiles - 2)):
                flux_out[k, n, layer] = flux[t][k]
        for t in inside:
            lat = lat_terms(flux, t, sub, True)
            there = [first_halo[0, layer, t], first_halo[1, layer, t], buoy_halo[layer, t]]
            laps, rho = longitudinal([x[t] for x in here], there, lane, False, True)
            stiff = fields[5][layer, at(t), :] * LAP_SCALE
            for g in range(2):
                update = stiff * (part_last[g, layer, t - 1] + lat[g] + laps[0][g])
                done[2 * g, layer, at(t - 1), :] = (
                    2.0 * here[g][t] - fields[g][layer, at(t), :] + update
                )
                done[2 * g + 1, layer, at(t - 1), :] = here[g][t]
            done[4, layer, at(t - 1), :] = sums[0, layer, t] + here[0][t] * update
            done[5, layer, at(t - 1), :] = sums[1, layer, t] + RHO_SCALE * (
                part_last[2, layer, t - 1] + lat[2] + rho
            )
        return carry

    lax.fori_loop(0, layers, last, 0, unroll=4)


def last_kernel(*refs):
    fields, from_core = refs[:6], refs[6]
    wide, first, first_pack, stiff_pack, buoy_halo, flux_in, sums, done = refs[7:15]
    edges, from_first, from_second, from_third = refs[15:19]
    outs = refs[19:25]
    fixed, fixed_halo, ring_buoy, made, sems = refs[25:]
    layers, rows, lanes = fields[0].shape
    tiles = rows // SUB
    sub, lane = iotas(lanes)
    core = lax.axis_index("rad")
    place, count = lax.axis_index("lat"), lax.axis_size("lat")
    even = place % 2 == 0
    near, border = places(core, layers)
    zero = jnp.zeros((SUB, lanes), F32)
    ends = ((0, sub < 3), (tiles - 1, sub >= SUB - 3))
    copies = [
        pltpu.make_async_copy(done.at[k], out.at[:, pl.ds(SUB, rows - 2 * SUB), :], sems.at[k, 0])
        for k, out in enumerate(outs)
    ]
    for copy in copies:
        copy.start()

    def at(t):
        return pl.ds(t * SUB, SUB)

    def received(k):
        one = jnp.where(place % 4 < 2, from_first[k], from_third[k])
        two = from_second[k]
        behind, ahead = jnp.where(even, two, one), jnp.where(even, one, two)
        return jnp.where(place > 0, behind, 0.0), jnp.where(place < count - 1, ahead, 0.0)

    def join(behind, ahead):
        return jnp.where(sub < 4, ahead, behind)

    def three(k):
        behind, ahead = received(k)
        return list(zip(unpack_three(behind, False), unpack_three(ahead, True)))

    def outer(own, halos):
        low = [jnp.where(sub < 4, x[0], h[0]) for x, h in zip(own, halos)]
        high = [jnp.where(sub < 4, h[1], x[1]) for x, h in zip(own, halos)]
        return lat_outer(*low, sub), lat_outer(*high, sub)

    for g in range(2):
        for k in range(3):
            for n in range(2):
                fixed[g, border + k, n] = zero

    per = lanes // SEGMENT
    for group in range(stiff_pack.shape[0]):
        if group % 2 == 0:
            k = group // 2
            mine = list(zip(unpack_three(edges[0, k], True), unpack_three(edges[1, k], False)))
            side = outer(mine, three(2 * layers + 4 + k))
        for n, (t, mask) in enumerate(ends):
            for g in range(2):
                lap = jnp.where(mask, unmerged(side[n][g], group), 0.0)
                x = first_pack[g, group, t] + stiff_pack[group, t] * lap
                for s in range(min(per, layers - group * per)):
                    fixed_halo[g, group * per + s, n] = spread(x, s)

    for e in range(3):
        halos = three(2 * layers + 1 + e)
        mine = [(wide[f, near + 3 + e, 0], wide[f, near + 3 + e, tiles - 1]) for f in range(3)]
        side = outer(mine, halos)
        for n, (t, mask) in enumerate(ends):
            stiff = from_core[24 + e, at(t), :] * LAP_SCALE
            for g in range(2):
                lap = jnp.where(mask, side[n][g], 0.0)
                fixed[g, near + e, n] = first[g, near + e, t] + stiff * lap

    third = received(2 * layers)
    for layer in range(layers):
        halos = three(layers + layer)
        mine = [(x[layer, at(0), :], x[layer, at(tiles - 1), :]) for x in fields[:3]]
        side = outer(mine, halos)
        for n, (t, mask) in enumerate(ends):
            stiff = fields[5][layer, at(t), :] * LAP_SCALE
            for g in range(2):
                update = stiff * jnp.where(mask, side[n][g], 0.0)
                fixed[g, layer + 3, n] = first[g, layer + 3, t] + update
            made[4, layer, n] = sums[0, layer, t] + mine[0][n] * update
            made[5, layer, n] = sums[1, layer, t] + RHO_SCALE * jnp.where(mask, side[n][2], 0.0)
        adj, fwd, stiff = three(layer)
        low, high = (rolled(third[k], row - layer, 0) for k, row in enumerate((SUB - 3, 2)))
        stiff = jnp.where(
            sub < 4,
            jnp.where(sub == 2, high, stiff[1]),
            jnp.where(sub == SUB - 3, low, stiff[0]),
        )
        for g, x in enumerate((adj, fwd)):
            lap = join(side[0][g], side[1][g])
            fixed[g, layer + 3, 2] = join(*x) + stiff * LAP_SCALE * lap
        ring_buoy[layer] = join(*halos[2])


    def last(layer, n, radials):
        t = ends[n][0]
        rings = [[fixed[f, layer + 3, 2], fixed[f, layer + 3, n]] for f in range(2)]
        rings.append([ring_buoy[layer], wide[2, layer + 6, t]])
        beside = [first[f, layer + 3, (1, tiles - 2)[n]] for f in range(2)]
        beside.append(wide[2, layer + 6, (1, tiles - 2)[n]])
        rings = [[x[0], x[1], y] if n == 0 else [y, x[1], x[0]] for x, y in zip(rings, beside)]
        flux = [None] * 3
        flux[1] = lat_flux(rings, 1, sub)
        flux[2 * n] = lat_flux(rings, 2 * n, sub)
        flux[2 - 2 * n] = [flux_in[k, n, layer] for k in range(3)]
        here = [x[1] for x in rings]
        lat = lat_terms(flux, 1, sub, True)
        there = [fixed_halo[0, layer, n], fixed_halo[1, layer, n], buoy_halo[layer, t]]
        laps, rho = longitudinal(here, there, lane, False, True)
        stiff = fields[5][layer, at(t), :] * LAP_SCALE
        for g in range(2):
            update = stiff * (radials[g] + lat[g] + laps[0][g])
            made[2 * g, layer, n] = 2.0 * here[g] - fields[g][layer, at(t), :] + update
        made[4, layer, n] += here[0] * update
        made[5, layer, n] += RHO_SCALE * (radials[2] + lat[2] + rho)

    for n, (t, _) in enumerate(ends):
        terms = radial(lambda f, k: fixed[f, 3 + k, n], lambda k: wide[2, 6 + k, t], layers)
        for layer in range(layers):
            last(layer, n, terms[layer])
        for k, out in enumerate(outs):
            source = fixed.at[k // 2, pl.ds(3, layers), n] if k in (1, 3) else made.at[k, :, n]
            copy = pltpu.make_async_copy(source, out.at[:, at(t), :], sems.at[k, 1 + n])
            copy.start()
            copies.append(copy)
    for copy in copies:
        copy.wait()


def pairs(count, start, step):
    partner = {i: i for i in range(count)}
    for i in range(start, count - 1, step):
        partner[i], partner[i + 1] = i + 1, i
    return [
        (2 * i + core, 2 * j + (core if i != j else 1 - core))
        for i, j in partner.items()
        for core in range(2)
    ]


def call(kernel, out_shape, args, in_specs=None, out_specs=None, **more):
    return pl.pallas_call(
        kernel,
        out_shape=out_shape,
        in_specs=in_specs or [VMEM] * len(args),
        out_specs=out_specs or (VMEM,) * len(out_shape),
        compiler_params=PARAMS,
        **more,
    )(*args)


def shards(
    adj_now, adj_next, fwd_now, fwd_next, stiffness, buoyancy, kernel_bulk_in, kernel_density_in
):
    layers, rows, lanes = adj_now.shape
    tiles = rows // SUB
    fields = (adj_now, fwd_now, buoyancy, adj_next, fwd_next, stiffness)
    groups = -(-layers // (lanes // SEGMENT))
    around, count = lax.axis_size("lon"), lax.axis_size("lat")
    ring = [(i, (i + 1) % around) for i in range(around)]
    swap = [(0, 1), (1, 0)]

    def made(*shape):
        return pltpu.VMEM(shape, F32)

    block = (layers, rows, lanes)
    edge = made(groups, rows, lanes)
    hbm = pl.BlockSpec(memory_space=pltpu.HBM)
    *fields, to_right, to_left, to_core = call(
        edges_kernel,
        (made(*block),) * 6 + (edge, edge, made(sum(WIDTHS), rows, lanes)),
        [pltpu.with_memory_space_constraint(x, pltpu.HBM) for x in fields],
        in_specs=[hbm] * 6,
        scratch_shapes=[pltpu.SemaphoreType.DMA((6,))],
    )
    from_left = lax.ppermute(to_right, "lon", ring)
    from_right = lax.ppermute(to_left, "lon", [(b, a) for a, b in ring])
    from_core = lax.ppermute(to_core, "rad", swap)
    pairs_of_groups = -(-groups // 2)
    lat_edge = made(2 * layers + 4 + pairs_of_groups, SUB, lanes)
    packs = [from_left, from_right, to_left, to_right]
    wide, part, base, to_first, to_second, to_third = call(
        inner_kernel,
        (
            made(3, layers + 12, tiles, SUB, lanes),
            made(3, layers + 6, tiles, SUB, lanes),
            made(4, layers, tiles, SUB, lanes),
            lat_edge,
            lat_edge,
            lat_edge,
        ),
        [*fields, kernel_bulk_in, kernel_density_in, from_core],
    )
    to_first, to_second, to_third, to_core, edges = call(
        turn_kernel,
        (lat_edge, lat_edge, lat_edge, made(4, rows, lanes), made(2, pairs_of_groups, SUB, lanes)),
        [*fields, *packs, part, to_first, to_second, to_third],
        input_output_aliases={11: 0, 12: 1, 13: 2},
    )
    from_first = lax.ppermute(to_first, ("lat", "rad"), pairs(count, 0, 4))
    from_second = lax.ppermute(to_second, ("lat", "rad"), pairs(count, 1, 2))
    from_third = lax.ppermute(to_third, ("lat", "rad"), pairs(count, 2, 4))
    from_core2 = lax.ppermute(to_core, "rad", swap)
    first, first_pack, stiff_pack, buoy_halo, flux, sums, done = call(
        middle_kernel,
        (
            made(2, layers + 6, tiles, SUB, lanes),
            made(2, groups, tiles, SUB, lanes),
            made(groups, tiles, SUB, lanes),
            made(layers, tiles, SUB, lanes),
            made(3, 2, layers, SUB, lanes),
            made(2, layers, tiles, SUB, lanes),
            made(6, layers, rows - 2 * SUB, lanes),
        ),
        [
            *fields,
            base,
            *packs,
            from_core,
            from_core2,
            wide,
            part,
        ],
        cost_estimate=HEAVY,
        scratch_shapes=[
            made(2, layers, tiles, SUB, lanes),
            made(3, groups + 1, tiles, SUB, lanes),
            made(3, layers, tiles - 2, SUB, lanes),
            made(3, groups, tiles, SUB, lanes),
            made(2, groups, tiles, SUB, lanes),
        ],
    )
    return call(
        last_kernel,
        (jax.ShapeDtypeStruct(block, F32),) * 6,
        [
            *fields,
            from_core,
            wide,
            first,
            first_pack,
            stiff_pack,
            buoy_halo,
            flux,
            sums,
            done,
            edges,
            from_first,
            from_second,
            from_third,
        ],
        out_specs=(hbm,) * 6,
        scratch_shapes=[
            made(2, layers + 6, 3, SUB, lanes),
            made(2, layers, 2, SUB, lanes),
            made(layers, SUB, lanes),
            made(6, layers, 2, SUB, lanes),
            pltpu.SemaphoreType.DMA((6, 3)),
        ],
    )


def solution(mesh):
    spec = P("rad", "lat", "lon")
    return jax.shard_map(
        shards, mesh=mesh, in_specs=(spec,) * 8, out_specs=(spec,) * 6, check_vma=False
    )
```
